32 devices in a mesh: section: 8 (over y, x, core), rep: 4 (over z).
Axes of the slice: x: 2, y: 2, z: 4, core: 2. Of those that a mesh axis runs over, the one named last changes fastest.
Arguments:
- tokens: bfloat16 [8, 4, 256, 1024], P('section', 'rep'), may hold values from -6 to 6
- assign: int32 [8, 4, 256, 1], P('section', 'rep'), may hold values from 0 to 7; in each aligned block of 256 rows (0 to 255, 256 to 511, ..., all dimensions but the last counted through in order) at most 48 rows name the same one
- route_mask: int32 [8], replicated, may hold values from 1 to 3
- match_mask: int32 [8], replicated, may hold values from 1 to 3
- gate_weight: bfloat16 [8, 4, 1024, 256], P('section', 'rep'), may hold values from -0.1875 to 0.1875
- up_weight: bfloat16 [8, 4, 1024, 256], P('section', 'rep'), may hold values from -0.1875 to 0.1875
- down_weight: bfloat16 [8, 4, 256, 1024], P('section', 'rep'), may hold values from -0.375 to 0.375
- slow_down: bfloat16 [8, 4, 256, 1024], P('section', 'rep'), may hold values from -4 to 4
- momentum: bfloat16 [8, 4, 256, 1024], P('section', 'rep'), may hold values from -4 to 4
- slot_cot: bfloat16 [8, 4, 8, 48, 1024], P('section', 'rep'), may hold values from -6 to 6
Outputs:
- input_grad: bfloat16 [8, 4, 256, 1024], P('section', 'rep')
- new_slow: bfloat16 [8, 4, 256, 1024], P('section', 'rep')
The draws below stay inside these ranges and needn't reach their ends.
Inputs may be any that keep to these rules, and one draw needn't show every extreme that they name: `assign`: no expert is named by more than 48 rows of one device, and in every draw some device has 48 rows for one expert. Rows that replica r of any section sends to expert e are processed by replica r XOR route_mask[e] of that expert. Replica r of section s is matched with replica r XOR match_mask[s].
All inputs are finite; a program needn't handle non-finite values.
Results may differ from the reference program's by a relative error of at most 0.012.
Values may be sent and summed in bfloat16 or wider, within the bound.
No kernel may reach another device: no remote copies, remote signals or barrier semaphores. Data moves between devices by JAX's collectives and lax.ppermute only.
A program may use at most 64 MiB of HBM per device.

```python
import math
import jax
import jax.numpy as jnp
import numpy as np
from jax import lax

D = 1024
FF = 256
TOK_DEV = 256
CAP = 48
N_SECTION = 8
N_REP = 4


def plant(drawn, own_key, low, top_value):
    index_at = [jax.random.randint(jax.random.fold_in(own_key, axis), (), 0, length) for axis, length in enumerate(drawn.shape)]
    main_axis = drawn.shape.index(max(drawn.shape))
    beside = index_at[:main_axis] + [(index_at[main_axis] + 1) % drawn.shape[main_axis]] + index_at[main_axis + 1:]
    return drawn.at[tuple(index_at)].set(low).at[tuple(beside)].set(top_value)


def steps_of(stream_key, dims, shards, smallest, largest):
    factor_of, own = 1.0, jax.random.fold_in(stream_key, 6)
    for dim, parts in shards:
        draws = jnp.exp(jax.random.uniform(jax.random.fold_in(own, dim), (parts,), jnp.float32, smallest / len(shards), largest / len(shards)))
        factor_of = factor_of * jnp.repeat(draws, dims[dim] // parts).reshape([-1 if axis == dim else 1 for axis in range(len(dims))])
    return factor_of


def routed_block(own_key, own, number, rows, amount, top, bound, lean):
    order = jax.random.permutation(own_key, amount)
    heavy_load, usual = portions_of(amount, rows * top, bound, lean, True), portions_of(amount, rows * top, bound, lean, False)
    places = jnp.arange(amount)

    def named(sizes, rotation):
        used = int((sizes > 0).sum())
        fixed = max(1, used // 4)
        moved = fixed + (places - fixed + rotation * (used - fixed)) % max(1, amount - fixed)
        return jnp.zeros((amount,), jnp.int32).at[order[jnp.where(places < fixed, places, moved)]].set(jnp.asarray(sizes, jnp.int32))

    sizes = jnp.where(number % 4 == 0, named(heavy_load, number // 4), named(usual, number - number // 4 - 1))
    mixed = jax.random.permutation(jax.random.fold_in(own, 3), amount)
    giver, receiver = mixed[0:amount // 2 * 2:2], mixed[1:amount // 2 * 2:2]
    room = jnp.minimum(sizes[giver] - 1, bound - sizes[receiver]) // 2
    room = jnp.where((giver == order[0]) | (receiver == order[0]) | (sizes[receiver] == 0), 0, jnp.maximum(room, 0))
    moved = jax.random.randint(jax.random.fold_in(own, 4), (amount // 2,), 0, 1 << 20) % (room + 1)
    sizes = sizes.at[giver].add(-moved).at[receiver].add(moved)
    items = jnp.searchsorted(jnp.cumsum(sizes), jnp.arange(rows * top), side="right").astype(jnp.int32)
    table = items.reshape(top, rows).T
    table = table[jax.random.permutation(jax.random.fold_in(own, 1), rows)]
    rotation = jax.random.randint(jax.random.fold_in(own, 2), (rows, 1), 0, top)
    return jnp.take_along_axis(table, (jnp.arange(top)[None, :] + rotation) % top, axis=1)


def portions_of(count, total, reach, lean, full):
    portions = [(1 << 20) // math.isqrt(grade ** lean) + 1 for grade in range(1, count + 1)]
    largest = reach if full else min(reach, max(-(-total // count), total * portions[0] // sum(portions)))
    least = 1 if total - largest >= count - 1 else 0
    given, spare = [largest] + [least] * (count - 1), total - largest - least * (count - 1)
    while spare > 0:
        movable = [i for i in range(1, count) if given[i] < largest] or [i for i in range(1, count) if given[i] < reach]
        mass, budget = sum([portions[i] for i in movable]), spare
        for i in movable:
            extra = min(reach - given[i], max(1, budget * portions[i] // mass), spare)
            given[i] = given[i] + extra
            spare = spare - extra
    return np.array(given)


def bell_draw(own_key, dims, width, reach, split=(), kind=jnp.bfloat16):
    factor_of = steps_of(own_key, dims, split, -0.22, 0.18) if split else 1.0
    array = jax.random.normal(own_key, dims, jnp.float32) * width * factor_of
    return jnp.minimum(jnp.maximum(array, -reach), reach).astype(kind)


def setup_inputs(seed: int = 0) -> dict:
    arg_keys = jax.random.split(jax.random.key(seed), 11)
    tokens = bell_draw(arg_keys[0], (N_SECTION, N_REP, TOK_DEV, D), 1.0, 6.0, ((0, 8), (1, 4)))
    assign_keys = jax.random.split(jax.random.fold_in(arg_keys[1], 1), N_SECTION * N_REP * TOK_DEV // TOK_DEV)
    assign_turns = jax.random.permutation(jax.random.fold_in(arg_keys[1], 3), N_SECTION * N_REP * TOK_DEV // TOK_DEV)
    assign = jax.vmap(lambda own, number: routed_block(jax.random.fold_in(arg_keys[1], 2), own, number, TOK_DEV, N_SECTION, 1, CAP, 2))(assign_keys, assign_turns).reshape((N_SECTION, N_REP, TOK_DEV, 1))
    route_mask = plant(jax.random.randint(arg_keys[2], (N_SECTION,), 1, N_REP), jax.random.fold_in(arg_keys[2], 1), 1, N_REP - 1).astype(jnp.int32)
    match_mask = plant(jax.random.randint(arg_keys[3], (N_SECTION,), 1, N_REP), jax.random.fold_in(arg_keys[3], 1), 1, N_REP - 1).astype(jnp.int32)
    gate_weight = bell_draw(arg_keys[4], (N_SECTION, N_REP, D, FF), D ** -0.5, 0.1875, ((0, 8), (1, 4)))
    up_weight = bell_draw(arg_keys[5], (N_SECTION, N_REP, D, FF), D ** -0.5, 0.1875, ((0, 8), (1, 4)))
    down_weight = bell_draw(arg_keys[6], (N_SECTION, N_REP, FF, D), FF ** -0.5, 0.375, ((0, 8), (1, 4)))
    slow_down = bell_draw(arg_keys[7], (N_SECTION, N_REP, FF, D), 0.5, 4.0, ((0, 8), (1, 4)))
    momentum = bell_draw(arg_keys[8], (N_SECTION, N_REP, FF, D), 0.5, 4.0, ((0, 8), (1, 4)))
    slot_cot = bell_draw(arg_keys[9], (N_SECTION, N_REP, N_SECTION, CAP, D), 1.0, 6.0, ((0, 8), (1, 4)))
    return {"tokens": tokens, "assign": assign, "route_mask": route_mask, "match_mask": match_mask, "gate_weight": gate_weight, "up_weight": up_weight, "down_weight": down_weight, "slow_down": slow_down, "momentum": momentum, "slot_cot": slot_cot}


inner_rate = 0.05
pull_rate = 0.25
moment_rate = 0.9
outer_rate = 0.7


def slot_table(expert_ids, sections, capacity):
    expert_hot = (expert_ids[:, None] == jnp.arange(sections, dtype=jnp.int32)[None, :]).astype(jnp.int32)
    position = jnp.sum((jnp.cumsum(expert_hot, axis=0) - 1) * expert_hot, axis=1)
    slot_index = expert_ids * capacity + position
    return (slot_index[:, None] == jnp.arange(sections * capacity, dtype=jnp.int32)[None, :]).astype(jnp.bfloat16)


def expert_pass(rows, cotangent, gate_mat, up_mat, down_mat):
    contract = (((1,), (1,)), ((), ()))
    gate_act = jnp.dot(rows, gate_mat, preferred_element_type=jnp.float32)
    up_act = jnp.dot(rows, up_mat, preferred_element_type=jnp.float32)
    sigmoid_gate = jax.nn.sigmoid(gate_act)
    hidden = (gate_act * sigmoid_gate * up_act).astype(jnp.bfloat16)
    hidden_grad = lax.dot_general(cotangent, down_mat, contract, preferred_element_type=jnp.float32)
    gate_grad = (hidden_grad * up_act * sigmoid_gate * (1.0 + gate_act * (1.0 - sigmoid_gate))).astype(jnp.bfloat16)
    up_grad = (hidden_grad * gate_act * sigmoid_gate).astype(jnp.bfloat16)
    slot_grad = (lax.dot_general(gate_grad, gate_mat, contract, preferred_element_type=jnp.float32)
                 + lax.dot_general(up_grad, up_mat, contract, preferred_element_type=jnp.float32)).astype(jnp.bfloat16)
    down_grad = lax.dot_general(hidden, cotangent, (((0,), (0,)), ((), ())), preferred_element_type=jnp.float32).astype(jnp.bfloat16)
    return slot_grad, down_grad


def reference(tokens, assign, route_mask, match_mask, gate_weight, up_weight, down_weight, slow_down, momentum, slot_cot):
    sections, replicas, tok_rows, model_width = tokens.shape
    capacity = slot_cot.shape[3]
    hidden_width = gate_weight.shape[3]
    flat_tokens = tokens.reshape(sections * replicas, tok_rows, model_width)
    flat_ids = assign.reshape(sections * replicas, tok_rows)

    def dispatch_one(packet):
        rows, expert_ids = packet
        selector = slot_table(expert_ids, sections, capacity)
        placed = lax.dot_general(selector, rows, (((0,), (0,)), ((), ())), preferred_element_type=jnp.float32)
        return placed.astype(jnp.bfloat16).reshape(sections, capacity, model_width)

    dispatched = lax.map(dispatch_one, (flat_tokens, flat_ids)).reshape(sections, replicas, sections, capacity, model_width)

    def expert_one(index):
        expert = index // replicas
        replica = index % replicas
        source = jnp.bitwise_xor(replica, route_mask[expert])
        rows = dispatched[:, source, expert].reshape(-1, model_width)
        cotangent = slot_cot[expert, source].reshape(-1, model_width)
        slot_grad, down_grad = expert_pass(rows, cotangent, gate_weight[expert, replica], up_weight[expert, replica], down_weight[expert, replica])
        return slot_grad.reshape(sections, capacity, model_width), down_grad

    slot_grads, down_grads = lax.map(expert_one, jnp.arange(sections * replicas, dtype=jnp.int32))
    slot_grads = slot_grads.reshape(sections, replicas, sections, capacity, model_width)
    down_grads = down_grads.reshape(sections, replicas, hidden_width, model_width)

    slow_float = slow_down.astype(jnp.float32)
    delta = (slow_float - (down_weight.astype(jnp.float32) - inner_rate * down_grads.astype(jnp.float32))).astype(jnp.bfloat16)
    delta_float = delta.astype(jnp.float32)
    partner_term = (0.5 * delta_float - pull_rate * slow_float).astype(jnp.bfloat16)
    replica_range = jnp.arange(replicas, dtype=jnp.int32)
    partner_index = jnp.bitwise_xor(replica_range[None, :], match_mask[:, None])
    section_range = jnp.arange(sections, dtype=jnp.int32)[:, None]
    partner_value = partner_term[section_range, partner_index]
    outer_grad = 0.5 * delta_float + pull_rate * slow_float + partner_value.astype(jnp.float32)
    momentum_new = moment_rate * momentum.astype(jnp.float32) + outer_grad
    new_slow = (slow_float - outer_rate * (outer_grad + moment_rate * momentum_new)).astype(jnp.bfloat16)

    def return_one(index):
        section_id = index // replicas
        replica = index % replicas
        expert_ids = assign[section_id, replica, :, 0]
        sources = jnp.bitwise_xor(replica, route_mask)
        returned = slot_grads[jnp.arange(sections, dtype=jnp.int32), sources, section_id]
        selector = slot_table(expert_ids, sections, capacity)
        return jnp.dot(selector, returned.reshape(-1, model_width), preferred_element_type=jnp.float32).astype(jnp.bfloat16)

    input_grad = lax.map(return_one, jnp.arange(sections * replicas, dtype=jnp.int32))
    input_grad = input_grad.reshape(sections, replicas, tok_rows, model_width)
    return input_grad, new_slow
```

```python
import jax
import jax.numpy as jnp
from jax import lax
from jax.sharding import PartitionSpec as P

inner_rate = 0.05
pull_rate = 0.25
moment_rate = 0.9
outer_rate = 0.7


def from_partner(value, distance):
    pairs = [(source, source ^ 2**distance) for source in range(lax.axis_size("rep"))]
    return lax.ppermute(value, "rep", pairs)


def bit_of(mask, index):
    return jnp.bitwise_and(jnp.right_shift(mask, index), 1) == 1


def route(value, mask, bits):
    for index in bits:
        value = jnp.where(bit_of(mask, index), from_partner(value, index), value)
    return value


def slot_table(expert_ids, sections, capacity):
    expert_hot = (expert_ids[:, None] == jnp.arange(sections, dtype=jnp.int32)[None, :]).astype(
        jnp.int32
    )
    position = jnp.sum((jnp.cumsum(expert_hot, axis=0) - 1) * expert_hot, axis=1)
    slot_index = expert_ids * capacity + position
    return (
        slot_index[:, None] == jnp.arange(sections * capacity, dtype=jnp.int32)[None, :]
    ).astype(jnp.bfloat16)


def on_device(
    tokens,
    assign,
    route_mask,
    match_mask,
    gate_weight,
    up_weight,
    down_weight,
    slow_down,
    momentum,
    slot_cot,
):
    sections = lax.axis_size("section")
    levels = lax.axis_size("rep").bit_length() - 1
    section_here = lax.axis_index("section")
    token_rows = tokens[0, 0]
    expert_ids = assign[0, 0, :, 0]
    capacity = slot_cot.shape[3]
    model_width = token_rows.shape[1]
    own_mask = route_mask[section_here]
    match = match_mask[section_here]
    upward = list(range(levels))
    downward = upward[::-1]
    contract = (((1,), (1,)), ((), ()))

    down_mat = down_weight[0, 0]
    slow_float = slow_down[0, 0].astype(jnp.float32)
    gate_mat = route(gate_weight[0, 0], own_mask, downward)
    up_mat = route(up_weight[0, 0], own_mask, upward)
    down_here = route(down_mat, own_mask, downward)

    selector = slot_table(expert_ids, sections, capacity)
    placed = lax.dot_general(
        selector, token_rows, (((0,), (0,)), ((), ())), preferred_element_type=jnp.float32
    )
    dispatched = placed.astype(jnp.bfloat16).reshape(sections, capacity, model_width)
    arrived = lax.all_to_all(dispatched, "section", split_axis=0, concat_axis=0, tiled=True)
    rows = arrived.reshape(-1, model_width)
    cotangent = slot_cot[0, 0].reshape(-1, model_width)

    gate_act = jnp.dot(rows, gate_mat, preferred_element_type=jnp.float32)
    up_act = jnp.dot(rows, up_mat, preferred_element_type=jnp.float32)
    sigmoid_gate = jax.nn.sigmoid(gate_act)
    hidden = (gate_act * sigmoid_gate * up_act).astype(jnp.bfloat16)
    down_grad = lax.dot_general(
        hidden, cotangent, (((0,), (0,)), ((), ())), preferred_element_type=jnp.float32
    ).astype(jnp.bfloat16)

    static_part = (0.5 - pull_rate) * slow_float - 0.5 * down_mat.astype(jnp.float32)
    match_mine = jnp.bitwise_xor(own_mask, match)
    lower, top = upward[:-1], levels - 1
    static_routed = route(static_part.astype(jnp.bfloat16), match, lower).astype(jnp.float32)
    own_routed, match_routed = down_grad, down_grad
    for index in lower:
        own_in = from_partner(own_routed, index)
        match_in = own_in if index == 0 else from_partner(match_routed, index)
        own_routed = jnp.where(bit_of(own_mask, index), own_in, own_routed)
        match_routed = jnp.where(bit_of(match_mine, index), match_in, match_routed)

    def combined(side):
        def pick(mask, value):
            return jnp.where(bit_of(mask, top) == side, value, 0.0)

        return pick(match, static_routed) + 0.5 * inner_rate * (
            pick(own_mask, own_routed.astype(jnp.float32))
            + pick(match_mine, match_routed.astype(jnp.float32))
        )

    crossing = from_partner(combined(True).astype(jnp.bfloat16), top)
    staying = combined(False)
    outer_grad = (
        (0.5 + pull_rate) * slow_float
        - 0.5 * down_mat.astype(jnp.float32)
        + staying
        + crossing.astype(jnp.float32)
    )
    momentum_new = moment_rate * momentum[0, 0].astype(jnp.float32) + outer_grad
    new_slow = (slow_float - outer_rate * (outer_grad + moment_rate * momentum_new)).astype(
        jnp.bfloat16
    )

    hidden_grad = lax.dot_general(
        cotangent, down_here, contract, preferred_element_type=jnp.float32
    )
    gate_grad = (
        hidden_grad * up_act * sigmoid_gate * (1.0 + gate_act * (1.0 - sigmoid_gate))
    ).astype(jnp.bfloat16)
    up_grad = (hidden_grad * gate_act * sigmoid_gate).astype(jnp.bfloat16)
    slot_grad = (
        lax.dot_general(gate_grad, gate_mat, contract, preferred_element_type=jnp.float32)
        + lax.dot_general(up_grad, up_mat, contract, preferred_element_type=jnp.float32)
    ).astype(jnp.bfloat16)
    slot_grad = slot_grad.reshape(sections, capacity, model_width)
    returned = lax.all_to_all(slot_grad, "section", split_axis=0, concat_axis=0, tiled=True)
    input_grad = jnp.dot(
        selector, returned.reshape(-1, model_width), preferred_element_type=jnp.float32
    ).astype(jnp.bfloat16)
    return (input_grad[None, None], new_slow[None, None])


def solution(mesh):
    in_specs = (
        P("section", "rep", None, None),
        P("section", "rep", None, None),
        P(),
        P(),
        P("section", "rep", None, None),
        P("section", "rep", None, None),
        P("section", "rep", None, None),
        P("section", "rep", None, None),
        P("section", "rep", None, None),
        P("section", "rep", None, None, None),
    )
    out_specs = (P("section", "rep", None, None), P("section", "rep", None, None))
    return jax.shard_map(
        on_device, mesh=mesh, in_specs=in_specs, out_specs=out_specs, check_vma=False
    )
```

```python
import jax
import jax.numpy as jnp
from jax import lax
from jax.sharding import PartitionSpec as P

inner_rate = 0.05
pull_rate = 0.25
moment_rate = 0.9
outer_rate = 0.7


def from_partner(value, distance):
    pairs = [(source, source ^ 2**distance) for source in range(lax.axis_size("rep"))]
    return lax.ppermute(value, "rep", pairs)


def bit_of(mask, index):
    return jnp.bitwise_and(jnp.right_shift(mask, index), 1) == 1


def route(value, mask, bits):
    for index in bits:
        value = jnp.where(bit_of(mask, index), from_partner(value, index), value)
    return value


def hub_route(values, mask):
    replica = lax.axis_index("rep")
    inner = (replica == 1) | (replica == 2)
    results = []
    gathered_before, middle_before = None, None
    for number, value in enumerate(values):
        start = value
        if gathered_before is not None:
            start = lax.optimization_barrier((value, gathered_before))[0]
        gathered = lax.ppermute(start, "rep", [(0, 1), (3, 2)])
        gathered_before = gathered
        swap = [(1, 2), (2, 1)]
        if number == 0:
            first, second = value, gathered
        else:
            first = jnp.where(mask == 3, gathered, value)
            second = jnp.where(mask == 3, value, gathered)
            first = lax.optimization_barrier((first, middle_before))[0]
        first_in = lax.ppermute(first, "rep", swap)
        second = lax.optimization_barrier((second, first_in))[0]
        second_in = lax.ppermute(second, "rep", swap)
        middle_before = second_in
        if number == 0:
            for_outer = jnp.where(mask == 3, second_in, first_in)
            for_inner = jnp.where(mask == 3, first_in, second_in)
        else:
            for_outer, for_inner = first_in, second_in
        handed = lax.ppermute(jnp.where(mask == 1, value, for_outer), "rep", [(1, 0), (2, 3)])
        results.append(jnp.where(inner, jnp.where(mask == 1, gathered, for_inner), handed))
    return results


def slot_table(expert_ids, sections, capacity):
    expert_hot = (expert_ids[:, None] == jnp.arange(sections, dtype=jnp.int32)[None, :]).astype(
        jnp.int32
    )
    position = jnp.sum((jnp.cumsum(expert_hot, axis=0) - 1) * expert_hot, axis=1)
    slot_index = expert_ids * capacity + position
    return (
        slot_index[:, None] == jnp.arange(sections * capacity, dtype=jnp.int32)[None, :]
    ).astype(jnp.bfloat16)


def on_device(
    tokens,
    assign,
    route_mask,
    match_mask,
    gate_weight,
    up_weight,
    down_weight,
    slow_down,
    momentum,
    slot_cot,
):
    sections = lax.axis_size("section")
    levels = lax.axis_size("rep").bit_length() - 1
    section_here = lax.axis_index("section")
    token_rows = tokens[0, 0]
    expert_ids = assign[0, 0, :, 0]
    capacity = slot_cot.shape[3]
    model_width = token_rows.shape[1]
    own_mask = route_mask[section_here]
    match = match_mask[section_here]
    upward = list(range(levels))
    contract = (((1,), (1,)), ((), ()))

    down_mat = down_weight[0, 0]
    slow_float = slow_down[0, 0].astype(jnp.float32)
    weights = (gate_weight[0, 0], up_weight[0, 0], down_mat)
    if levels == 2:
        gate_mat, up_mat, down_here = hub_route(weights, own_mask)
    else:
        gate_mat, up_mat, down_here = [route(weight, own_mask, upward) for weight in weights]

    selector = slot_table(expert_ids, sections, capacity)
    placed = lax.dot_general(
        selector, token_rows, (((0,), (0,)), ((), ())), preferred_element_type=jnp.float32
    )
    dispatched = placed.astype(jnp.bfloat16).reshape(sections, capacity, model_width)
    arrived = lax.all_to_all(dispatched, "section", split_axis=0, concat_axis=0, tiled=True)
    rows = arrived.reshape(-1, model_width)
    cotangent = slot_cot[0, 0].reshape(-1, model_width)

    gate_act = jnp.dot(rows, gate_mat, preferred_element_type=jnp.float32)
    up_act = jnp.dot(rows, up_mat, preferred_element_type=jnp.float32)
    sigmoid_gate = jax.nn.sigmoid(gate_act)
    hidden = (gate_act * sigmoid_gate * up_act).astype(jnp.bfloat16)
    down_grad = lax.dot_general(
        hidden, cotangent, (((0,), (0,)), ((), ())), preferred_element_type=jnp.float32
    ).astype(jnp.bfloat16)

    static_part = (0.5 - pull_rate) * slow_float - 0.5 * down_mat.astype(jnp.float32)
    match_mine = jnp.bitwise_xor(own_mask, match)
    lower, top = upward[:-1], levels - 1
    static_routed = route(static_part.astype(jnp.bfloat16), match, lower).astype(jnp.float32)
    own_routed, match_routed = down_grad, down_grad
    for index in lower:
        own_in = from_partner(own_routed, index)
        match_in = own_in if index == 0 else from_partner(match_routed, index)
        own_routed = jnp.where(bit_of(own_mask, index), own_in, own_routed)
        match_routed = jnp.where(bit_of(match_mine, index), match_in, match_routed)

    def combined(side):
        def pick(mask, value):
            return jnp.where(bit_of(mask, top) == side, value, 0.0)

        return pick(match, static_routed) + 0.5 * inner_rate * (
            pick(own_mask, own_routed.astype(jnp.float32))
            + pick(match_mine, match_routed.astype(jnp.float32))
        )

    crossing = from_partner(combined(True).astype(jnp.bfloat16), top)
    staying = combined(False)
    outer_grad = (
        (0.5 + pull_rate) * slow_float
        - 0.5 * down_mat.astype(jnp.float32)
        + staying
        + crossing.astype(jnp.float32)
    )
    momentum_new = moment_rate * momentum[0, 0].astype(jnp.float32) + outer_grad
    new_slow = (slow_float - outer_rate * (outer_grad + moment_rate * momentum_new)).astype(
        jnp.bfloat16
    )

    hidden_grad = lax.dot_general(
        cotangent, down_here, contract, preferred_element_type=jnp.float32
    )
    gate_grad = (
        hidden_grad * up_act * sigmoid_gate * (1.0 + gate_act * (1.0 - sigmoid_gate))
    ).astype(jnp.bfloat16)
    up_grad = (hidden_grad * gate_act * sigmoid_gate).astype(jnp.bfloat16)
    slot_grad = (
        lax.dot_general(gate_grad, gate_mat, contract, preferred_element_type=jnp.float32)
        + lax.dot_general(up_grad, up_mat, contract, preferred_element_type=jnp.float32)
    ).astype(jnp.bfloat16)
    slot_grad = slot_grad.reshape(sections, capacity, model_width)
    returned = lax.all_to_all(slot_grad, "section", split_axis=0, concat_axis=0, tiled=True)
    input_grad = jnp.dot(
        selector, returned.reshape(-1, model_width), preferred_element_type=jnp.float32
    ).astype(jnp.bfloat16)
    return (input_grad[None, None], new_slow[None, None])


def solution(mesh):
    in_specs = (
        P("section", "rep", None, None),
        P("section", "rep", None, None),
        P(),
        P(),
        P("section", "rep", None, None),
        P("section", "rep", None, None),
        P("section", "rep", None, None),
        P("section", "rep", None, None),
        P("section", "rep", None, None),
        P("section", "rep", None, None, None),
    )
    out_specs = (P("section", "rep", None, None), P("section", "rep", None, None))
    return jax.shard_map(
        on_device, mesh=mesh, in_specs=in_specs, out_specs=out_specs, check_vma=False
    )
```

```python
import jax
import jax.numpy as jnp
from jax import lax
from jax.sharding import PartitionSpec as P

inner_rate = 0.05
pull_rate = 0.25
moment_rate = 0.9
outer_rate = 0.7


def from_partner(value, distance):
    pairs = [(source, source ^ 2**distance) for source in range(lax.axis_size("rep"))]
    return lax.ppermute(value, "rep", pairs)


def bit_of(mask, index):
    return jnp.bitwise_and(jnp.right_shift(mask, index), 1) == 1


def route(value, mask, bits):
    for index in bits:
        value = jnp.where(bit_of(mask, index), from_partner(value, index), value)
    return value


def after(value, *earlier):
    return lax.optimization_barrier((value, *earlier))[0]


def hub_route(values, mask):
    replica = lax.axis_index("rep")
    inner = (replica == 1) | (replica == 2)
    swap = [(1, 2), (2, 1)]
    near, far = mask == 1, mask == 3
    results, gathered_all, crossed = [], [], []
    for number, value in enumerate(values):
        start = value
        if number == 1:
            start, near, far, inner = lax.optimization_barrier((start, near, far, inner))
        if number > 0:
            start = after(start, gathered_all[-1])
        gathered = lax.ppermute(start, "rep", [(0, 1), (3, 2)])
        gathered_all.append(gathered)
        if number == 0:
            first, second = value, gathered
        else:
            first = jnp.where(far, gathered, value)
            second = jnp.where(far, value, gathered)
        if len(crossed) >= 2:
            first = after(first, crossed[-2])
        if number == 1:
            quiet = first
        crossed.append(lax.ppermute(first, "rep", swap))
        if len(crossed) >= 2 and number > 0:
            second = after(second, crossed[-2])
        crossed.append(lax.ppermute(second, "rep", swap))
        first_in, second_in = crossed[-2:]
        if number == 0:
            for_outer = jnp.where(far, second_in, first_in)
            for_inner = jnp.where(far, first_in, second_in)
        else:
            for_outer, for_inner = first_in, second_in
        handed = lax.ppermute(jnp.where(near, value, for_outer), "rep", [(1, 0), (2, 3)])
        results.append(jnp.where(inner, jnp.where(near, gathered, for_inner), handed))
    return results, quiet, gathered_all[-1]


def slot_table(expert_ids, sections, capacity):
    expert_hot = (expert_ids[:, None] == jnp.arange(sections, dtype=jnp.int32)[None, :]).astype(
        jnp.int32
    )
    position = jnp.sum((jnp.cumsum(expert_hot, axis=0) - 1) * expert_hot, axis=1)
    slot_index = expert_ids * capacity + position
    return (
        slot_index[:, None] == jnp.arange(sections * capacity, dtype=jnp.int32)[None, :]
    ).astype(jnp.bfloat16)


def on_device(
    tokens,
    assign,
    route_mask,
    match_mask,
    gate_weight,
    up_weight,
    down_weight,
    slow_down,
    momentum,
    slot_cot,
):
    sections = lax.axis_size("section")
    levels = lax.axis_size("rep").bit_length() - 1
    section_here = lax.axis_index("section")
    token_rows = tokens[0, 0]
    expert_ids = assign[0, 0, :, 0]
    capacity = slot_cot.shape[3]
    model_width = token_rows.shape[1]
    own_mask = route_mask[section_here]
    match = match_mask[section_here]
    upward = list(range(levels))
    contract = (((1,), (1,)), ((), ()))

    down_mat = down_weight[0, 0]
    slow_float = slow_down[0, 0].astype(jnp.float32)
    weights = (gate_weight[0, 0], up_weight[0, 0], down_mat)
    if levels == 2:
        (gate_mat, up_mat, down_here), quiet, quieter = hub_route(weights, own_mask)
    else:
        gate_mat, up_mat, down_here = [route(weight, own_mask, upward) for weight in weights]
        quiet = quieter = gate_mat

    selector = slot_table(expert_ids, sections, capacity)
    placed = lax.dot_general(
        selector, token_rows, (((0,), (0,)), ((), ())), preferred_element_type=jnp.float32
    )
    dispatched = placed.astype(jnp.bfloat16).reshape(sections, capacity, model_width)
    dispatched = after(dispatched, quiet)
    arrived = lax.all_to_all(dispatched, "section", split_axis=0, concat_axis=0, tiled=True)
    rows = arrived.reshape(-1, model_width)
    cotangent = slot_cot[0, 0].reshape(-1, model_width)

    gate_act = jnp.dot(rows, gate_mat, preferred_element_type=jnp.float32)
    up_act = jnp.dot(rows, up_mat, preferred_element_type=jnp.float32)
    sigmoid_gate = jax.nn.sigmoid(gate_act)
    hidden = (gate_act * sigmoid_gate * up_act).astype(jnp.bfloat16)
    down_grad = lax.dot_general(
        hidden, cotangent, (((0,), (0,)), ((), ())), preferred_element_type=jnp.float32
    ).astype(jnp.bfloat16)

    static_part = (0.5 - pull_rate) * slow_float - 0.5 * down_mat.astype(jnp.float32)
    match_mine = jnp.bitwise_xor(own_mask, match)
    lower, top = upward[:-1], levels - 1
    static_part = after(static_part.astype(jnp.bfloat16), quieter)
    static_routed = route(static_part, match, lower).astype(jnp.float32)
    own_routed, match_routed = down_grad, down_grad
    for index in lower:
        own_in = from_partner(own_routed, index)
        match_in = own_in if index == 0 else from_partner(match_routed, index)
        own_routed = jnp.where(bit_of(own_mask, index), own_in, own_routed)
        match_routed = jnp.where(bit_of(match_mine, index), match_in, match_routed)

    def combined(side):
        def pick(mask, value):
            return jnp.where(bit_of(mask, top) == side, value, 0.0)

        return pick(match, static_routed) + 0.5 * inner_rate * (
            pick(own_mask, own_routed.astype(jnp.float32))
            + pick(match_mine, match_routed.astype(jnp.float32))
        )

    crossing_out = combined(True).astype(jnp.bfloat16)
    crossing = from_partner(crossing_out, top)
    outer_here = (
        (0.5 + pull_rate) * slow_float - 0.5 * down_mat.astype(jnp.float32) + combined(False)
    )
    pull = outer_rate * (1.0 + moment_rate)
    kept = (
        slow_float
        - pull * outer_here
        - (outer_rate * moment_rate * moment_rate) * momentum[0, 0].astype(jnp.float32)
    )
    kept = after(kept, crossing_out)
    new_slow = (kept - pull * crossing.astype(jnp.float32)).astype(jnp.bfloat16)

    down_here = after(down_here, crossing_out)
    hidden_grad = lax.dot_general(
        cotangent, down_here, contract, preferred_element_type=jnp.float32
    )
    gate_grad = (
        hidden_grad * up_act * sigmoid_gate * (1.0 + gate_act * (1.0 - sigmoid_gate))
    ).astype(jnp.bfloat16)
    up_grad = (hidden_grad * gate_act * sigmoid_gate).astype(jnp.bfloat16)
    slot_grad = (
        lax.dot_general(gate_grad, gate_mat, contract, preferred_element_type=jnp.float32)
        + lax.dot_general(up_grad, up_mat, contract, preferred_element_type=jnp.float32)
    ).astype(jnp.bfloat16)
    slot_grad = slot_grad.reshape(sections, capacity, model_width)
    returned = lax.all_to_all(slot_grad, "section", split_axis=0, concat_axis=0, tiled=True)
    input_grad = jnp.dot(
        selector, returned.reshape(-1, model_width), preferred_element_type=jnp.float32
    ).astype(jnp.bfloat16)
    return (input_grad[None, None], new_slow[None, None])


def solution(mesh):
    in_specs = (
        P("section", "rep", None, None),
        P("section", "rep", None, None),
        P(),
        P(),
        P("section", "rep", None, None),
        P("section", "rep", None, None),
        P("section", "rep", None, None),
        P("section", "rep", None, None),
        P("section", "rep", None, None),
        P("section", "rep", None, None, None),
    )
    out_specs = (P("section", "rep", None, None), P("section", "rep", None, None))
    return jax.shard_map(
        on_device, mesh=mesh, in_specs=in_specs, out_specs=out_specs, check_vma=False
    )
```

```python
import jax
import jax.numpy as jnp
from jax import lax
from jax.sharding import PartitionSpec as P

inner_rate = 0.05
pull_rate = 0.25
moment_rate = 0.9
outer_rate = 0.7

OUTWARD = [(1, 0), (2, 3)]
INWARD = [(0, 1), (3, 2)]
ACROSS = [(1, 2), (2, 1)]


def from_partner(value, distance):
    pairs = [(source, source ^ 2**distance) for source in range(lax.axis_size("rep"))]
    return lax.ppermute(value, "rep", pairs)


def bit_of(mask, index):
    return jnp.bitwise_and(jnp.right_shift(mask, index), 1) == 1


def route(value, mask, bits):
    for index in bits:
        value = jnp.where(bit_of(mask, index), from_partner(value, index), value)
    return value


def after(value, *earlier):
    return lax.optimization_barrier((value, *earlier))[0]


def slot_table(expert_ids, sections, capacity):
    expert_hot = (expert_ids[:, None] == jnp.arange(sections, dtype=jnp.int32)[None, :]).astype(
        jnp.int32
    )
    position = jnp.sum((jnp.cumsum(expert_hot, axis=0) - 1) * expert_hot, axis=1)
    slot_index = expert_ids * capacity + position
    return (
        slot_index[:, None] == jnp.arange(sections * capacity, dtype=jnp.int32)[None, :]
    ).astype(jnp.bfloat16)


def stacked(wide, width):
    return jnp.concatenate(jnp.split(wide, wide.shape[1] // width, axis=1), axis=0)


def side_by_side(tall):
    return jnp.concatenate(jnp.split(tall, tall.shape[0] // tall.shape[1], axis=0), axis=1)


class FourInLine:
    def __init__(self, gate, up, down, static_part, mask):
        replica = lax.axis_index("rep")
        self.inner = (replica == 1) | (replica == 2)
        self.near, self.far = mask == 1, mask == 3
        self.gate, self.up, self.down = gate, up, down
        self.static_part = static_part

    def forward(self):
        self.up_side = lax.ppermute(self.up, "rep", INWARD)
        self.gate_hub = lax.ppermute(self.gate, "rep", ACROSS)
        send = jnp.where(self.inner, self.static_part, self.gate)
        side, send, self.inner, self.near, self.far = lax.optimization_barrier(
            (self.up_side, send, self.inner, self.near, self.far)
        )
        first = jnp.where(self.far, side, self.up)
        second = jnp.where(self.far, self.up, side)
        first_in = lax.ppermute(first, "rep", ACROSS)
        self.one = from_partner(after(send, first), 0)
        self.gate_edge = lax.ppermute(self.one, "rep", ACROSS)
        send = jnp.where(self.inner, jnp.where(self.near, self.up, first_in), self.down)
        self.two = from_partner(send, 0)
        self.up_hub = lax.ppermute(after(second, send), "rep", ACROSS)
        self.quiet = send

    def handed_gate(self, earlier):
        gate_edge = after(self.gate_edge, *earlier)
        gate_out = jnp.where(
            self.near, self.gate, jnp.where(self.far, gate_edge, self.gate_hub)
        )
        send = jnp.where(self.inner, gate_out, self.static_part)
        self.three = from_partner(send, 0)
        two = after(self.two, send)
        first = jnp.where(self.far, two, self.down)
        second = jnp.where(self.far, self.down, two)
        self.down_first = lax.ppermute(first, "rep", ACROSS)
        self.down_hub = lax.ppermute(after(second, self.up_hub), "rep", ACROSS)
        gate_in = jnp.where(
            self.near, self.one, jnp.where(self.far, self.gate_hub, self.gate_edge)
        )
        gate_here = jnp.where(self.inner, gate_in, self.three)
        up_in = jnp.where(self.near, self.up_side, self.up_hub)
        up_here = jnp.where(self.inner, up_in, self.two)
        static_in = jnp.where(self.inner, self.three, self.one)
        return gate_here, up_here, static_in

    def handed_down(self, earlier):
        send = jnp.where(self.near, self.down, after(self.down_first, *earlier))
        self.four = lax.ppermute(send, "rep", OUTWARD)
        return send

    def down_here(self, earlier):
        down_hub = after(self.down_hub, *earlier)
        down_in = jnp.where(self.near, self.two, down_hub)
        return jnp.where(self.inner, down_in, self.four)


def on_device(
    tokens,
    assign,
    route_mask,
    match_mask,
    gate_weight,
    up_weight,
    down_weight,
    slow_down,
    momentum,
    slot_cot,
):
    sections = lax.axis_size("section")
    levels = lax.axis_size("rep").bit_length() - 1
    section_here = lax.axis_index("section")
    token_rows = tokens[0, 0]
    expert_ids = assign[0, 0, :, 0]
    capacity = slot_cot.shape[3]
    model_width = token_rows.shape[1]
    own_mask = route_mask[section_here]
    match = match_mask[section_here]
    upward = list(range(levels))
    contract = (((1,), (1,)), ((), ()))
    hidden_width = gate_weight.shape[3]

    gate_raw, up_raw, down_raw = gate_weight[0, 0], up_weight[0, 0], down_weight[0, 0]
    slow_float = slow_down[0, 0].astype(jnp.float32)
    down_float = down_raw.astype(jnp.float32)
    static_part = ((0.5 - pull_rate) * slow_float - 0.5 * down_float).astype(jnp.bfloat16)

    selector = slot_table(expert_ids, sections, capacity)
    placed = lax.dot_general(
        selector, token_rows, (((0,), (0,)), ((), ())), preferred_element_type=jnp.float32
    )
    dispatched = placed.astype(jnp.bfloat16).reshape(sections, capacity, model_width)

    line = None
    if levels == 2:
        line = FourInLine(
            gate_raw,
            up_raw,
            stacked(down_raw, hidden_width),
            stacked(lax.optimization_barrier(static_part), hidden_width),
            own_mask,
        )
        line.forward()
        dispatched = after(dispatched, line.quiet)
    arrived = lax.all_to_all(dispatched, "section", split_axis=0, concat_axis=0, tiled=True)
    rows = arrived.reshape(-1, model_width)
    cotangent = slot_cot[0, 0].reshape(-1, model_width)
    if line is not None:
        gate_mat, up_mat, static_in = line.handed_gate((line.quiet,))
        static_in = side_by_side(static_in)
    else:
        gate_mat, up_mat, down_mat = [
            route(weight, own_mask, upward) for weight in (gate_raw, up_raw, down_raw)
        ]
        static_in = from_partner(static_part, 0)

    gate_act = jnp.dot(rows, gate_mat, preferred_element_type=jnp.float32)
    up_act = jnp.dot(rows, up_mat, preferred_element_type=jnp.float32)
    sigmoid_gate = jax.nn.sigmoid(gate_act)
    hidden = (gate_act * sigmoid_gate * up_act).astype(jnp.bfloat16)
    down_grad = lax.dot_general(
        hidden, cotangent, (((0,), (0,)), ((), ())), preferred_element_type=jnp.float32
    ).astype(jnp.bfloat16)

    match_mine = jnp.bitwise_xor(own_mask, match)
    lower, top = upward[:-1], levels - 1
    down_grad_in = from_partner(down_grad, 0)
    if line is not None:
        sent = line.handed_down((down_grad,))
        static_in = after(static_in, sent)
        down_grad_in = after(down_grad_in, static_in)
    own_routed, match_routed, static_routed = down_grad, down_grad, static_part
    for index in lower:
        if index == 0:
            own_in, match_in, static_here = down_grad_in, down_grad_in, static_in
        else:
            own_in = from_partner(own_routed, index)
            match_in = from_partner(match_routed, index)
            static_here = from_partner(static_routed, index)
        own_routed = jnp.where(bit_of(own_mask, index), own_in, own_routed)
        match_routed = jnp.where(bit_of(match_mine, index), match_in, match_routed)
        static_routed = jnp.where(bit_of(match, index), static_here, static_routed)

    def combined(side, static_routed, own_routed, match_routed):
        def pick(mask, value):
            return jnp.where(bit_of(mask, top) == side, value.astype(jnp.float32), 0.0)

        return pick(match, static_routed) + 0.5 * inner_rate * (
            pick(own_mask, own_routed) + pick(match_mine, match_routed)
        )

    crossing_out = combined(True, static_routed, own_routed, match_routed).astype(jnp.bfloat16)
    crossing = from_partner(crossing_out, top)
    slow_float = after(slow_down[0, 0], crossing_out).astype(jnp.float32)
    staying = combined(False, static_routed, own_routed, match_routed)
    outer_here = (0.5 + pull_rate) * slow_float - 0.5 * down_float + staying
    pull = outer_rate * (1.0 + moment_rate)
    kept = (
        slow_float
        - pull * outer_here
        - (outer_rate * moment_rate * moment_rate) * momentum[0, 0].astype(jnp.float32)
    )
    kept = after(kept, crossing_out)
    new_slow = (kept - pull * crossing.astype(jnp.float32)).astype(jnp.bfloat16)

    if line is not None:
        down_mat = side_by_side(line.down_here((crossing_out,)))
    hidden_grad = lax.dot_general(
        cotangent, down_mat, contract, preferred_element_type=jnp.float32
    )
    gate_grad = (
        hidden_grad * up_act * sigmoid_gate * (1.0 + gate_act * (1.0 - sigmoid_gate))
    ).astype(jnp.bfloat16)
    up_grad = (hidden_grad * gate_act * sigmoid_gate).astype(jnp.bfloat16)
    slot_grad = (
        lax.dot_general(gate_grad, gate_mat, contract, preferred_element_type=jnp.float32)
        + lax.dot_general(up_grad, up_mat, contract, preferred_element_type=jnp.float32)
    ).astype(jnp.bfloat16)
    slot_grad = slot_grad.reshape(sections, capacity, model_width)
    returned = lax.all_to_all(slot_grad, "section", split_axis=0, concat_axis=0, tiled=True)
    input_grad = jnp.dot(
        selector, returned.reshape(-1, model_width), preferred_element_type=jnp.float32
    ).astype(jnp.bfloat16)
    return (input_grad[None, None], new_slow[None, None])


def solution(mesh):
    in_specs = (
        P("section", "rep", None, None),
        P("section", "rep", None, None),
        P(),
        P(),
        P("section", "rep", None, None),
        P("section", "rep", None, None),
        P("section", "rep", None, None),
        P("section", "rep", None, None),
        P("section", "rep", None, None),
        P("section", "rep", None, None, None),
    )
    out_specs = (P("section", "rep", None, None), P("section", "rep", None, None))
    return jax.shard_map(
        on_device, mesh=mesh, in_specs=in_specs, out_specs=out_specs, check_vma=False
    )
```

```python
import jax
import jax.numpy as jnp
from jax import lax
from jax.sharding import PartitionSpec as P

inner_rate = 0.05
pull_rate = 0.25
moment_rate = 0.9
outer_rate = 0.7

OUTWARD = [(1, 0), (2, 3)]
INWARD = [(0, 1), (3, 2)]
ACROSS = [(1, 2), (2, 1)]


def from_partner(value, distance):
    pairs = [(source, source ^ 2**distance) for source in range(lax.axis_size("rep"))]
    return lax.ppermute(value, "rep", pairs)


def bit_of(mask, index):
    return jnp.bitwise_and(jnp.right_shift(mask, index), 1) == 1


def route(value, mask, bits):
    for index in bits:
        value = jnp.where(bit_of(mask, index), from_partner(value, index), value)
    return value


def after(value, *earlier):
    return lax.optimization_barrier((value, *earlier))[0]


def slot_table(expert_ids, sections, capacity):
    expert_hot = (expert_ids[:, None] == jnp.arange(sections, dtype=jnp.int32)[None, :]).astype(
        jnp.int32
    )
    position = jnp.sum((jnp.cumsum(expert_hot, axis=0) - 1) * expert_hot, axis=1)
    slot_index = expert_ids * capacity + position
    return (
        slot_index[:, None] == jnp.arange(sections * capacity, dtype=jnp.int32)[None, :]
    ).astype(jnp.bfloat16)


def stacked(wide, width):
    return jnp.concatenate(jnp.split(wide, wide.shape[1] // width, axis=1), axis=0)


def side_by_side(tall):
    return jnp.concatenate(jnp.split(tall, tall.shape[0] // tall.shape[1], axis=0), axis=1)


class FourInLine:
    def __init__(self, gate, up, down, static_part, mask):
        replica = lax.axis_index("rep")
        self.inner = (replica == 1) | (replica == 2)
        self.near, self.far = mask == 1, mask == 3
        self.gate, self.up, self.down = gate, up, down
        self.static_part = static_part

    def forward(self):
        self.up_side = lax.ppermute(self.up, "rep", INWARD)
        self.gate_hub = lax.ppermute(self.gate, "rep", ACROSS)
        side, static_part, self.inner, self.near, self.far = lax.optimization_barrier(
            (self.up_side, self.static_part, self.inner, self.near, self.far)
        )
        first = jnp.where(self.far, side, self.up)
        second = jnp.where(self.far, self.up, side)
        first_in = lax.ppermute(first, "rep", ACROSS)
        send = jnp.where(self.inner, after(static_part, first), self.gate)
        self.one = from_partner(send, 0)
        self.quiet, self.first_in = send, first_in
        self.gate_edge = lax.ppermute(self.one, "rep", ACROSS)
        self.second = second

    def handed_up(self, earlier):
        first_in = after(self.first_in, *earlier)
        send = jnp.where(self.inner, jnp.where(self.near, self.up, first_in), self.down)
        self.two = from_partner(send, 0)
        self.up_hub = lax.ppermute(after(self.second, send), "rep", ACROSS)
        self.later = send

    def handed_gate(self, earlier):
        gate_edge = after(self.gate_edge, self.later, *earlier)
        gate_out = jnp.where(
            self.near, self.gate, jnp.where(self.far, gate_edge, self.gate_hub)
        )
        send = jnp.where(self.inner, gate_out, self.static_part)
        self.three = from_partner(send, 0)
        two = after(self.two, send)
        first = jnp.where(self.far, two, self.down)
        second = jnp.where(self.far, self.down, two)
        self.down_first = lax.ppermute(first, "rep", ACROSS)
        gate_in = jnp.where(
            self.near, self.one, jnp.where(self.far, self.gate_hub, self.gate_edge)
        )
        gate_here = jnp.where(self.inner, gate_in, self.three)
        self.up_hub, second, gate_here = lax.optimization_barrier(
            (self.up_hub, second, gate_here)
        )
        self.down_hub = lax.ppermute(second, "rep", ACROSS)
        up_in = jnp.where(self.near, self.up_side, self.up_hub)
        up_here = jnp.where(self.inner, up_in, self.two)
        static_in = jnp.where(self.inner, self.three, self.one)
        return gate_here, up_here, static_in

    def handed_down(self, earlier):
        send = jnp.where(self.near, self.down, after(self.down_first, *earlier))
        self.four = lax.ppermute(send, "rep", OUTWARD)
        return send

    def down_here(self, earlier):
        down_hub = after(self.down_hub, *earlier)
        down_in = jnp.where(self.near, self.two, down_hub)
        return jnp.where(self.inner, down_in, self.four)


def on_device(
    tokens,
    assign,
    route_mask,
    match_mask,
    gate_weight,
    up_weight,
    down_weight,
    slow_down,
    momentum,
    slot_cot,
):
    sections = lax.axis_size("section")
    levels = lax.axis_size("rep").bit_length() - 1
    section_here = lax.axis_index("section")
    token_rows = tokens[0, 0]
    expert_ids = assign[0, 0, :, 0]
    capacity = slot_cot.shape[3]
    model_width = token_rows.shape[1]
    own_mask = route_mask[section_here]
    match = match_mask[section_here]
    upward = list(range(levels))
    contract = (((1,), (1,)), ((), ()))
    hidden_width = gate_weight.shape[3]

    gate_raw, up_raw, down_raw = gate_weight[0, 0], up_weight[0, 0], down_weight[0, 0]
    slow_float = slow_down[0, 0].astype(jnp.float32)
    down_float = down_raw.astype(jnp.float32)
    static_part = ((0.5 - pull_rate) * slow_float - 0.5 * down_float).astype(jnp.bfloat16)

    selector = slot_table(expert_ids, sections, capacity)
    placed = lax.dot_general(
        selector, token_rows, (((0,), (0,)), ((), ())), preferred_element_type=jnp.float32
    )
    dispatched = placed.astype(jnp.bfloat16).reshape(sections, capacity, model_width)

    line = None
    if levels == 2:
        line = FourInLine(
            gate_raw,
            up_raw,
            stacked(down_raw, hidden_width),
            stacked(lax.optimization_barrier(static_part), hidden_width),
            own_mask,
        )
        line.forward()
        dispatched = after(dispatched, line.quiet)
        line.handed_up((dispatched,))
    arrived = lax.all_to_all(dispatched, "section", split_axis=0, concat_axis=0, tiled=True)
    rows = arrived.reshape(-1, model_width)
    cotangent = slot_cot[0, 0].reshape(-1, model_width)
    if line is not None:
        gate_mat, up_mat, static_in = line.handed_gate((rows,))
        static_in = side_by_side(static_in)
    else:
        gate_mat, up_mat, down_mat = [
            route(weight, own_mask, upward) for weight in (gate_raw, up_raw, down_raw)
        ]
        static_in = from_partner(static_part, 0)

    gate_act = jnp.dot(rows, gate_mat, preferred_element_type=jnp.float32)
    up_act = jnp.dot(rows, up_mat, preferred_element_type=jnp.float32)
    sigmoid_gate = jax.nn.sigmoid(gate_act)
    hidden = (gate_act * sigmoid_gate * up_act).astype(jnp.bfloat16)
    down_grad = lax.dot_general(
        hidden, cotangent, (((0,), (0,)), ((), ())), preferred_element_type=jnp.float32
    ).astype(jnp.bfloat16)

    match_mine = jnp.bitwise_xor(own_mask, match)
    lower, top = upward[:-1], levels - 1
    down_grad_in = from_partner(down_grad, 0)
    if line is not None:
        sent = line.handed_down((down_grad,))
        static_in = after(static_in, sent)
        down_grad_in = after(down_grad_in, static_in)
    own_routed, match_routed, static_routed = down_grad, down_grad, static_part
    for index in lower:
        if index == 0:
            own_in, match_in, static_here = down_grad_in, down_grad_in, static_in
        else:
            own_in = from_partner(own_routed, index)
            match_in = from_partner(match_routed, index)
            static_here = from_partner(static_routed, index)
        own_routed = jnp.where(bit_of(own_mask, index), own_in, own_routed)
        match_routed = jnp.where(bit_of(match_mine, index), match_in, match_routed)
        static_routed = jnp.where(bit_of(match, index), static_here, static_routed)

    def combined(side, static_routed, own_routed, match_routed):
        def pick(mask, value):
            return jnp.where(bit_of(mask, top) == side, value.astype(jnp.float32), 0.0)

        return pick(match, static_routed) + 0.5 * inner_rate * (
            pick(own_mask, own_routed) + pick(match_mine, match_routed)
        )

    crossing_out = combined(True, static_routed, own_routed, match_routed).astype(jnp.bfloat16)
    crossing = from_partner(crossing_out, top)
    slow_float = after(slow_down[0, 0], crossing_out).astype(jnp.float32)
    staying = combined(False, static_routed, own_routed, match_routed)
    outer_here = (0.5 + pull_rate) * slow_float - 0.5 * down_float + staying
    pull = outer_rate * (1.0 + moment_rate)
    kept = (
        slow_float
        - pull * outer_here
        - (outer_rate * moment_rate * moment_rate) * momentum[0, 0].astype(jnp.float32)
    )
    kept = after(kept, crossing_out)
    new_slow = (kept - pull * crossing.astype(jnp.float32)).astype(jnp.bfloat16)

    if line is not None:
        down_mat = side_by_side(line.down_here((crossing_out,)))
    hidden_grad = lax.dot_general(
        cotangent, down_mat, contract, preferred_element_type=jnp.float32
    )
    gate_grad = (
        hidden_grad * up_act * sigmoid_gate * (1.0 + gate_act * (1.0 - sigmoid_gate))
    ).astype(jnp.bfloat16)
    up_grad = (hidden_grad * gate_act * sigmoid_gate).astype(jnp.bfloat16)
    slot_grad = (
        lax.dot_general(gate_grad, gate_mat, contract, preferred_element_type=jnp.float32)
        + lax.dot_general(up_grad, up_mat, contract, preferred_element_type=jnp.float32)
    ).astype(jnp.bfloat16)
    slot_grad = slot_grad.reshape(sections, capacity, model_width)
    returned = lax.all_to_all(slot_grad, "section", split_axis=0, concat_axis=0, tiled=True)
    input_grad = jnp.dot(
        selector, returned.reshape(-1, model_width), preferred_element_type=jnp.float32
    ).astype(jnp.bfloat16)
    return (input_grad[None, None], new_slow[None, None])


def solution(mesh):
    in_specs = (
        P("section", "rep", None, None),
        P("section", "rep", None, None),
        P(),
        P(),
        P("section", "rep", None, None),
        P("section", "rep", None, None),
        P("section", "rep", None, None),
        P("section", "rep", None, None),
        P("section", "rep", None, None),
        P("section", "rep", None, None, None),
    )
    out_specs = (P("section", "rep", None, None), P("section", "rep", None, None))
    return jax.shard_map(
        on_device, mesh=mesh, in_specs=in_specs, out_specs=out_specs, check_vma=False
    )
```

```python
import jax
import jax.numpy as jnp
from jax import lax
from jax.sharding import PartitionSpec as P

inner_rate = 0.05
pull_rate = 0.25
moment_rate = 0.9
outer_rate = 0.7

OUTWARD = [(1, 0), (2, 3)]
INWARD = [(0, 1), (3, 2)]
ACROSS = [(1, 2), (2, 1)]


def from_partner(value, distance):
    pairs = [(source, source ^ 2**distance) for source in range(lax.axis_size("rep"))]
    return lax.ppermute(value, "rep", pairs)


def bit_of(mask, index):
    return jnp.bitwise_and(jnp.right_shift(mask, index), 1) == 1


def route(value, mask, bits):
    for index in bits:
        value = jnp.where(bit_of(mask, index), from_partner(value, index), value)
    return value


def after(value, *earlier):
    return lax.optimization_barrier((value, *earlier))[0]


def slot_table(expert_ids, sections, capacity):
    expert_hot = (expert_ids[:, None] == jnp.arange(sections, dtype=jnp.int32)[None, :]).astype(
        jnp.int32
    )
    position = jnp.sum((jnp.cumsum(expert_hot, axis=0) - 1) * expert_hot, axis=1)
    slot_index = expert_ids * capacity + position
    return (
        slot_index[:, None] == jnp.arange(sections * capacity, dtype=jnp.int32)[None, :]
    ).astype(jnp.bfloat16)


def stacked(wide, width):
    return jnp.concatenate(jnp.split(wide, wide.shape[1] // width, axis=1), axis=0)


def side_by_side(tall):
    return jnp.concatenate(jnp.split(tall, tall.shape[0] // tall.shape[1], axis=0), axis=1)


class FourInLine:
    def __init__(self, gate, up, down, static_part, mask):
        replica = lax.axis_index("rep")
        self.inner = (replica == 1) | (replica == 2)
        self.near, self.far = mask == 1, mask == 3
        self.gate, self.up, self.down = gate, up, down
        self.static_part = static_part

    def forward(self):
        self.up_side = lax.ppermute(self.up, "rep", INWARD)
        self.gate_hub = lax.ppermute(self.gate, "rep", ACROSS)
        side, self.gate_hub, static_part, self.inner, self.near, self.far = (
            lax.optimization_barrier(
                (
                    self.up_side,
                    self.gate_hub,
                    self.static_part,
                    self.inner,
                    self.near,
                    self.far,
                )
            )
        )
        first = jnp.where(self.far, side, self.up)
        second = jnp.where(self.far, self.up, side)
        first_in = lax.ppermute(first, "rep", ACROSS)
        send = jnp.where(self.inner, after(static_part, first), self.gate)
        self.one = from_partner(send, 0)
        self.quiet, self.first_in = send, first_in
        self.gate_edge = lax.ppermute(self.one, "rep", ACROSS)
        self.second = second

    def handed_up(self, earlier):
        first_in = after(self.first_in, *earlier)
        send = jnp.where(self.inner, jnp.where(self.near, self.up, first_in), self.down)
        self.two = from_partner(send, 0)
        self.up_hub = lax.ppermute(after(self.second, send), "rep", ACROSS)
        self.later = send

    def handed_gate(self, earlier):
        gate_edge = after(self.gate_edge, self.later, *earlier)
        gate_out = jnp.where(
            self.near, self.gate, jnp.where(self.far, gate_edge, self.gate_hub)
        )
        send = jnp.where(self.inner, gate_out, self.static_part)
        self.three = from_partner(send, 0)
        two, self.up_hub = lax.optimization_barrier((self.two, self.up_hub, send))[:2]
        first = jnp.where(self.far, two, self.down)
        second = jnp.where(self.far, self.down, two)
        self.down_first = lax.ppermute(first, "rep", ACROSS)
        gate_in = jnp.where(
            self.near, self.one, jnp.where(self.far, self.gate_hub, self.gate_edge)
        )
        gate_here = jnp.where(self.inner, gate_in, self.three)
        second, gate_here = lax.optimization_barrier((second, gate_here))
        self.down_hub = lax.ppermute(second, "rep", ACROSS)
        up_in = jnp.where(self.near, self.up_side, self.up_hub)
        up_here = jnp.where(self.inner, up_in, self.two)
        static_in = jnp.where(self.inner, self.three, self.one)
        return gate_here, up_here, static_in

    def handed_down(self, earlier):
        send = jnp.where(self.near, self.down, after(self.down_first, *earlier))
        self.four = lax.ppermute(send, "rep", OUTWARD)
        return send

    def down_here(self, earlier):
        down_hub = after(self.down_hub, *earlier)
        down_in = jnp.where(self.near, self.two, down_hub)
        return jnp.where(self.inner, down_in, self.four)


def on_device(
    tokens,
    assign,
    route_mask,
    match_mask,
    gate_weight,
    up_weight,
    down_weight,
    slow_down,
    momentum,
    slot_cot,
):
    sections = lax.axis_size("section")
    levels = lax.axis_size("rep").bit_length() - 1
    section_here = lax.axis_index("section")
    token_rows = tokens[0, 0]
    expert_ids = assign[0, 0, :, 0]
    capacity = slot_cot.shape[3]
    model_width = token_rows.shape[1]
    own_mask = route_mask[section_here]
    match = match_mask[section_here]
    upward = list(range(levels))
    contract = (((1,), (1,)), ((), ()))
    hidden_width = gate_weight.shape[3]

    gate_raw, up_raw, down_raw = gate_weight[0, 0], up_weight[0, 0], down_weight[0, 0]
    slow_float = slow_down[0, 0].astype(jnp.float32)
    down_float = down_raw.astype(jnp.float32)
    static_part = ((0.5 - pull_rate) * slow_float - 0.5 * down_float).astype(jnp.bfloat16)

    selector = slot_table(expert_ids, sections, capacity)
    placed = lax.dot_general(
        selector, token_rows, (((0,), (0,)), ((), ())), preferred_element_type=jnp.float32
    )
    dispatched = placed.astype(jnp.bfloat16).reshape(sections, capacity, model_width)

    line = None
    if levels == 2:
        line = FourInLine(
            gate_raw,
            up_raw,
            stacked(down_raw, hidden_width),
            stacked(lax.optimization_barrier(static_part), hidden_width),
            own_mask,
        )
        line.forward()
        dispatched = after(dispatched, line.quiet)
        line.handed_up((dispatched,))
    arrived = lax.all_to_all(dispatched, "section", split_axis=0, concat_axis=0, tiled=True)
    rows = arrived.reshape(-1, model_width)
    cotangent = slot_cot[0, 0].reshape(-1, model_width)
    if line is not None:
        gate_mat, up_mat, static_in = line.handed_gate((rows,))
        static_in = side_by_side(static_in)
    else:
        gate_mat, up_mat, down_mat = [
            route(weight, own_mask, upward) for weight in (gate_raw, up_raw, down_raw)
        ]
        static_in = from_partner(static_part, 0)

    gate_act = jnp.dot(rows, gate_mat, preferred_element_type=jnp.float32)
    up_act = jnp.dot(rows, up_mat, preferred_element_type=jnp.float32)
    sigmoid_gate = jax.nn.sigmoid(gate_act)
    hidden = (gate_act * sigmoid_gate * up_act).astype(jnp.bfloat16)
    down_grad = lax.dot_general(
        hidden, cotangent, (((0,), (0,)), ((), ())), preferred_element_type=jnp.float32
    ).astype(jnp.bfloat16)

    match_mine = jnp.bitwise_xor(own_mask, match)
    lower, top = upward[:-1], levels - 1
    down_grad_in = from_partner(down_grad, 0)
    if line is not None:
        sent = line.handed_down((down_grad,))
        static_in = after(static_in, sent)
        down_grad_in = after(down_grad_in, static_in, line.down_hub)
    own_routed, match_routed, static_routed = down_grad, down_grad, static_part
    for index in lower:
        if index == 0:
            own_in, match_in, static_here = down_grad_in, down_grad_in, static_in
        else:
            own_in = from_partner(own_routed, index)
            match_in = from_partner(match_routed, index)
            static_here = from_partner(static_routed, index)
        own_routed = jnp.where(bit_of(own_mask, index), own_in, own_routed)
        match_routed = jnp.where(bit_of(match_mine, index), match_in, match_routed)
        static_routed = jnp.where(bit_of(match, index), static_here, static_routed)

    def combined(side, static_routed, own_routed, match_routed):
        def pick(mask, value):
            return jnp.where(bit_of(mask, top) == side, value.astype(jnp.float32), 0.0)

        return pick(match, static_routed) + 0.5 * inner_rate * (
            pick(own_mask, own_routed) + pick(match_mine, match_routed)
        )

    crossing_out = combined(True, static_routed, own_routed, match_routed).astype(jnp.bfloat16)
    crossing = from_partner(crossing_out, top)
    slow_float = after(slow_down[0, 0], crossing_out).astype(jnp.float32)
    staying = combined(False, static_routed, own_routed, match_routed)
    outer_here = (0.5 + pull_rate) * slow_float - 0.5 * down_float + staying
    pull = outer_rate * (1.0 + moment_rate)
    kept = (
        slow_float
        - pull * outer_here
        - (outer_rate * moment_rate * moment_rate) * momentum[0, 0].astype(jnp.float32)
    )
    kept = after(kept, crossing_out)
    new_slow = (kept - pull * crossing.astype(jnp.float32)).astype(jnp.bfloat16)

    if line is not None:
        down_mat = side_by_side(line.down_here((crossing_out,)))
    hidden_grad = lax.dot_general(
        cotangent, down_mat, contract, preferred_element_type=jnp.float32
    )
    gate_grad = (
        hidden_grad * up_act * sigmoid_gate * (1.0 + gate_act * (1.0 - sigmoid_gate))
    ).astype(jnp.bfloat16)
    up_grad = (hidden_grad * gate_act * sigmoid_gate).astype(jnp.bfloat16)
    slot_grad = (
        lax.dot_general(gate_grad, gate_mat, contract, preferred_element_type=jnp.float32)
        + lax.dot_general(up_grad, up_mat, contract, preferred_element_type=jnp.float32)
    ).astype(jnp.bfloat16)
    slot_grad = slot_grad.reshape(sections, capacity, model_width)
    returned = lax.all_to_all(slot_grad, "section", split_axis=0, concat_axis=0, tiled=True)
    input_grad = jnp.dot(
        selector, returned.reshape(-1, model_width), preferred_element_type=jnp.float32
    ).astype(jnp.bfloat16)
    return (input_grad[None, None], new_slow[None, None])


def solution(mesh):
    in_specs = (
        P("section", "rep", None, None),
        P("section", "rep", None, None),
        P(),
        P(),
        P("section", "rep", None, None),
        P("section", "rep", None, None),
        P("section", "rep", None, None),
        P("section", "rep", None, None),
        P("section", "rep", None, None),
        P("section", "rep", None, None, None),
    )
    out_specs = (P("section", "rep", None, None), P("section", "rep", None, None))
    return jax.shard_map(
        on_device, mesh=mesh, in_specs=in_specs, out_specs=out_specs, check_vma=False
    )
```

```python
import jax
import jax.numpy as jnp
from jax import lax
from jax.sharding import PartitionSpec as P

inner_rate = 0.05
pull_rate = 0.25
moment_rate = 0.9
outer_rate = 0.7

OUTWARD = [(1, 0), (2, 3)]
INWARD = [(0, 1), (3, 2)]
ACROSS = [(1, 2), (2, 1)]


def from_partner(value, distance):
    pairs = [(source, source ^ 2**distance) for source in range(lax.axis_size("rep"))]
    return lax.ppermute(value, "rep", pairs)


def bit_of(mask, index):
    return jnp.bitwise_and(jnp.right_shift(mask, index), 1) == 1


def route(value, mask, bits):
    for index in bits:
        value = jnp.where(bit_of(mask, index), from_partner(value, index), value)
    return value


def after(value, *earlier):
    return lax.optimization_barrier((value, *earlier))[0]


def slot_table(expert_ids, sections, capacity):
    expert_hot = (expert_ids[:, None] == jnp.arange(sections, dtype=jnp.int32)[None, :]).astype(
        jnp.int32
    )
    position = jnp.sum((jnp.cumsum(expert_hot, axis=0) - 1) * expert_hot, axis=1)
    slot_index = expert_ids * capacity + position
    return (
        slot_index[:, None] == jnp.arange(sections * capacity, dtype=jnp.int32)[None, :]
    ).astype(jnp.bfloat16)


def stacked(wide, width):
    return jnp.concatenate(jnp.split(wide, wide.shape[1] // width, axis=1), axis=0)


def side_by_side(tall):
    return jnp.concatenate(jnp.split(tall, tall.shape[0] // tall.shape[1], axis=0), axis=1)


class FourInLine:
    def __init__(self, gate, up, down, static_wide, width, mask):
        replica = lax.axis_index("rep")
        self.inner = (replica == 1) | (replica == 2)
        self.near, self.far = mask == 1, mask == 3
        self.gate, self.up, self.down = gate, up, stacked(down, width)
        self.static_wide = static_wide
        self.static_part = stacked(lax.optimization_barrier(static_wide), width)

    def start(self):
        gate_side = lax.ppermute(self.gate, "rep", INWARD)
        gate_hub = lax.ppermute(self.gate, "rep", ACROSS)
        send = jnp.where(self.inner, self.down, self.up)
        gate_side, gate_hub, send, self.inner, self.near, self.far = lax.optimization_barrier(
            (gate_side, gate_hub, send, self.inner, self.near, self.far)
        )
        self.gate_side, self.gate_hub = gate_side, gate_hub
        self.gate_edge = lax.ppermute(gate_side, "rep", ACROSS)
        self.one = from_partner(send, 0)
        return gate_side

    def hand_gate(self, *earlier):
        gate_edge = after(self.gate_edge, *earlier)
        gate_out = jnp.where(
            self.near, self.gate, jnp.where(self.far, gate_edge, self.gate_hub)
        )
        send = jnp.where(self.inner, gate_out, self.down)
        self.two = from_partner(send, 0)
        one = after(self.one, send)
        first = jnp.where(self.far, one, self.up)
        self.second = jnp.where(self.far, self.up, one)
        self.up_first = lax.ppermute(first, "rep", ACROSS)
        self.static_out = lax.ppermute(self.static_wide, "rep", OUTWARD)
        return send

    def hand_up(self, *earlier):
        up_first, static_out = lax.optimization_barrier(
            (self.up_first, self.static_out, *earlier)
        )[:2]
        self.static_out = static_out
        up_out = jnp.where(self.near, self.up, up_first)
        send = jnp.where(self.inner, up_out, self.static_part)
        self.three = from_partner(send, 0)
        self.up_hub = lax.ppermute(after(self.second, send), "rep", ACROSS)
        two = after(self.two, send)
        self.down_side = jnp.where(self.inner, two, self.one)
        crossing = jnp.where(self.far, self.down_side, self.down)
        self.down_far = from_partner(crossing, 1)
        gate_in = jnp.where(
            self.near, self.gate_side, jnp.where(self.far, self.gate_hub, self.gate_edge)
        )
        gate_here = jnp.where(self.inner, gate_in, two)
        up_in = jnp.where(self.near, self.one, self.up_hub)
        up_here = jnp.where(self.inner, up_in, self.three)
        static_in = jnp.where(self.inner, side_by_side(self.three), self.static_out)
        return gate_here, up_here, static_in

    def down_here(self, *earlier):
        down_far = after(self.down_far, *earlier)
        return side_by_side(jnp.where(self.near, self.down_side, down_far))


def on_device(
    tokens,
    assign,
    route_mask,
    match_mask,
    gate_weight,
    up_weight,
    down_weight,
    slow_down,
    momentum,
    slot_cot,
):
    sections = lax.axis_size("section")
    levels = lax.axis_size("rep").bit_length() - 1
    section_here = lax.axis_index("section")
    token_rows = tokens[0, 0]
    expert_ids = assign[0, 0, :, 0]
    capacity = slot_cot.shape[3]
    model_width = token_rows.shape[1]
    own_mask = route_mask[section_here]
    match = match_mask[section_here]
    upward = list(range(levels))
    contract = (((1,), (1,)), ((), ()))
    hidden_width = gate_weight.shape[3]

    gate_raw, up_raw, down_raw = gate_weight[0, 0], up_weight[0, 0], down_weight[0, 0]
    slow_float = slow_down[0, 0].astype(jnp.float32)
    down_float = down_raw.astype(jnp.float32)
    static_part = ((0.5 - pull_rate) * slow_float - 0.5 * down_float).astype(jnp.bfloat16)

    selector = slot_table(expert_ids, sections, capacity)
    placed = lax.dot_general(
        selector, token_rows, (((0,), (0,)), ((), ())), preferred_element_type=jnp.float32
    )
    dispatched = placed.astype(jnp.bfloat16).reshape(sections, capacity, model_width)

    line = None
    if levels == 2:
        line = FourInLine(gate_raw, up_raw, down_raw, static_part, hidden_width, own_mask)
        dispatched = after(dispatched, line.start())
    arrived = lax.all_to_all(dispatched, "section", split_axis=0, concat_axis=0, tiled=True)
    rows = arrived.reshape(-1, model_width)
    cotangent = slot_cot[0, 0].reshape(-1, model_width)
    if line is not None:
        line.hand_gate(dispatched)
        gate_mat, up_mat, static_in = line.hand_up(rows)
    else:
        gate_mat, up_mat, down_mat = [
            route(weight, own_mask, upward) for weight in (gate_raw, up_raw, down_raw)
        ]
        static_in = from_partner(static_part, 0)

    gate_act = jnp.dot(rows, gate_mat, preferred_element_type=jnp.float32)
    up_act = jnp.dot(rows, up_mat, preferred_element_type=jnp.float32)
    sigmoid_gate = jax.nn.sigmoid(gate_act)
    hidden = (gate_act * sigmoid_gate * up_act).astype(jnp.bfloat16)
    down_grad = lax.dot_general(
        hidden, cotangent, (((0,), (0,)), ((), ())), preferred_element_type=jnp.float32
    ).astype(jnp.bfloat16)

    match_mine = jnp.bitwise_xor(own_mask, match)
    lower, top = upward[:-1], levels - 1
    down_grad_in = from_partner(down_grad, 0)
    if line is not None:
        down_grad_in = after(down_grad_in, line.down_far)
    own_routed, match_routed, static_routed = down_grad, down_grad, static_part
    for index in lower:
        if index == 0:
            own_in, match_in, static_here = down_grad_in, down_grad_in, static_in
        else:
            own_in = from_partner(own_routed, index)
            match_in = from_partner(match_routed, index)
            static_here = from_partner(static_routed, index)
        own_routed = jnp.where(bit_of(own_mask, index), own_in, own_routed)
        match_routed = jnp.where(bit_of(match_mine, index), match_in, match_routed)
        static_routed = jnp.where(bit_of(match, index), static_here, static_routed)

    def combined(side, static_routed, own_routed, match_routed):
        def pick(mask, value):
            return jnp.where(bit_of(mask, top) == side, value.astype(jnp.float32), 0.0)

        return pick(match, static_routed) + 0.5 * inner_rate * (
            pick(own_mask, own_routed) + pick(match_mine, match_routed)
        )

    crossing_out = combined(True, static_routed, own_routed, match_routed).astype(jnp.bfloat16)
    crossing = from_partner(crossing_out, top)
    slow_float = after(slow_down[0, 0], crossing_out).astype(jnp.float32)
    staying = combined(False, static_routed, own_routed, match_routed)
    outer_here = (0.5 + pull_rate) * slow_float - 0.5 * down_float + staying
    pull = outer_rate * (1.0 + moment_rate)
    kept = (
        slow_float
        - pull * outer_here
        - (outer_rate * moment_rate * moment_rate) * momentum[0, 0].astype(jnp.float32)
    )
    kept = after(kept, crossing_out)
    new_slow = (kept - pull * crossing.astype(jnp.float32)).astype(jnp.bfloat16)

    if line is not None:
        down_mat = line.down_here(crossing_out)
    hidden_grad = lax.dot_general(
        cotangent, down_mat, contract, preferred_element_type=jnp.float32
    )
    gate_grad = (
        hidden_grad * up_act * sigmoid_gate * (1.0 + gate_act * (1.0 - sigmoid_gate))
    ).astype(jnp.bfloat16)
    up_grad = (hidden_grad * gate_act * sigmoid_gate).astype(jnp.bfloat16)
    slot_grad = (
        lax.dot_general(gate_grad, gate_mat, contract, preferred_element_type=jnp.float32)
        + lax.dot_general(up_grad, up_mat, contract, preferred_element_type=jnp.float32)
    ).astype(jnp.bfloat16)
    slot_grad = slot_grad.reshape(sections, capacity, model_width)
    returned = lax.all_to_all(slot_grad, "section", split_axis=0, concat_axis=0, tiled=True)
    input_grad = jnp.dot(
        selector, returned.reshape(-1, model_width), preferred_element_type=jnp.float32
    ).astype(jnp.bfloat16)
    return (input_grad[None, None], new_slow[None, None])


def solution(mesh):
    in_specs = (
        P("section", "rep", None, None),
        P("section", "rep", None, None),
        P(),
        P(),
        P("section", "rep", None, None),
        P("section", "rep", None, None),
        P("section", "rep", None, None),
        P("section", "rep", None, None),
        P("section", "rep", None, None),
        P("section", "rep", None, None, None),
    )
    out_specs = (P("section", "rep", None, None), P("section", "rep", None, None))
    return jax.shard_map(
        on_device, mesh=mesh, in_specs=in_specs, out_specs=out_specs, check_vma=False
    )
```

```python
import jax
import jax.numpy as jnp
from jax import lax
from jax.sharding import PartitionSpec as P

inner_rate = 0.05
pull_rate = 0.25
moment_rate = 0.9
outer_rate = 0.7

OUTWARD = [(1, 0), (2, 3)]
INWARD = [(0, 1), (3, 2)]
ACROSS = [(1, 2), (2, 1)]


def from_partner(value, distance):
    pairs = [(source, source ^ 2**distance) for source in range(lax.axis_size("rep"))]
    return lax.ppermute(value, "rep", pairs)


def bit_of(mask, index):
    return jnp.bitwise_and(jnp.right_shift(mask, index), 1) == 1


def route(value, mask, bits):
    for index in bits:
        value = jnp.where(bit_of(mask, index), from_partner(value, index), value)
    return value


def after(value, *earlier):
    return lax.optimization_barrier((value, *earlier))[0]


def slot_table(expert_ids, sections, capacity):
    expert_hot = (expert_ids[:, None] == jnp.arange(sections, dtype=jnp.int32)[None, :]).astype(
        jnp.int32
    )
    position = jnp.sum((jnp.cumsum(expert_hot, axis=0) - 1) * expert_hot, axis=1)
    slot_index = expert_ids * capacity + position
    return (
        slot_index[:, None] == jnp.arange(sections * capacity, dtype=jnp.int32)[None, :]
    ).astype(jnp.bfloat16)


def stacked(wide, width):
    return jnp.concatenate(jnp.split(wide, wide.shape[1] // width, axis=1), axis=0)


def side_by_side(tall):
    return jnp.concatenate(jnp.split(tall, tall.shape[0] // tall.shape[1], axis=0), axis=1)


class FourInLine:
    def __init__(self, lead, rest, down, static_wide, width, mask):
        replica = lax.axis_index("rep")
        self.inner = (replica == 1) | (replica == 2)
        self.near, self.far = mask == 1, mask == 3
        self.lead, self.rest, self.down = lead, rest, stacked(down, width)
        self.static_wide = static_wide
        self.static_part = stacked(lax.optimization_barrier(static_wide), width)

    def start(self):
        lead_side = lax.ppermute(self.lead, "rep", INWARD)
        lead_hub = lax.ppermute(self.lead, "rep", ACROSS)
        inner, self.near, self.far, self.static_part = lax.optimization_barrier(
            (self.inner, self.near, self.far, self.static_part)
        )
        send = lax.optimization_barrier(jnp.where(inner, self.down, self.rest))
        self.one = from_partner(send, 0)
        self.static_out = lax.ppermute(self.static_wide, "rep", OUTWARD)
        lead_side, lead_hub, self.near, self.far = lax.optimization_barrier(
            (lead_side, lead_hub, self.near, self.far)
        )
        self.lead_side, self.lead_hub = lead_side, lead_hub
        self.lead_edge = lax.ppermute(lead_side, "rep", ACROSS)
        self.sent = send
        return lead_side

    def hand_lead(self, *earlier):
        self.lead_edge, self.one = lax.optimization_barrier(
            (self.lead_edge, self.one, self.sent, *earlier)
        )[:2]
        lead_out = jnp.where(
            self.near, self.lead, jnp.where(self.far, self.lead_edge, self.lead_hub)
        )
        send = lax.optimization_barrier(jnp.where(self.inner, lead_out, self.down))
        self.two = from_partner(send, 0)
        self.one, self.static_out = lax.optimization_barrier((self.one, self.static_out, send))[:2]
        first = jnp.where(self.far, self.one, self.rest)
        self.second = jnp.where(self.far, self.rest, self.one)
        self.rest_first = lax.ppermute(first, "rep", ACROSS)
        self.rest_hub = lax.ppermute(self.second, "rep", ACROSS)

    def lead_here(self, *earlier):
        rest_first = after(self.rest_first, *earlier)
        rest_out = jnp.where(self.near, self.rest, rest_first)
        send = lax.optimization_barrier(jnp.where(self.inner, rest_out, self.static_part))
        self.three = from_partner(send, 0)
        two = after(self.two, send)
        self.down_side = jnp.where(self.inner, two, self.one)
        crossing = lax.optimization_barrier(jnp.where(self.far, self.down_side, self.down))
        self.down_far = from_partner(crossing, 1)
        two, self.rest_hub = lax.optimization_barrier((two, self.rest_hub, crossing))[:2]
        lead_in = jnp.where(
            self.near, self.lead_side, jnp.where(self.far, self.lead_hub, self.lead_edge)
        )
        return jnp.where(self.inner, lead_in, two)

    def rest_here(self, *earlier):
        three, rest_hub = lax.optimization_barrier((self.three, self.rest_hub, *earlier))[:2]
        self.three = three
        rest_in = jnp.where(self.near, self.one, rest_hub)
        return jnp.where(self.inner, rest_in, three)

    def static_in(self, *earlier):
        three = after(self.three, *earlier)
        return jnp.where(self.inner, side_by_side(three), self.static_out)

    def down_here(self, *earlier):
        down_far = after(self.down_far, *earlier)
        return side_by_side(jnp.where(self.near, self.down_side, down_far))


def on_device(
    tokens,
    assign,
    route_mask,
    match_mask,
    gate_weight,
    up_weight,
    down_weight,
    slow_down,
    momentum,
    slot_cot,
):
    sections = lax.axis_size("section")
    levels = lax.axis_size("rep").bit_length() - 1
    section_here = lax.axis_index("section")
    token_rows = tokens[0, 0]
    expert_ids = assign[0, 0, :, 0]
    capacity = slot_cot.shape[3]
    model_width = token_rows.shape[1]
    own_mask = route_mask[section_here]
    match = match_mask[section_here]
    upward = list(range(levels))
    contract = (((1,), (1,)), ((), ()))
    hidden_width = gate_weight.shape[3]

    gate_raw, up_raw, down_raw = gate_weight[0, 0], up_weight[0, 0], down_weight[0, 0]
    half = hidden_width // 2
    pieces = [
        jnp.concatenate([gate_raw[:, start : start + half], up_raw[:, start : start + half]], axis=1)
        for start in (0, half)
    ]
    slow_float = slow_down[0, 0].astype(jnp.float32)
    down_float = down_raw.astype(jnp.float32)
    static_part = ((0.5 - pull_rate) * slow_float - 0.5 * down_float).astype(jnp.bfloat16)

    selector = slot_table(expert_ids, sections, capacity)
    placed = lax.dot_general(
        selector, token_rows, (((0,), (0,)), ((), ())), preferred_element_type=jnp.float32
    )
    dispatched = placed.astype(jnp.bfloat16).reshape(sections, capacity, model_width)

    line = None
    if levels == 2:
        line = FourInLine(*pieces, down_raw, static_part, hidden_width, own_mask)
        dispatched = after(dispatched, line.start())
    arrived = lax.all_to_all(dispatched, "section", split_axis=0, concat_axis=0, tiled=True)
    rows = arrived.reshape(-1, model_width)
    cotangent = slot_cot[0, 0].reshape(-1, model_width)
    if line is not None:
        line.hand_lead(dispatched)
        pieces = [line.lead_here(rows), None]
    else:
        *pieces, down_mat = [route(weight, own_mask, upward) for weight in (*pieces, down_raw)]
        static_in = from_partner(static_part, 0)

    acts, down_grads, down_grads_in = [], [], []
    for number in range(2):
        if pieces[number] is None:
            pieces[number] = line.rest_here(down_grads[-1])
        act = jnp.dot(rows, pieces[number], preferred_element_type=jnp.float32)
        gate_act, up_act = act[:, :half], act[:, half:]
        sigmoid_gate = jax.nn.sigmoid(gate_act)
        acts.append((gate_act, up_act, sigmoid_gate))
        hidden = (gate_act * sigmoid_gate * up_act).astype(jnp.bfloat16)
        down_grads.append(
            lax.dot_general(
                hidden, cotangent, (((0,), (0,)), ((), ())), preferred_element_type=jnp.float32
            ).astype(jnp.bfloat16)
        )
        down_grads_in.append(from_partner(down_grads[-1], 0))
    if line is not None:
        static_in = lax.optimization_barrier(line.static_in(down_grads[-1]))
        *down_grads_in, _, _ = lax.optimization_barrier((*down_grads_in, line.down_far, static_in))
    down_grad = jnp.concatenate(down_grads, axis=0)
    down_grad_in = jnp.concatenate(down_grads_in, axis=0)

    match_mine = jnp.bitwise_xor(own_mask, match)
    lower, top = upward[:-1], levels - 1
    own_routed, match_routed, static_routed = down_grad, down_grad, static_part
    for index in lower:
        if index == 0:
            own_in, match_in, static_here = down_grad_in, down_grad_in, static_in
        else:
            own_in = from_partner(own_routed, index)
            match_in = from_partner(match_routed, index)
            static_here = from_partner(static_routed, index)
        own_routed = jnp.where(bit_of(own_mask, index), own_in, own_routed)
        match_routed = jnp.where(bit_of(match_mine, index), match_in, match_routed)
        static_routed = jnp.where(bit_of(match, index), static_here, static_routed)

    def combined(side):
        def pick(mask, value):
            return jnp.where(bit_of(mask, top) == side, value.astype(jnp.float32), 0.0)

        return pick(match, static_routed) + 0.5 * inner_rate * (
            pick(own_mask, own_routed) + pick(match_mine, match_routed)
        )

    crossing_out = lax.optimization_barrier(combined(True).astype(jnp.bfloat16))
    crossing = from_partner(crossing_out, top)
    slow_float = after(slow_down[0, 0], crossing_out).astype(jnp.float32)
    outer_here = (0.5 + pull_rate) * slow_float - 0.5 * down_float + combined(False)
    pull = outer_rate * (1.0 + moment_rate)
    kept = (
        slow_float
        - pull * outer_here
        - (outer_rate * moment_rate * moment_rate) * momentum[0, 0].astype(jnp.float32)
    )
    kept = after(kept, crossing_out)
    new_slow = (kept - pull * crossing.astype(jnp.float32)).astype(jnp.bfloat16)

    if line is not None:
        down_mat = line.down_here(crossing_out)
    hidden_grad = lax.dot_general(
        cotangent, down_mat, contract, preferred_element_type=jnp.float32
    )
    slot_grad = 0.0
    for number, (gate_act, up_act, sigmoid_gate) in enumerate(acts):
        grad = hidden_grad[:, number * half : (number + 1) * half]
        gate_grad = grad * up_act * sigmoid_gate * (1.0 + gate_act * (1.0 - sigmoid_gate))
        up_grad = grad * gate_act * sigmoid_gate
        both = jnp.concatenate([gate_grad, up_grad], axis=1).astype(jnp.bfloat16)
        slot_grad += lax.dot_general(
            both, pieces[number], contract, preferred_element_type=jnp.float32
        )
    slot_grad = slot_grad.astype(jnp.bfloat16)
    slot_grad = slot_grad.reshape(sections, capacity, model_width)
    returned = lax.all_to_all(slot_grad, "section", split_axis=0, concat_axis=0, tiled=True)
    input_grad = jnp.dot(
        selector, returned.reshape(-1, model_width), preferred_element_type=jnp.float32
    ).astype(jnp.bfloat16)
    return (input_grad[None, None], new_slow[None, None])


def solution(mesh):
    in_specs = (
        P("section", "rep", None, None),
        P("section", "rep", None, None),
        P(),
        P(),
        P("section", "rep", None, None),
        P("section", "rep", None, None),
        P("section", "rep", None, None),
        P("section", "rep", None, None),
        P("section", "rep", None, None),
        P("section", "rep", None, None, None),
    )
    out_specs = (P("section", "rep", None, None), P("section", "rep", None, None))
    return jax.shard_map(
        on_device, mesh=mesh, in_specs=in_specs, out_specs=out_specs, check_vma=False
    )
```

```python
import jax
import jax.numpy as jnp
from jax import lax
from jax.sharding import PartitionSpec as P

inner_rate = 0.05
pull_rate = 0.25
moment_rate = 0.9
outer_rate = 0.7

OUTWARD = [(1, 0), (2, 3)]
INWARD = [(0, 1), (3, 2)]
ACROSS = [(1, 2), (2, 1)]


def from_partner(value, distance):
    pairs = [(source, source ^ 2**distance) for source in range(lax.axis_size("rep"))]
    return lax.ppermute(value, "rep", pairs)


def bit_of(mask, index):
    return jnp.bitwise_and(jnp.right_shift(mask, index), 1) == 1


def route(value, mask, bits):
    for index in bits:
        value = jnp.where(bit_of(mask, index), from_partner(value, index), value)
    return value


def after(value, *earlier):
    return lax.optimization_barrier((value, *earlier))[0]


def slot_table(expert_ids, sections, capacity):
    expert_hot = (expert_ids[:, None] == jnp.arange(sections, dtype=jnp.int32)[None, :]).astype(
        jnp.int32
    )
    position = jnp.sum((jnp.cumsum(expert_hot, axis=0) - 1) * expert_hot, axis=1)
    slot_index = expert_ids * capacity + position
    return (
        slot_index[:, None] == jnp.arange(sections * capacity, dtype=jnp.int32)[None, :]
    ).astype(jnp.bfloat16)


def stacked(wide, width):
    return jnp.concatenate(jnp.split(wide, wide.shape[1] // width, axis=1), axis=0)


def side_by_side(tall):
    return jnp.concatenate(jnp.split(tall, tall.shape[0] // tall.shape[1], axis=0), axis=1)


class FourInLine:
    def __init__(self, gate, up, down, static_part, mask):
        replica = lax.axis_index("rep")
        self.inner = (replica == 1) | (replica == 2)
        self.near, self.far = mask == 1, mask == 3
        self.gate, self.up, self.down = gate, up, down
        self.static_part = static_part
        self.static_tall = stacked(lax.optimization_barrier(static_part), gate.shape[1])

    def start(self, bits):
        self.up_side = lax.ppermute(self.up, "rep", INWARD)
        self.gate_far = from_partner(self.gate, 1)
        static_part = after(self.static_part, self.near)
        self.static_out = lax.ppermute(static_part, "rep", OUTWARD)
        up_side, self.inner, self.near, self.far, *bits = lax.optimization_barrier(
            (self.up_side, self.inner, self.near, self.far, *bits)
        )
        first = jnp.where(self.far, up_side, self.up)
        self.second = jnp.where(self.far, self.up, up_side)
        self.up_first = lax.ppermute(first, "rep", ACROSS)
        self.down_side = lax.ppermute(after(self.down, first), "rep", INWARD)
        self.up_hub = lax.ppermute(self.second, "rep", ACROSS)
        gate_far = after(self.gate_far, first)
        send = lax.optimization_barrier(jnp.where(self.far, gate_far, self.gate))
        self.gate_side = from_partner(send, 0)
        self.sent = send
        return bits

    def gate_up(self, *earlier):
        up_first, self.static_out = lax.optimization_barrier(
            (self.up_first, self.static_out, self.sent, *earlier)
        )[:2]
        up_out = jnp.where(self.near, self.up, up_first)
        send = lax.optimization_barrier(jnp.where(self.inner, up_out, self.static_tall))
        self.up_edge = from_partner(send, 0)
        down_side = after(self.down_side, send)
        first = jnp.where(self.far, down_side, self.down)
        second = jnp.where(self.far, self.down, down_side)
        self.down_first = lax.ppermute(first, "rep", ACROSS)
        self.down_hub = lax.ppermute(second, "rep", ACROSS)
        gate_side, up_hub = lax.optimization_barrier((self.gate_side, self.up_hub, first))[:2]
        gate_here = jnp.where(self.near | self.far, gate_side, self.gate_far)
        gate_here = lax.optimization_barrier(gate_here)
        self.up_edge = after(self.up_edge, gate_here)
        up_in = jnp.where(self.near, self.up_side, up_hub)
        return gate_here, jnp.where(self.inner, up_in, self.up_edge)

    def static_in(self, *earlier):
        edge = after(self.up_edge, *earlier)
        return jnp.where(self.inner, side_by_side(edge), self.static_out)

    def hand_down(self, *earlier):
        send = jnp.where(self.near, self.down, after(self.down_first, *earlier))
        self.handed = lax.ppermute(send, "rep", OUTWARD)
        return send

    def down_here(self, *earlier):
        down_hub = after(self.down_hub, *earlier)
        down_in = jnp.where(self.near, self.down_side, down_hub)
        return jnp.where(self.inner, down_in, self.handed)


def on_device(
    tokens,
    assign,
    route_mask,
    match_mask,
    gate_weight,
    up_weight,
    down_weight,
    slow_down,
    momentum,
    slot_cot,
):
    sections = lax.axis_size("section")
    levels = lax.axis_size("rep").bit_length() - 1
    section_here = lax.axis_index("section")
    token_rows = tokens[0, 0]
    expert_ids = assign[0, 0, :, 0]
    capacity = slot_cot.shape[3]
    model_width = token_rows.shape[1]
    own_mask = route_mask[section_here]
    match = match_mask[section_here]
    upward = list(range(levels))
    contract = (((1,), (1,)), ((), ()))
    match_mine = jnp.bitwise_xor(own_mask, match)
    masks = (own_mask, match_mine, match)
    bits = [bit_of(mask, index) for mask in masks for index in upward]
    gate_raw, up_raw, down_raw = gate_weight[0, 0], up_weight[0, 0], down_weight[0, 0]
    slow_float = slow_down[0, 0].astype(jnp.float32)
    down_float = down_raw.astype(jnp.float32)
    static_part = ((0.5 - pull_rate) * slow_float - 0.5 * down_float).astype(jnp.bfloat16)

    selector = slot_table(expert_ids, sections, capacity)
    placed = lax.dot_general(
        selector, token_rows, (((0,), (0,)), ((), ())), preferred_element_type=jnp.float32
    )
    dispatched = placed.astype(jnp.bfloat16).reshape(sections, capacity, model_width)

    line = None
    if levels == 2:
        line = FourInLine(gate_raw, up_raw, down_raw, static_part, own_mask)
        bits = line.start(bits)
    own_bits, mine_bits, match_bits = [
        bits[number * levels : (number + 1) * levels] for number in range(3)
    ]
    arrived = lax.all_to_all(dispatched, "section", split_axis=0, concat_axis=0, tiled=True)
    rows = arrived.reshape(-1, model_width)
    cotangent = slot_cot[0, 0].reshape(-1, model_width)
    if line is not None:
        gate_mat, up_mat = line.gate_up(rows)
    else:
        gate_mat, up_mat, down_mat = [
            route(weight, own_mask, upward) for weight in (gate_raw, up_raw, down_raw)
        ]
        static_in = from_partner(static_part, 0)

    gate_act = jnp.dot(rows, gate_mat, preferred_element_type=jnp.float32)
    up_act = jnp.dot(rows, up_mat, preferred_element_type=jnp.float32)
    sigmoid_gate = jax.nn.sigmoid(gate_act)
    hidden = (gate_act * sigmoid_gate * up_act).astype(jnp.bfloat16)
    down_grad = lax.dot_general(
        hidden, cotangent, (((0,), (0,)), ((), ())), preferred_element_type=jnp.float32
    ).astype(jnp.bfloat16)

    lower, top = upward[:-1], levels - 1
    down_grad_in = from_partner(down_grad, 0)
    if line is not None:
        sent = line.hand_down(down_grad)
        static_in = lax.optimization_barrier(line.static_in(down_grad))
        down_grad_in = after(down_grad_in, line.down_hub, static_in, sent)
    own_routed, match_routed, static_routed = down_grad, down_grad, static_part
    for index in lower:
        if index == 0:
            own_in, match_in, static_here = down_grad_in, down_grad_in, static_in
        else:
            own_in = from_partner(own_routed, index)
            match_in = from_partner(match_routed, index)
            static_here = from_partner(static_routed, index)
        own_routed = jnp.where(own_bits[index], own_in, own_routed)
        match_routed = jnp.where(mine_bits[index], match_in, match_routed)
        static_routed = jnp.where(match_bits[index], static_here, static_routed)

    def combined(side):
        def pick(bit, value):
            return jnp.where(bit == side, value.astype(jnp.float32), 0.0)

        return pick(match_bits[top], static_routed) + 0.5 * inner_rate * (
            pick(own_bits[top], own_routed) + pick(mine_bits[top], match_routed)
        )

    crossing_out = lax.optimization_barrier(combined(True).astype(jnp.bfloat16))
    crossing = from_partner(crossing_out, top)
    slow_float = after(slow_down[0, 0], crossing_out).astype(jnp.float32)
    outer_here = (0.5 + pull_rate) * slow_float - 0.5 * down_float + combined(False)
    pull = outer_rate * (1.0 + moment_rate)
    kept = (
        slow_float
        - pull * outer_here
        - (outer_rate * moment_rate * moment_rate) * momentum[0, 0].astype(jnp.float32)
    )
    kept = after(kept, crossing_out)
    new_slow = (kept - pull * crossing.astype(jnp.float32)).astype(jnp.bfloat16)

    if line is not None:
        down_mat = line.down_here(crossing_out)
    hidden_grad = lax.dot_general(
        cotangent, down_mat, contract, preferred_element_type=jnp.float32
    )
    gate_grad = (
        hidden_grad * up_act * sigmoid_gate * (1.0 + gate_act * (1.0 - sigmoid_gate))
    ).astype(jnp.bfloat16)
    up_grad = (hidden_grad * gate_act * sigmoid_gate).astype(jnp.bfloat16)
    slot_grad = (
        lax.dot_general(gate_grad, gate_mat, contract, preferred_element_type=jnp.float32)
        + lax.dot_general(up_grad, up_mat, contract, preferred_element_type=jnp.float32)
    ).astype(jnp.bfloat16)
    slot_grad = slot_grad.reshape(sections, capacity, model_width)
    returned = lax.all_to_all(slot_grad, "section", split_axis=0, concat_axis=0, tiled=True)
    input_grad = jnp.dot(
        selector, returned.reshape(-1, model_width), preferred_element_type=jnp.float32
    ).astype(jnp.bfloat16)
    return (input_grad[None, None], new_slow[None, None])


def solution(mesh):
    in_specs = (
        P("section", "rep", None, None),
        P("section", "rep", None, None),
        P(),
        P(),
        P("section", "rep", None, None),
        P("section", "rep", None, None),
        P("section", "rep", None, None),
        P("section", "rep", None, None),
        P("section", "rep", None, None),
        P("section", "rep", None, None, None),
    )
    out_specs = (P("section", "rep", None, None), P("section", "rep", None, None))
    return jax.shard_map(
        on_device, mesh=mesh, in_specs=in_specs, out_specs=out_specs, check_vma=False
    )
```

```python
import jax
import jax.numpy as jnp
from jax import lax
from jax.sharding import PartitionSpec as P

inner_rate = 0.05
pull_rate = 0.25
moment_rate = 0.9
outer_rate = 0.7

OUTWARD = [(1, 0), (2, 3)]
INWARD = [(0, 1), (3, 2)]
ACROSS = [(1, 2), (2, 1)]


def from_partner(value, distance):
    pairs = [(source, source ^ 2**distance) for source in range(lax.axis_size("rep"))]
    return lax.ppermute(value, "rep", pairs)


def bit_of(mask, index):
    return jnp.bitwise_and(jnp.right_shift(mask, index), 1) == 1


def route(value, mask, bits):
    for index in bits:
        value = jnp.where(bit_of(mask, index), from_partner(value, index), value)
    return value


def after(value, *earlier):
    return lax.optimization_barrier((value, *earlier))[0]


def slot_table(expert_ids, sections, capacity):
    expert_hot = (expert_ids[:, None] == jnp.arange(sections, dtype=jnp.int32)[None, :]).astype(
        jnp.int32
    )
    position = jnp.sum((jnp.cumsum(expert_hot, axis=0) - 1) * expert_hot, axis=1)
    slot_index = expert_ids * capacity + position
    return (
        slot_index[:, None] == jnp.arange(sections * capacity, dtype=jnp.int32)[None, :]
    ).astype(jnp.bfloat16)


def stacked(wide, width):
    return jnp.concatenate(jnp.split(wide, wide.shape[1] // width, axis=1), axis=0)


def side_by_side(tall):
    return jnp.concatenate(jnp.split(tall, tall.shape[0] // tall.shape[1], axis=0), axis=1)


class FourInLine:
    def __init__(self, gate, up, down, static_part, mask):
        replica = lax.axis_index("rep")
        self.inner = (replica == 1) | (replica == 2)
        self.near, self.far = mask == 1, mask == 3
        self.gate, self.up, self.down = gate, up, down
        self.static_part = static_part
        self.static_tall = stacked(lax.optimization_barrier(static_part), gate.shape[1])

    def start(self, bits):
        self.up_side = lax.ppermute(self.up, "rep", INWARD)
        self.gate_far = from_partner(self.gate, 1)
        static_part = after(self.static_part, self.near)
        self.static_out = lax.ppermute(static_part, "rep", OUTWARD)
        up_side, self.gate_far, self.inner, self.near, self.far, *bits = (
            lax.optimization_barrier(
                (self.up_side, self.gate_far, self.inner, self.near, self.far, *bits)
            )
        )
        first = jnp.where(self.far, up_side, self.up)
        self.second = jnp.where(self.far, self.up, up_side)
        self.up_first = lax.ppermute(first, "rep", ACROSS)
        self.down_side = lax.ppermute(after(self.down, first), "rep", INWARD)
        self.up_hub = lax.ppermute(self.second, "rep", ACROSS)
        self.sent = first
        return bits

    def gate_up(self, *earlier):
        gate_far = after(self.gate_far, self.sent, *earlier)
        send = lax.optimization_barrier(jnp.where(self.far, gate_far, self.gate))
        self.gate_side = from_partner(send, 0)
        up_first, self.static_out, down_side = lax.optimization_barrier(
            (self.up_first, self.static_out, self.down_side, send)
        )[:3]
        up_out = jnp.where(self.near, self.up, up_first)
        send = lax.optimization_barrier(jnp.where(self.inner, up_out, self.static_tall))
        self.up_edge = from_partner(send, 0)
        down_side = after(down_side, send)
        first = jnp.where(self.far, down_side, self.down)
        second = jnp.where(self.far, self.down, down_side)
        self.down_first = lax.ppermute(first, "rep", ACROSS)
        self.down_hub = lax.ppermute(second, "rep", ACROSS)
        gate_side, up_hub = lax.optimization_barrier((self.gate_side, self.up_hub, first))[:2]
        gate_here = jnp.where(self.near | self.far, gate_side, self.gate_far)
        gate_here = lax.optimization_barrier(gate_here)
        self.up_edge = after(self.up_edge, gate_here)
        up_in = jnp.where(self.near, self.up_side, up_hub)
        return gate_here, jnp.where(self.inner, up_in, self.up_edge)

    def static_in(self, *earlier):
        edge = after(self.up_edge, *earlier)
        return jnp.where(self.inner, side_by_side(edge), self.static_out)

    def hand_down(self, *earlier):
        send = jnp.where(self.near, self.down, after(self.down_first, *earlier))
        self.handed = lax.ppermute(send, "rep", OUTWARD)
        return send

    def down_here(self, *earlier):
        down_hub = after(self.down_hub, *earlier)
        down_in = jnp.where(self.near, self.down_side, down_hub)
        return jnp.where(self.inner, down_in, self.handed)


def on_device(
    tokens,
    assign,
    route_mask,
    match_mask,
    gate_weight,
    up_weight,
    down_weight,
    slow_down,
    momentum,
    slot_cot,
):
    sections = lax.axis_size("section")
    levels = lax.axis_size("rep").bit_length() - 1
    section_here = lax.axis_index("section")
    token_rows = tokens[0, 0]
    expert_ids = assign[0, 0, :, 0]
    capacity = slot_cot.shape[3]
    model_width = token_rows.shape[1]
    masks_here = lax.dynamic_index_in_dim(
        jnp.stack([route_mask, match_mask]), section_here, axis=1, keepdims=False
    )
    own_mask, match = masks_here[0], masks_here[1]
    upward = list(range(levels))
    contract = (((1,), (1,)), ((), ()))
    match_mine = jnp.bitwise_xor(own_mask, match)
    masks = (own_mask, match_mine, match)
    bits = [bit_of(mask, index) for mask in masks for index in upward]
    gate_raw, up_raw, down_raw = gate_weight[0, 0], up_weight[0, 0], down_weight[0, 0]
    slow_float = slow_down[0, 0].astype(jnp.float32)
    down_float = down_raw.astype(jnp.float32)
    static_part = ((0.5 - pull_rate) * slow_float - 0.5 * down_float).astype(jnp.bfloat16)

    selector = slot_table(expert_ids, sections, capacity)
    placed = lax.dot_general(
        selector, token_rows, (((0,), (0,)), ((), ())), preferred_element_type=jnp.float32
    )
    dispatched = placed.astype(jnp.bfloat16).reshape(sections, capacity, model_width)

    line = None
    if levels == 2:
        line = FourInLine(gate_raw, up_raw, down_raw, static_part, own_mask)
        bits = line.start(bits)
    own_bits, mine_bits, match_bits = [
        bits[number * levels : (number + 1) * levels] for number in range(3)
    ]
    arrived = lax.all_to_all(dispatched, "section", split_axis=0, concat_axis=0, tiled=True)
    rows = arrived.reshape(-1, model_width)
    cotangent = slot_cot[0, 0].reshape(-1, model_width)
    if line is not None:
        gate_mat, up_mat = line.gate_up(rows)
    else:
        gate_mat, up_mat, down_mat = [
            route(weight, own_mask, upward) for weight in (gate_raw, up_raw, down_raw)
        ]
        static_in = from_partner(static_part, 0)

    gate_act = jnp.dot(rows, gate_mat, preferred_element_type=jnp.float32)
    up_act = jnp.dot(rows, up_mat, preferred_element_type=jnp.float32)
    sigmoid_gate = jax.nn.sigmoid(gate_act)
    hidden = (gate_act * sigmoid_gate * up_act).astype(jnp.bfloat16)
    down_grad = lax.dot_general(
        hidden, cotangent, (((0,), (0,)), ((), ())), preferred_element_type=jnp.float32
    ).astype(jnp.bfloat16)

    lower, top = upward[:-1], levels - 1
    down_grad_in = from_partner(down_grad, 0)
    if line is not None:
        sent = line.hand_down(down_grad)
        static_in = lax.optimization_barrier(line.static_in(down_grad))
        down_grad_in = after(down_grad_in, line.down_hub, static_in, sent)
    own_routed, match_routed, static_routed = down_grad, down_grad, static_part
    for index in lower:
        if index == 0:
            own_in, match_in, static_here = down_grad_in, down_grad_in, static_in
        else:
            own_in = from_partner(own_routed, index)
            match_in = from_partner(match_routed, index)
            static_here = from_partner(static_routed, index)
        own_routed = jnp.where(own_bits[index], own_in, own_routed)
        match_routed = jnp.where(mine_bits[index], match_in, match_routed)
        static_routed = jnp.where(match_bits[index], static_here, static_routed)

    def combined(side):
        def pick(bit, value):
            return jnp.where(bit == side, value.astype(jnp.float32), 0.0)

        return pick(match_bits[top], static_routed) + 0.5 * inner_rate * (
            pick(own_bits[top], own_routed) + pick(mine_bits[top], match_routed)
        )

    crossing_out = lax.optimization_barrier(combined(True).astype(jnp.bfloat16))
    crossing = from_partner(crossing_out, top)
    slow_float = after(slow_down[0, 0], crossing_out).astype(jnp.float32)
    outer_here = (0.5 + pull_rate) * slow_float - 0.5 * down_float + combined(False)
    pull = outer_rate * (1.0 + moment_rate)
    kept = (
        slow_float
        - pull * outer_here
        - (outer_rate * moment_rate * moment_rate) * momentum[0, 0].astype(jnp.float32)
    )
    kept = after(kept, crossing_out)
    new_slow = (kept - pull * crossing.astype(jnp.float32)).astype(jnp.bfloat16)

    if line is not None:
        down_mat = line.down_here(crossing_out)
    hidden_grad = lax.dot_general(
        cotangent, down_mat, contract, preferred_element_type=jnp.float32
    )
    gate_grad = (
        hidden_grad * up_act * sigmoid_gate * (1.0 + gate_act * (1.0 - sigmoid_gate))
    ).astype(jnp.bfloat16)
    up_grad = (hidden_grad * gate_act * sigmoid_gate).astype(jnp.bfloat16)
    slot_grad = (
        lax.dot_general(gate_grad, gate_mat, contract, preferred_element_type=jnp.float32)
        + lax.dot_general(up_grad, up_mat, contract, preferred_element_type=jnp.float32)
    ).astype(jnp.bfloat16)
    slot_grad = slot_grad.reshape(sections, capacity, model_width)
    returned = lax.all_to_all(slot_grad, "section", split_axis=0, concat_axis=0, tiled=True)
    input_grad = jnp.dot(
        selector, returned.reshape(-1, model_width), preferred_element_type=jnp.float32
    ).astype(jnp.bfloat16)
    return (input_grad[None, None], new_slow[None, None])


def solution(mesh):
    in_specs = (
        P("section", "rep", None, None),
        P("section", "rep", None, None),
        P(),
        P(),
        P("section", "rep", None, None),
        P("section", "rep", None, None),
        P("section", "rep", None, None),
        P("section", "rep", None, None),
        P("section", "rep", None, None),
        P("section", "rep", None, None, None),
    )
    out_specs = (P("section", "rep", None, None), P("section", "rep", None, None))
    return jax.shard_map(
        on_device, mesh=mesh, in_specs=in_specs, out_specs=out_specs, check_vma=False
    )
```

```python
import jax
import jax.numpy as jnp
from jax import lax
from jax.sharding import PartitionSpec as P

inner_rate = 0.05
pull_rate = 0.25
moment_rate = 0.9
outer_rate = 0.7

OUTWARD = [(1, 0), (2, 3)]
INWARD = [(0, 1), (3, 2)]
ACROSS = [(1, 2), (2, 1)]


def from_partner(value, distance):
    pairs = [(source, source ^ 2**distance) for source in range(lax.axis_size("rep"))]
    return lax.ppermute(value, "rep", pairs)


def bit_of(mask, index):
    return jnp.bitwise_and(jnp.right_shift(mask, index), 1) == 1


def route(value, mask, bits):
    for index in bits:
        value = jnp.where(bit_of(mask, index), from_partner(value, index), value)
    return value


def after(value, *earlier):
    return lax.optimization_barrier((value, *earlier))[0]


def slot_table(expert_ids, sections, capacity):
    expert_hot = (expert_ids[:, None] == jnp.arange(sections, dtype=jnp.int32)[None, :]).astype(
        jnp.int32
    )
    position = jnp.sum((jnp.cumsum(expert_hot, axis=0) - 1) * expert_hot, axis=1)
    slot_index = expert_ids * capacity + position
    return (
        slot_index[:, None] == jnp.arange(sections * capacity, dtype=jnp.int32)[None, :]
    ).astype(jnp.bfloat16)


def stacked(wide, width):
    return jnp.concatenate(jnp.split(wide, wide.shape[1] // width, axis=1), axis=0)


def side_by_side(tall):
    return jnp.concatenate(jnp.split(tall, tall.shape[0] // tall.shape[1], axis=0), axis=1)


class FourInLine:
    def __init__(self, gate, up, down, static_part, mask):
        replica = lax.axis_index("rep")
        self.inner = (replica == 1) | (replica == 2)
        self.near, self.far = mask == 1, mask == 3
        self.gate, self.up, self.down = gate, up, down
        self.static_part = static_part

    def forward(self, bits):
        self.up_side = lax.ppermute(self.up, "rep", INWARD)
        self.gate_hub = lax.ppermute(self.gate, "rep", ACROSS)
        inner, self.near, self.far, *bits = lax.optimization_barrier(
            (self.inner, self.near, self.far, *bits)
        )
        send = lax.optimization_barrier(jnp.where(inner, self.static_part, self.gate))
        self.one = from_partner(send, 0)
        side, self.gate_hub, self.near, self.far = lax.optimization_barrier(
            (self.up_side, self.gate_hub, self.near, self.far)
        )
        first = jnp.where(self.far, side, self.up)
        second = jnp.where(self.far, self.up, side)
        first_in = lax.ppermute(first, "rep", ACROSS)
        self.quiet, self.first_in = first, first_in
        self.gate_edge = lax.ppermute(self.one, "rep", ACROSS)
        self.second = second
        return bits

    def handed_up(self, earlier):
        first_in = after(self.first_in, *earlier)
        send = jnp.where(self.inner, jnp.where(self.near, self.up, first_in), self.down)
        self.two = from_partner(send, 0)
        self.up_hub = lax.ppermute(after(self.second, send), "rep", ACROSS)
        self.later = send

    def handed_gate(self, earlier):
        gate_edge = after(self.gate_edge, self.later, *earlier)
        gate_out = jnp.where(
            self.near, self.gate, jnp.where(self.far, gate_edge, self.gate_hub)
        )
        send = jnp.where(self.inner, gate_out, self.static_part)
        self.three = from_partner(send, 0)
        two, self.up_hub = lax.optimization_barrier((self.two, self.up_hub, send))[:2]
        first = jnp.where(self.far, two, self.down)
        second = jnp.where(self.far, self.down, two)
        self.down_first = lax.ppermute(first, "rep", ACROSS)
        gate_in = jnp.where(
            self.near, self.one, jnp.where(self.far, self.gate_hub, self.gate_edge)
        )
        self.three = after(self.three, first)
        gate_here = lax.optimization_barrier(jnp.where(self.inner, gate_in, self.three))
        self.down_hub = lax.ppermute(second, "rep", ACROSS)
        up_in = jnp.where(self.near, self.up_side, self.up_hub)
        up_here = jnp.where(self.inner, up_in, self.two)
        static_in = jnp.where(self.inner, self.three, self.one)
        return gate_here, up_here, static_in

    def handed_down(self, earlier):
        send = jnp.where(self.near, self.down, after(self.down_first, *earlier))
        self.four = lax.ppermute(send, "rep", OUTWARD)
        return send

    def down_here(self, earlier):
        down_hub = after(self.down_hub, *earlier)
        down_in = jnp.where(self.near, self.two, down_hub)
        return jnp.where(self.inner, down_in, self.four)


def on_device(
    tokens,
    assign,
    route_mask,
    match_mask,
    gate_weight,
    up_weight,
    down_weight,
    slow_down,
    momentum,
    slot_cot,
):
    sections = lax.axis_size("section")
    levels = lax.axis_size("rep").bit_length() - 1
    section_here = lax.axis_index("section")
    token_rows = tokens[0, 0]
    expert_ids = assign[0, 0, :, 0]
    capacity = slot_cot.shape[3]
    model_width = token_rows.shape[1]
    masks_here = lax.dynamic_index_in_dim(
        jnp.stack([route_mask, match_mask]), section_here, axis=1, keepdims=False
    )
    own_mask, match = masks_here[0], masks_here[1]
    match_mine = jnp.bitwise_xor(own_mask, match)
    upward = list(range(levels))
    bits = [bit_of(mask, index) for mask in (own_mask, match_mine, match) for index in upward]
    contract = (((1,), (1,)), ((), ()))
    hidden_width = gate_weight.shape[3]

    gate_raw, up_raw, down_raw = gate_weight[0, 0], up_weight[0, 0], down_weight[0, 0]
    slow_float = slow_down[0, 0].astype(jnp.float32)
    down_float = down_raw.astype(jnp.float32)
    static_part = ((0.5 - pull_rate) * slow_float - 0.5 * down_float).astype(jnp.bfloat16)

    selector = slot_table(expert_ids, sections, capacity)
    placed = lax.dot_general(
        selector, token_rows, (((0,), (0,)), ((), ())), preferred_element_type=jnp.float32
    )
    dispatched = placed.astype(jnp.bfloat16).reshape(sections, capacity, model_width)

    line = None
    if levels == 2:
        line = FourInLine(
            gate_raw,
            up_raw,
            stacked(down_raw, hidden_width),
            stacked(lax.optimization_barrier(static_part), hidden_width),
            own_mask,
        )
        bits = line.forward(bits)
        dispatched = after(dispatched, line.quiet)
        line.handed_up((dispatched,))
    arrived = lax.all_to_all(dispatched, "section", split_axis=0, concat_axis=0, tiled=True)
    rows = arrived.reshape(-1, model_width)
    cotangent = slot_cot[0, 0].reshape(-1, model_width)
    if line is not None:
        gate_mat, up_mat, static_in = line.handed_gate((rows,))
        static_in = side_by_side(static_in)
    else:
        gate_mat, up_mat, down_mat = [
            route(weight, own_mask, upward) for weight in (gate_raw, up_raw, down_raw)
        ]
        static_in = from_partner(static_part, 0)

    gate_act = jnp.dot(rows, gate_mat, preferred_element_type=jnp.float32)
    up_act = jnp.dot(rows, up_mat, preferred_element_type=jnp.float32)
    sigmoid_gate = jax.nn.sigmoid(gate_act)
    hidden = (gate_act * sigmoid_gate * up_act).astype(jnp.bfloat16)
    down_grad = lax.dot_general(
        hidden, cotangent, (((0,), (0,)), ((), ())), preferred_element_type=jnp.float32
    ).astype(jnp.bfloat16)

    own_bits, mine_bits, match_bits = [
        bits[number * levels : (number + 1) * levels] for number in range(3)
    ]
    lower, top = upward[:-1], levels - 1
    down_grad_in = from_partner(down_grad, 0)
    if line is not None:
        sent = line.handed_down((down_grad,))
        static_in = after(static_in, sent)
        down_grad_in = after(down_grad_in, static_in, line.down_hub)
    own_routed, match_routed, static_routed = down_grad, down_grad, static_part
    for index in lower:
        if index == 0:
            own_in, match_in, static_here = down_grad_in, down_grad_in, static_in
        else:
            own_in = from_partner(own_routed, index)
            match_in = from_partner(match_routed, index)
            static_here = from_partner(static_routed, index)
        own_routed = jnp.where(own_bits[index], own_in, own_routed)
        match_routed = jnp.where(mine_bits[index], match_in, match_routed)
        static_routed = jnp.where(match_bits[index], static_here, static_routed)

    def combined(side, static_routed, own_routed, match_routed):
        def pick(bit, value):
            return jnp.where(bit == side, value.astype(jnp.float32), 0.0)

        return pick(match_bits[top], static_routed) + 0.5 * inner_rate * (
            pick(own_bits[top], own_routed) + pick(mine_bits[top], match_routed)
        )

    crossing_out = combined(True, static_routed, own_routed, match_routed).astype(jnp.bfloat16)
    crossing = from_partner(crossing_out, top)
    slow_float = after(slow_down[0, 0], crossing_out).astype(jnp.float32)
    staying = combined(False, static_routed, own_routed, match_routed)
    outer_here = (0.5 + pull_rate) * slow_float - 0.5 * down_float + staying
    pull = outer_rate * (1.0 + moment_rate)
    kept = (
        slow_float
        - pull * outer_here
        - (outer_rate * moment_rate * moment_rate) * momentum[0, 0].astype(jnp.float32)
    )
    kept = after(kept, crossing_out)
    new_slow = (kept - pull * crossing.astype(jnp.float32)).astype(jnp.bfloat16)

    if line is not None:
        down_mat = side_by_side(line.down_here((crossing_out,)))
    hidden_grad = lax.dot_general(
        cotangent, down_mat, contract, preferred_element_type=jnp.float32
    )
    gate_grad = (
        hidden_grad * up_act * sigmoid_gate * (1.0 + gate_act * (1.0 - sigmoid_gate))
    ).astype(jnp.bfloat16)
    up_grad = (hidden_grad * gate_act * sigmoid_gate).astype(jnp.bfloat16)
    slot_grad = (
        lax.dot_general(gate_grad, gate_mat, contract, preferred_element_type=jnp.float32)
        + lax.dot_general(up_grad, up_mat, contract, preferred_element_type=jnp.float32)
    ).astype(jnp.bfloat16)
    slot_grad = slot_grad.reshape(sections, capacity, model_width)
    returned = lax.all_to_all(slot_grad, "section", split_axis=0, concat_axis=0, tiled=True)
    input_grad = jnp.dot(
        selector, returned.reshape(-1, model_width), preferred_element_type=jnp.float32
    ).astype(jnp.bfloat16)
    return (input_grad[None, None], new_slow[None, None])


def solution(mesh):
    in_specs = (
        P("section", "rep", None, None),
        P("section", "rep", None, None),
        P(),
        P(),
        P("section", "rep", None, None),
        P("section", "rep", None, None),
        P("section", "rep", None, None),
        P("section", "rep", None, None),
        P("section", "rep", None, None),
        P("section", "rep", None, None, None),
    )
    out_specs = (P("section", "rep", None, None), P("section", "rep", None, None))
    return jax.shard_map(
        on_device, mesh=mesh, in_specs=in_specs, out_specs=out_specs, check_vma=False
    )
```

```python
import jax
import jax.numpy as jnp
from jax import lax
from jax.sharding import PartitionSpec as P

inner_rate = 0.05
pull_rate = 0.25
moment_rate = 0.9
outer_rate = 0.7

OUTWARD = [(1, 0), (2, 3)]
INWARD = [(0, 1), (3, 2)]
ACROSS = [(1, 2), (2, 1)]


def from_partner(value, distance):
    pairs = [(source, source ^ 2**distance) for source in range(lax.axis_size("rep"))]
    return lax.ppermute(value, "rep", pairs)


def bit_of(mask, index):
    return jnp.bitwise_and(jnp.right_shift(mask, index), 1) == 1


def route(value, mask, bits):
    for index in bits:
        value = jnp.where(bit_of(mask, index), from_partner(value, index), value)
    return value


def after(value, *earlier):
    return lax.optimization_barrier((value, *earlier))[0]


def slot_table(expert_ids, sections, capacity):
    expert_hot = (expert_ids[:, None] == jnp.arange(sections, dtype=jnp.int32)[None, :]).astype(
        jnp.int32
    )
    position = jnp.sum((jnp.cumsum(expert_hot, axis=0) - 1) * expert_hot, axis=1)
    slot_index = expert_ids * capacity + position
    return (
        slot_index[:, None] == jnp.arange(sections * capacity, dtype=jnp.int32)[None, :]
    ).astype(jnp.bfloat16)


def stacked(wide, width):
    return jnp.concatenate(jnp.split(wide, wide.shape[1] // width, axis=1), axis=0)


def side_by_side(tall):
    return jnp.concatenate(jnp.split(tall, tall.shape[0] // tall.shape[1], axis=0), axis=1)


class FourInLine:
    def __init__(self, gate, up, down, static_part, mask):
        replica = lax.axis_index("rep")
        self.inner = (replica == 1) | (replica == 2)
        self.near, self.far = mask == 1, mask == 3
        self.gate, self.up, self.down = gate, up, down
        self.static_part = static_part

    def forward(self, bits):
        self.up_side = lax.ppermute(self.up, "rep", INWARD)
        self.gate_hub = lax.ppermute(self.gate, "rep", ACROSS)
        inner, self.near, self.far, *bits = lax.optimization_barrier(
            (self.inner, self.near, self.far, *bits)
        )
        send = lax.optimization_barrier(jnp.where(inner, self.static_part, self.gate))
        self.one = from_partner(send, 0)
        side, self.gate_hub, self.near, self.far = lax.optimization_barrier(
            (self.up_side, self.gate_hub, self.near, self.far)
        )
        first = jnp.where(self.far, side, self.up)
        second = jnp.where(self.far, self.up, side)
        first_in = lax.ppermute(first, "rep", ACROSS)
        self.quiet, self.first_in = first, first_in
        self.gate_edge = lax.ppermute(self.one, "rep", ACROSS)
        self.second = second
        return bits

    def handed_up(self, earlier):
        first_in = after(self.first_in, *earlier)
        send = jnp.where(self.inner, jnp.where(self.near, self.up, first_in), self.down)
        self.two = from_partner(send, 0)
        self.up_hub = lax.ppermute(after(self.second, send), "rep", ACROSS)
        self.later = send

    def handed_gate(self, earlier):
        gate_edge = after(self.gate_edge, self.later, *earlier)
        gate_out = jnp.where(
            self.near, self.gate, jnp.where(self.far, gate_edge, self.gate_hub)
        )
        send = jnp.where(self.inner, gate_out, self.static_part)
        self.three = from_partner(send, 0)
        two, self.up_hub = lax.optimization_barrier((self.two, self.up_hub, send))[:2]
        first = jnp.where(self.far, two, self.down)
        second = jnp.where(self.far, self.down, two)
        self.down_first = lax.ppermute(first, "rep", ACROSS)
        gate_in = jnp.where(
            self.near, self.one, jnp.where(self.far, self.gate_hub, self.gate_edge)
        )
        self.three = after(self.three, first)
        gate_here = lax.optimization_barrier(jnp.where(self.inner, gate_in, self.three))
        self.second_down = second
        up_in = jnp.where(self.near, self.up_side, self.up_hub)
        up_here = jnp.where(self.inner, up_in, self.two)
        static_in = jnp.where(self.inner, self.three, self.one)
        return gate_here, up_here, static_in

    def swap_down(self, earlier):
        second = after(self.second_down, *earlier)
        self.down_hub = lax.ppermute(second, "rep", ACROSS)

    def handed_down(self, earlier):
        send = jnp.where(self.near, self.down, after(self.down_first, *earlier))
        self.four = lax.ppermute(send, "rep", OUTWARD)
        return send

    def down_here(self, earlier):
        down_hub = after(self.down_hub, *earlier)
        down_in = jnp.where(self.near, self.two, down_hub)
        return jnp.where(self.inner, down_in, self.four)


def on_device(
    tokens,
    assign,
    route_mask,
    match_mask,
    gate_weight,
    up_weight,
    down_weight,
    slow_down,
    momentum,
    slot_cot,
):
    sections = lax.axis_size("section")
    levels = lax.axis_size("rep").bit_length() - 1
    section_here = lax.axis_index("section")
    token_rows = tokens[0, 0]
    expert_ids = assign[0, 0, :, 0]
    capacity = slot_cot.shape[3]
    model_width = token_rows.shape[1]
    masks_here = lax.dynamic_index_in_dim(
        jnp.stack([route_mask, match_mask]), section_here, axis=1, keepdims=False
    )
    own_mask, match = masks_here[0], masks_here[1]
    match_mine = jnp.bitwise_xor(own_mask, match)
    upward = list(range(levels))
    bits = [bit_of(mask, index) for mask in (own_mask, match_mine, match) for index in upward]
    contract = (((1,), (1,)), ((), ()))
    hidden_width = gate_weight.shape[3]

    gate_raw, up_raw, down_raw = gate_weight[0, 0], up_weight[0, 0], down_weight[0, 0]
    slow_float = slow_down[0, 0].astype(jnp.float32)
    down_float = down_raw.astype(jnp.float32)
    static_part = ((0.5 - pull_rate) * slow_float - 0.5 * down_float).astype(jnp.bfloat16)

    selector = slot_table(expert_ids, sections, capacity)
    placed = lax.dot_general(
        selector, token_rows, (((0,), (0,)), ((), ())), preferred_element_type=jnp.float32
    )
    dispatched = placed.astype(jnp.bfloat16).reshape(sections, capacity, model_width)

    line = None
    if levels == 2:
        line = FourInLine(
            gate_raw,
            up_raw,
            stacked(down_raw, hidden_width),
            stacked(lax.optimization_barrier(static_part), hidden_width),
            own_mask,
        )
        bits = line.forward(bits)
        dispatched = after(dispatched, line.quiet)
        line.handed_up((dispatched,))
    arrived = lax.all_to_all(dispatched, "section", split_axis=0, concat_axis=0, tiled=True)
    rows = arrived.reshape(-1, model_width)
    cotangent = slot_cot[0, 0].reshape(-1, model_width)
    if line is not None:
        gate_mat, up_mat, static_in = line.handed_gate((rows,))
        static_in = side_by_side(static_in)
    else:
        gate_mat, up_mat, down_mat = [
            route(weight, own_mask, upward) for weight in (gate_raw, up_raw, down_raw)
        ]
        static_in = from_partner(static_part, 0)

    gate_act = jnp.dot(rows, gate_mat, preferred_element_type=jnp.float32)
    up_act = jnp.dot(rows, up_mat, preferred_element_type=jnp.float32)
    if line is not None:
        line.swap_down((up_act,))
    sigmoid_gate = jax.nn.sigmoid(gate_act)
    hidden = (gate_act * sigmoid_gate * up_act).astype(jnp.bfloat16)
    down_grad = lax.dot_general(
        hidden, cotangent, (((0,), (0,)), ((), ())), preferred_element_type=jnp.float32
    ).astype(jnp.bfloat16)

    own_bits, mine_bits, match_bits = [
        bits[number * levels : (number + 1) * levels] for number in range(3)
    ]
    lower, top = upward[:-1], levels - 1
    down_grad_in = from_partner(down_grad, 0)
    if line is not None:
        sent = line.handed_down((down_grad,))
        static_in = after(static_in, sent)
        down_grad_in = after(down_grad_in, static_in, line.down_hub)
    own_routed, match_routed, static_routed = down_grad, down_grad, static_part
    for index in lower:
        if index == 0:
            own_in, match_in, static_here = down_grad_in, down_grad_in, static_in
        else:
            own_in = from_partner(own_routed, index)
            match_in = from_partner(match_routed, index)
            static_here = from_partner(static_routed, index)
        own_routed = jnp.where(own_bits[index], own_in, own_routed)
        match_routed = jnp.where(mine_bits[index], match_in, match_routed)
        static_routed = jnp.where(match_bits[index], static_here, static_routed)

    def combined(side, static_routed, own_routed, match_routed):
        def pick(bit, value):
            return jnp.where(bit == side, value.astype(jnp.float32), 0.0)

        return pick(match_bits[top], static_routed) + 0.5 * inner_rate * (
            pick(own_bits[top], own_routed) + pick(mine_bits[top], match_routed)
        )

    crossing_out = combined(True, static_routed, own_routed, match_routed).astype(jnp.bfloat16)
    crossing = from_partner(crossing_out, top)
    slow_float = after(slow_down[0, 0], crossing_out).astype(jnp.float32)
    staying = combined(False, static_routed, own_routed, match_routed)
    outer_here = (0.5 + pull_rate) * slow_float - 0.5 * down_float + staying
    pull = outer_rate * (1.0 + moment_rate)
    kept = (
        slow_float
        - pull * outer_here
        - (outer_rate * moment_rate * moment_rate) * momentum[0, 0].astype(jnp.float32)
    )
    kept = after(kept, crossing_out)
    new_slow = (kept - pull * crossing.astype(jnp.float32)).astype(jnp.bfloat16)

    if line is not None:
        down_mat = side_by_side(line.down_here((crossing_out,)))
    hidden_grad = lax.dot_general(
        cotangent, down_mat, contract, preferred_element_type=jnp.float32
    )
    gate_grad = (
        hidden_grad * up_act * sigmoid_gate * (1.0 + gate_act * (1.0 - sigmoid_gate))
    ).astype(jnp.bfloat16)
    up_grad = (hidden_grad * gate_act * sigmoid_gate).astype(jnp.bfloat16)
    slot_grad = (
        lax.dot_general(gate_grad, gate_mat, contract, preferred_element_type=jnp.float32)
        + lax.dot_general(up_grad, up_mat, contract, preferred_element_type=jnp.float32)
    ).astype(jnp.bfloat16)
    slot_grad = slot_grad.reshape(sections, capacity, model_width)
    returned = lax.all_to_all(slot_grad, "section", split_axis=0, concat_axis=0, tiled=True)
    input_grad = jnp.dot(
        selector, returned.reshape(-1, model_width), preferred_element_type=jnp.float32
    ).astype(jnp.bfloat16)
    return (input_grad[None, None], new_slow[None, None])


def solution(mesh):
    in_specs = (
        P("section", "rep", None, None),
        P("section", "rep", None, None),
        P(),
        P(),
        P("section", "rep", None, None),
        P("section", "rep", None, None),
        P("section", "rep", None, None),
        P("section", "rep", None, None),
        P("section", "rep", None, None),
        P("section", "rep", None, None, None),
    )
    out_specs = (P("section", "rep", None, None), P("section", "rep", None, None))
    return jax.shard_map(
        on_device, mesh=mesh, in_specs=in_specs, out_specs=out_specs, check_vma=False
    )
```

```python
import jax
import jax.numpy as jnp
from jax import lax
from jax.sharding import PartitionSpec as P

inner_rate = 0.05
pull_rate = 0.25
moment_rate = 0.9
outer_rate = 0.7

OUTWARD = [(1, 0), (2, 3)]
INWARD = [(0, 1), (3, 2)]
ACROSS = [(1, 2), (2, 1)]


def from_partner(value, distance):
    pairs = [(source, source ^ 2**distance) for source in range(lax.axis_size("rep"))]
    return lax.ppermute(value, "rep", pairs)


def bit_of(mask, index):
    return jnp.bitwise_and(jnp.right_shift(mask, index), 1) == 1


def route(value, mask, bits):
    for index in bits:
        value = jnp.where(bit_of(mask, index), from_partner(value, index), value)
    return value


def after(value, *earlier):
    return lax.optimization_barrier((value, *earlier))[0]


def slot_table(expert_ids, sections, capacity):
    expert_hot = (expert_ids[:, None] == jnp.arange(sections, dtype=jnp.int32)[None, :]).astype(
        jnp.int32
    )
    position = jnp.sum((jnp.cumsum(expert_hot, axis=0) - 1) * expert_hot, axis=1)
    slot_index = expert_ids * capacity + position
    return (
        slot_index[:, None] == jnp.arange(sections * capacity, dtype=jnp.int32)[None, :]
    ).astype(jnp.bfloat16)


def stacked(wide, width):
    return jnp.concatenate(jnp.split(wide, wide.shape[1] // width, axis=1), axis=0)


def side_by_side(tall):
    return jnp.concatenate(jnp.split(tall, tall.shape[0] // tall.shape[1], axis=0), axis=1)


class FourInLine:
    def __init__(self, gate, up, down, static_part, mask):
        replica = lax.axis_index("rep")
        self.inner = (replica == 1) | (replica == 2)
        self.near, self.far = mask == 1, mask == 3
        self.gate, self.up, self.down = gate, up, down
        self.static_part = static_part

    def forward(self, bits):
        self.up_side = lax.ppermute(self.up, "rep", INWARD)
        self.gate_hub = lax.ppermute(self.gate, "rep", ACROSS)
        inner, self.near, self.far, *bits = lax.optimization_barrier(
            (self.inner, self.near, self.far, *bits)
        )
        send = lax.optimization_barrier(jnp.where(inner, self.static_part, self.gate))
        self.one = from_partner(send, 0)
        side, self.gate_hub, self.near, self.far = lax.optimization_barrier(
            (self.up_side, self.gate_hub, self.near, self.far)
        )
        first = jnp.where(self.far, side, self.up)
        second = jnp.where(self.far, self.up, side)
        first_in = lax.ppermute(first, "rep", ACROSS)
        self.quiet, self.first_in = first, first_in
        self.gate_edge = lax.ppermute(self.one, "rep", ACROSS)
        self.second = second
        return bits

    def handed_up(self, earlier):
        first_in = after(self.first_in, *earlier)
        send = jnp.where(self.inner, jnp.where(self.near, self.up, first_in), self.down)
        self.two = from_partner(send, 0)
        self.up_hub = lax.ppermute(after(self.second, send), "rep", ACROSS)
        self.later = send

    def handed_gate(self, earlier):
        gate_edge = after(self.gate_edge, self.later, *earlier)
        gate_out = jnp.where(
            self.near, self.gate, jnp.where(self.far, gate_edge, self.gate_hub)
        )
        send = jnp.where(self.inner, gate_out, self.static_part)
        self.three = from_partner(send, 0)
        two, self.up_hub = lax.optimization_barrier((self.two, self.up_hub, send))[:2]
        first = jnp.where(self.far, two, self.down)
        second = jnp.where(self.far, self.down, two)
        self.down_first = lax.ppermute(first, "rep", ACROSS)
        gate_in = jnp.where(
            self.near, self.one, jnp.where(self.far, self.gate_hub, self.gate_edge)
        )
        self.three = after(self.three, first)
        gate_here = lax.optimization_barrier(jnp.where(self.inner, gate_in, self.three))
        self.second_down = second
        up_in = jnp.where(self.near, self.up_side, self.up_hub)
        up_here = jnp.where(self.inner, up_in, self.two)
        static_in = jnp.where(self.inner, self.three, self.one)
        return gate_here, up_here, static_in

    def swap_down(self, earlier):
        second = after(self.second_down, *earlier)
        self.down_hub = lax.ppermute(second, "rep", ACROSS)

    def handed_down(self, earlier):
        send = jnp.where(self.near, self.down, after(self.down_first, *earlier))
        self.four = lax.ppermute(send, "rep", OUTWARD)
        return send

    def down_here(self, earlier):
        down_hub = after(self.down_hub, *earlier)
        down_in = jnp.where(self.near, self.two, down_hub)
        return jnp.where(self.inner, down_in, self.four)


def on_device(
    tokens,
    assign,
    route_mask,
    match_mask,
    gate_weight,
    up_weight,
    down_weight,
    slow_down,
    momentum,
    slot_cot,
):
    sections = lax.axis_size("section")
    levels = lax.axis_size("rep").bit_length() - 1
    section_here = lax.axis_index("section")
    token_rows = tokens[0, 0]
    expert_ids = assign[0, 0, :, 0]
    capacity = slot_cot.shape[3]
    model_width = token_rows.shape[1]
    masks_here = lax.dynamic_index_in_dim(
        jnp.stack([route_mask, match_mask]), section_here, axis=1, keepdims=False
    )
    own_mask, match = masks_here[0], masks_here[1]
    match_mine = jnp.bitwise_xor(own_mask, match)
    upward = list(range(levels))
    bits = [bit_of(mask, index) for mask in (own_mask, match_mine, match) for index in upward]
    contract = (((1,), (1,)), ((), ()))
    hidden_width = gate_weight.shape[3]

    gate_raw, up_raw, down_raw = gate_weight[0, 0], up_weight[0, 0], down_weight[0, 0]
    slow_float = slow_down[0, 0].astype(jnp.float32)
    down_float = down_raw.astype(jnp.float32)
    static_part = ((0.5 - pull_rate) * slow_float - 0.5 * down_float).astype(jnp.bfloat16)

    selector = slot_table(expert_ids, sections, capacity)
    placed = lax.dot_general(
        selector, token_rows, (((0,), (0,)), ((), ())), preferred_element_type=jnp.float32
    )
    dispatched = placed.astype(jnp.bfloat16).reshape(sections, capacity, model_width)

    line = None
    if levels == 2:
        line = FourInLine(
            gate_raw,
            up_raw,
            stacked(down_raw, hidden_width),
            stacked(lax.optimization_barrier(static_part), hidden_width),
            own_mask,
        )
        bits = line.forward(bits)
        dispatched = after(dispatched, line.quiet)
        line.handed_up((dispatched,))
    arrived = lax.all_to_all(dispatched, "section", split_axis=0, concat_axis=0, tiled=True)
    rows = arrived.reshape(-1, model_width)
    cotangent = slot_cot[0, 0].reshape(-1, model_width)
    if line is not None:
        gate_mat, up_mat, static_in = line.handed_gate((rows,))
        static_in = side_by_side(static_in)
    else:
        gate_mat, up_mat, down_mat = [
            route(weight, own_mask, upward) for weight in (gate_raw, up_raw, down_raw)
        ]
        static_in = from_partner(static_part, 0)

    gate_act = jnp.dot(rows, gate_mat, preferred_element_type=jnp.float32)
    up_act = jnp.dot(rows, up_mat, preferred_element_type=jnp.float32)
    if line is not None:
        line.swap_down((up_act, gate_act))
    sigmoid_gate = jax.nn.sigmoid(gate_act)
    hidden = (gate_act * sigmoid_gate * up_act).astype(jnp.bfloat16)
    down_grad = lax.dot_general(
        hidden, cotangent, (((0,), (0,)), ((), ())), preferred_element_type=jnp.float32
    ).astype(jnp.bfloat16)

    own_bits, mine_bits, match_bits = [
        bits[number * levels : (number + 1) * levels] for number in range(3)
    ]
    lower, top = upward[:-1], levels - 1
    down_grad_in = from_partner(down_grad, 0)
    if line is not None:
        sent = line.handed_down((down_grad,))
        static_in = after(static_in, sent)
        down_grad_in = after(down_grad_in, static_in, line.down_hub)
    own_routed, match_routed, static_routed = down_grad, down_grad, static_part
    for index in lower:
        if index == 0:
            own_in, match_in, static_here = down_grad_in, down_grad_in, static_in
        else:
            own_in = from_partner(own_routed, index)
            match_in = from_partner(match_routed, index)
            static_here = from_partner(static_routed, index)
        own_routed = jnp.where(own_bits[index], own_in, own_routed)
        match_routed = jnp.where(mine_bits[index], match_in, match_routed)
        static_routed = jnp.where(match_bits[index], static_here, static_routed)

    def combined(side, static_routed, own_routed, match_routed):
        def pick(bit, value):
            return jnp.where(bit == side, value.astype(jnp.float32), 0.0)

        return pick(match_bits[top], static_routed) + 0.5 * inner_rate * (
            pick(own_bits[top], own_routed) + pick(mine_bits[top], match_routed)
        )

    crossing_out = combined(True, static_routed, own_routed, match_routed).astype(jnp.bfloat16)
    crossing = from_partner(crossing_out, top)
    slow_float = after(slow_down[0, 0], crossing_out).astype(jnp.float32)
    staying = combined(False, static_routed, own_routed, match_routed)
    outer_here = (0.5 + pull_rate) * slow_float - 0.5 * down_float + staying
    pull = outer_rate * (1.0 + moment_rate)
    kept = (
        slow_float
        - pull * outer_here
        - (outer_rate * moment_rate * moment_rate) * momentum[0, 0].astype(jnp.float32)
    )
    kept = after(kept, crossing_out)
    new_slow = (kept - pull * crossing.astype(jnp.float32)).astype(jnp.bfloat16)

    if line is not None:
        down_mat = side_by_side(line.down_here((crossing_out,)))
    hidden_grad = lax.dot_general(
        cotangent, down_mat, contract, preferred_element_type=jnp.float32
    )
    gate_grad = (
        hidden_grad * up_act * sigmoid_gate * (1.0 + gate_act * (1.0 - sigmoid_gate))
    ).astype(jnp.bfloat16)
    up_grad = (hidden_grad * gate_act * sigmoid_gate).astype(jnp.bfloat16)
    slot_grad = (
        lax.dot_general(gate_grad, gate_mat, contract, preferred_element_type=jnp.float32)
        + lax.dot_general(up_grad, up_mat, contract, preferred_element_type=jnp.float32)
    ).astype(jnp.bfloat16)
    slot_grad = slot_grad.reshape(sections, capacity, model_width)
    returned = lax.all_to_all(slot_grad, "section", split_axis=0, concat_axis=0, tiled=True)
    input_grad = jnp.dot(
        selector, returned.reshape(-1, model_width), preferred_element_type=jnp.float32
    ).astype(jnp.bfloat16)
    return (input_grad[None, None], new_slow[None, None])


def solution(mesh):
    in_specs = (
        P("section", "rep", None, None),
        P("section", "rep", None, None),
        P(),
        P(),
        P("section", "rep", None, None),
        P("section", "rep", None, None),
        P("section", "rep", None, None),
        P("section", "rep", None, None),
        P("section", "rep", None, None),
        P("section", "rep", None, None, None),
    )
    out_specs = (P("section", "rep", None, None), P("section", "rep", None, None))
    return jax.shard_map(
        on_device, mesh=mesh, in_specs=in_specs, out_specs=out_specs, check_vma=False
    )
```

```python
import jax
import jax.numpy as jnp
from jax import lax
from jax.sharding import PartitionSpec as P

inner_rate = 0.05
pull_rate = 0.25
moment_rate = 0.9
outer_rate = 0.7

OUTWARD = [(1, 0), (2, 3)]
INWARD = [(0, 1), (3, 2)]
ACROSS = [(1, 2), (2, 1)]


def from_partner(value, distance):
    pairs = [(source, source ^ 2**distance) for source in range(lax.axis_size("rep"))]
    return lax.ppermute(value, "rep", pairs)


def bit_of(mask, index):
    return jnp.bitwise_and(jnp.right_shift(mask, index), 1) == 1


def route(value, mask, bits):
    for index in bits:
        value = jnp.where(bit_of(mask, index), from_partner(value, index), value)
    return value


def after(value, *earlier):
    return lax.optimization_barrier((value, *earlier))[0]


def slot_table(expert_ids, sections, capacity):
    expert_hot = (expert_ids[:, None] == jnp.arange(sections, dtype=jnp.int32)[None, :]).astype(
        jnp.int32
    )
    position = jnp.sum((jnp.cumsum(expert_hot, axis=0) - 1) * expert_hot, axis=1)
    slot_index = expert_ids * capacity + position
    return (
        slot_index[:, None] == jnp.arange(sections * capacity, dtype=jnp.int32)[None, :]
    ).astype(jnp.bfloat16)


def stacked(wide, width):
    return jnp.concatenate(jnp.split(wide, wide.shape[1] // width, axis=1), axis=0)


def side_by_side(tall):
    return jnp.concatenate(jnp.split(tall, tall.shape[0] // tall.shape[1], axis=0), axis=1)


class FourInLine:
    def __init__(self, gate, up, down, static_part, mask):
        replica = lax.axis_index("rep")
        self.inner = (replica == 1) | (replica == 2)
        self.near, self.far = mask == 1, mask == 3
        self.gate, self.up, self.down = gate, up, down
        self.static_part = static_part

    def forward(self, bits):
        self.up_side = lax.ppermute(self.up, "rep", INWARD)
        self.gate_hub = lax.ppermute(self.gate, "rep", ACROSS)
        inner, self.near, self.far, *bits = lax.optimization_barrier(
            (self.inner, self.near, self.far, *bits)
        )
        send = lax.optimization_barrier(jnp.where(inner, self.static_part, self.gate))
        self.one = from_partner(send, 0)
        self.up_hub = lax.ppermute(self.up, "rep", ACROSS)
        self.up_edge = lax.ppermute(self.up_side, "rep", ACROSS)
        self.one, self.up_hub, self.gate_hub = lax.optimization_barrier(
            (self.one, self.up_hub, self.gate_hub, self.up_side)
        )[:3]
        self.gate_edge = lax.ppermute(self.one, "rep", ACROSS)
        self.quiet = self.up_side
        return bits

    def handed_up(self, earlier):
        up_edge = after(self.up_edge, *earlier)
        up_out = jnp.where(self.near, self.up, jnp.where(self.far, up_edge, self.up_hub))
        send = lax.optimization_barrier(jnp.where(self.inner, up_out, self.down))
        self.two = from_partner(send, 0)
        self.later = send

    def handed_gate(self, earlier):
        gate_edge = after(self.gate_edge, self.later, *earlier)
        gate_out = jnp.where(
            self.near, self.gate, jnp.where(self.far, gate_edge, self.gate_hub)
        )
        send = jnp.where(self.inner, gate_out, self.static_part)
        self.three = from_partner(send, 0)
        two = after(self.two, send)
        first = jnp.where(self.far, two, self.down)
        self.second_down = jnp.where(self.far, self.down, two)
        self.down_first = lax.ppermute(first, "rep", ACROSS)
        gate_in = jnp.where(
            self.near, self.one, jnp.where(self.far, self.gate_hub, self.gate_edge)
        )
        self.three = after(self.three, first)
        gate_here = lax.optimization_barrier(jnp.where(self.inner, gate_in, self.three))
        up_in = jnp.where(
            self.near, self.up_side, jnp.where(self.far, self.up_hub, self.up_edge)
        )
        up_here = jnp.where(self.inner, up_in, two)
        static_in = jnp.where(self.inner, self.three, self.one)
        return gate_here, up_here, static_in

    def swap_down(self, earlier):
        second = after(self.second_down, *earlier)
        self.down_hub = lax.ppermute(second, "rep", ACROSS)

    def handed_down(self, earlier):
        send = jnp.where(self.near, self.down, after(self.down_first, *earlier))
        self.four = lax.ppermute(send, "rep", OUTWARD)
        return send

    def down_here(self, earlier):
        down_hub = after(self.down_hub, *earlier)
        down_in = jnp.where(self.near, self.two, down_hub)
        return jnp.where(self.inner, down_in, self.four)


def on_device(
    tokens,
    assign,
    route_mask,
    match_mask,
    gate_weight,
    up_weight,
    down_weight,
    slow_down,
    momentum,
    slot_cot,
):
    sections = lax.axis_size("section")
    levels = lax.axis_size("rep").bit_length() - 1
    section_here = lax.axis_index("section")
    token_rows = tokens[0, 0]
    expert_ids = assign[0, 0, :, 0]
    capacity = slot_cot.shape[3]
    model_width = token_rows.shape[1]
    masks_here = lax.dynamic_index_in_dim(
        jnp.stack([route_mask, match_mask]), section_here, axis=1, keepdims=False
    )
    own_mask, match = masks_here[0], masks_here[1]
    match_mine = jnp.bitwise_xor(own_mask, match)
    upward = list(range(levels))
    bits = [bit_of(mask, index) for mask in (own_mask, match_mine, match) for index in upward]
    contract = (((1,), (1,)), ((), ()))
    hidden_width = gate_weight.shape[3]

    gate_raw, up_raw, down_raw = gate_weight[0, 0], up_weight[0, 0], down_weight[0, 0]
    slow_float = slow_down[0, 0].astype(jnp.float32)
    down_float = down_raw.astype(jnp.float32)
    static_part = ((0.5 - pull_rate) * slow_float - 0.5 * down_float).astype(jnp.bfloat16)

    selector = slot_table(expert_ids, sections, capacity)
    placed = lax.dot_general(
        selector, token_rows, (((0,), (0,)), ((), ())), preferred_element_type=jnp.float32
    )
    dispatched = placed.astype(jnp.bfloat16).reshape(sections, capacity, model_width)

    line = None
    if levels == 2:
        line = FourInLine(
            gate_raw,
            up_raw,
            stacked(down_raw, hidden_width),
            stacked(lax.optimization_barrier(static_part), hidden_width),
            own_mask,
        )
        bits = line.forward(bits)
        dispatched = after(dispatched, line.quiet)
        line.handed_up((dispatched,))
    arrived = lax.all_to_all(dispatched, "section", split_axis=0, concat_axis=0, tiled=True)
    rows = arrived.reshape(-1, model_width)
    cotangent = slot_cot[0, 0].reshape(-1, model_width)
    if line is not None:
        gate_mat, up_mat, static_in = line.handed_gate((rows,))
        static_in = side_by_side(static_in)
    else:
        gate_mat, up_mat, down_mat = [
            route(weight, own_mask, upward) for weight in (gate_raw, up_raw, down_raw)
        ]
        static_in = from_partner(static_part, 0)

    gate_act = jnp.dot(rows, gate_mat, preferred_element_type=jnp.float32)
    up_act = jnp.dot(rows, up_mat, preferred_element_type=jnp.float32)
    if line is not None:
        line.swap_down((up_act, gate_act))
    sigmoid_gate = jax.nn.sigmoid(gate_act)
    hidden = (gate_act * sigmoid_gate * up_act).astype(jnp.bfloat16)
    half = hidden_width // 2
    parts = [slice(0, half), slice(half, hidden_width)]
    down_grads, down_grads_in = [], []
    for part in parts:
        down_grads.append(
            lax.dot_general(
                hidden[:, part],
                cotangent,
                (((0,), (0,)), ((), ())),
                preferred_element_type=jnp.float32,
            ).astype(jnp.bfloat16)
        )
        down_grads_in.append(from_partner(down_grads[-1], 0))

    lower, top = upward[:-1], levels - 1
    own_bits, mine_bits, match_bits = [
        bits[number * levels : (number + 1) * levels] for number in range(3)
    ]
    if line is not None:
        sent = line.handed_down((down_grads[1],))
        static_in = lax.optimization_barrier(after(static_in, sent))
        down_grads_in[0] = after(down_grads_in[0], static_in)
        down_grads_in[1] = after(down_grads_in[1], line.down_hub)

    def combined(side, own_routed, match_routed, static_routed):
        def pick(bit, value):
            return jnp.where(bit == side, value.astype(jnp.float32), 0.0)

        return pick(match_bits[top], static_routed) + 0.5 * inner_rate * (
            pick(own_bits[top], own_routed) + pick(mine_bits[top], match_routed)
        )

    crossing_out, crossings, stayings = static_part, [], []
    for number, part in enumerate(parts):
        own_routed = match_routed = down_grads[number]
        down_grad_in = after(down_grads_in[number], crossing_out)
        static_routed = static_part[part]
        for index in lower:
            if index == 0:
                own_in, match_in, static_here = down_grad_in, down_grad_in, static_in[part]
            else:
                own_in = from_partner(own_routed, index)
                match_in = from_partner(match_routed, index)
                static_here = from_partner(static_routed, index)
            own_routed = jnp.where(own_bits[index], own_in, own_routed)
            match_routed = jnp.where(mine_bits[index], match_in, match_routed)
            static_routed = jnp.where(match_bits[index], static_here, static_routed)
        routed = (own_routed, match_routed, static_routed)
        crossing_out = lax.optimization_barrier(combined(True, *routed).astype(jnp.bfloat16))
        crossings.append(from_partner(crossing_out, top))
        stayings.append(combined(False, *(after(value, crossing_out) for value in routed)))
    slow_float = after(slow_down[0, 0], crossing_out).astype(jnp.float32)
    outer_here = (
        (0.5 + pull_rate) * slow_float - 0.5 * down_float + jnp.concatenate(stayings, axis=0)
    )
    pull = outer_rate * (1.0 + moment_rate)
    kept = (
        slow_float
        - pull * outer_here
        - (outer_rate * moment_rate * moment_rate) * momentum[0, 0].astype(jnp.float32)
    )
    if line is not None:
        down_mat = side_by_side(line.down_here((crossing_out,)))
    hidden_grad = lax.dot_general(
        cotangent, down_mat, contract, preferred_element_type=jnp.float32
    )
    gate_grad = (
        hidden_grad * up_act * sigmoid_gate * (1.0 + gate_act * (1.0 - sigmoid_gate))
    ).astype(jnp.bfloat16)
    up_grad = (hidden_grad * gate_act * sigmoid_gate).astype(jnp.bfloat16)
    slot_grad = (
        lax.dot_general(gate_grad, gate_mat, contract, preferred_element_type=jnp.float32)
        + lax.dot_general(up_grad, up_mat, contract, preferred_element_type=jnp.float32)
    ).astype(jnp.bfloat16)
    kept, *crossings = lax.optimization_barrier((kept, *crossings, slot_grad))[:3]
    crossing = jnp.concatenate(crossings, axis=0)
    new_slow = (kept - pull * crossing.astype(jnp.float32)).astype(jnp.bfloat16)
    slot_grad = slot_grad.reshape(sections, capacity, model_width)
    returned = lax.all_to_all(slot_grad, "section", split_axis=0, concat_axis=0, tiled=True)
    input_grad = jnp.dot(
        selector, returned.reshape(-1, model_width), preferred_element_type=jnp.float32
    ).astype(jnp.bfloat16)
    return (input_grad[None, None], new_slow[None, None])


def solution(mesh):
    in_specs = (
        P("section", "rep", None, None),
        P("section", "rep", None, None),
        P(),
        P(),
        P("section", "rep", None, None),
        P("section", "rep", None, None),
        P("section", "rep", None, None),
        P("section", "rep", None, None),
        P("section", "rep", None, None),
        P("section", "rep", None, None, None),
    )
    out_specs = (P("section", "rep", None, None), P("section", "rep", None, None))
    return jax.shard_map(
        on_device, mesh=mesh, in_specs=in_specs, out_specs=out_specs, check_vma=False
    )
```

```python
import jax
import jax.numpy as jnp
from jax import lax
from jax.sharding import PartitionSpec as P

inner_rate = 0.05
pull_rate = 0.25
moment_rate = 0.9
outer_rate = 0.7

OUTWARD = [(1, 0), (2, 3)]
INWARD = [(0, 1), (3, 2)]
ACROSS = [(1, 2), (2, 1)]


def from_partner(value, distance):
    pairs = [(source, source ^ 2**distance) for source in range(lax.axis_size("rep"))]
    return lax.ppermute(value, "rep", pairs)


def bit_of(mask, index):
    return jnp.bitwise_and(jnp.right_shift(mask, index), 1) == 1


def route(value, mask, bits):
    for index in bits:
        value = jnp.where(bit_of(mask, index), from_partner(value, index), value)
    return value


def after(value, *earlier):
    return lax.optimization_barrier((value, *earlier))[0]


def slot_table(expert_ids, sections, capacity):
    expert_hot = (expert_ids[:, None] == jnp.arange(sections, dtype=jnp.int32)[None, :]).astype(
        jnp.int32
    )
    position = jnp.sum((jnp.cumsum(expert_hot, axis=0) - 1) * expert_hot, axis=1)
    slot_index = expert_ids * capacity + position
    return (
        slot_index[:, None] == jnp.arange(sections * capacity, dtype=jnp.int32)[None, :]
    ).astype(jnp.bfloat16)


def stacked(wide, width):
    return jnp.concatenate(jnp.split(wide, wide.shape[1] // width, axis=1), axis=0)


def side_by_side(tall):
    return jnp.concatenate(jnp.split(tall, tall.shape[0] // tall.shape[1], axis=0), axis=1)


class FourInLine:
    def __init__(self, gate, up, down, static_part, mask):
        replica = lax.axis_index("rep")
        self.inner = (replica == 1) | (replica == 2)
        self.near, self.far = mask == 1, mask == 3
        self.gate, self.up, self.down = gate, up, down
        self.static_part = static_part

    def forward(self, bits):
        self.up_side = lax.ppermute(self.up, "rep", INWARD)
        self.gate_hub = lax.ppermute(self.gate, "rep", ACROSS)
        inner, self.near, self.far, *bits = lax.optimization_barrier(
            (self.inner, self.near, self.far, *bits)
        )
        send = lax.optimization_barrier(jnp.where(inner, self.static_part, self.gate))
        self.one = from_partner(send, 0)
        side, self.gate_hub, self.near, self.far = lax.optimization_barrier(
            (self.up_side, self.gate_hub, self.near, self.far)
        )
        first = jnp.where(self.far, side, self.up)
        second = jnp.where(self.far, self.up, side)
        first_in = lax.ppermute(first, "rep", ACROSS)
        self.quiet, self.first_in = first, first_in
        self.gate_edge = lax.ppermute(self.one, "rep", ACROSS)
        self.second = second
        return bits

    def handed_up(self, earlier):
        first_in = after(self.first_in, *earlier)
        send = jnp.where(self.inner, jnp.where(self.near, self.up, first_in), self.down)
        self.two = from_partner(send, 0)
        self.up_hub = lax.ppermute(after(self.second, send), "rep", ACROSS)
        self.later = send

    def handed_gate(self, earlier):
        gate_edge = after(self.gate_edge, self.later, *earlier)
        gate_out = jnp.where(
            self.near, self.gate, jnp.where(self.far, gate_edge, self.gate_hub)
        )
        send = jnp.where(self.inner, gate_out, self.static_part)
        self.three = from_partner(send, 0)
        two, self.up_hub = lax.optimization_barrier((self.two, self.up_hub, send))[:2]
        first = jnp.where(self.far, two, self.down)
        second = jnp.where(self.far, self.down, two)
        self.down_first = lax.ppermute(first, "rep", ACROSS)
        gate_in = jnp.where(
            self.near, self.one, jnp.where(self.far, self.gate_hub, self.gate_edge)
        )
        self.three = after(self.three, first)
        gate_here = lax.optimization_barrier(jnp.where(self.inner, gate_in, self.three))
        self.second_down = second
        up_in = jnp.where(self.near, self.up_side, self.up_hub)
        up_here = jnp.where(self.inner, up_in, self.two)
        static_in = jnp.where(self.inner, self.three, self.one)
        return gate_here, up_here, static_in

    def swap_down(self, earlier):
        second = after(self.second_down, *earlier)
        self.down_hub = lax.ppermute(second, "rep", ACROSS)

    def handed_down(self, earlier):
        send = jnp.where(self.near, self.down, after(self.down_first, *earlier))
        self.four = lax.ppermute(send, "rep", OUTWARD)
        return send

    def down_here(self, earlier):
        down_hub = after(self.down_hub, *earlier)
        down_in = jnp.where(self.near, self.two, down_hub)
        return jnp.where(self.inner, down_in, self.four)


def on_device(
    tokens,
    assign,
    route_mask,
    match_mask,
    gate_weight,
    up_weight,
    down_weight,
    slow_down,
    momentum,
    slot_cot,
):
    sections = lax.axis_size("section")
    levels = lax.axis_size("rep").bit_length() - 1
    section_here = lax.axis_index("section")
    token_rows = tokens[0, 0]
    expert_ids = assign[0, 0, :, 0]
    capacity = slot_cot.shape[3]
    model_width = token_rows.shape[1]
    masks_here = lax.dynamic_index_in_dim(
        jnp.stack([route_mask, match_mask]), section_here, axis=1, keepdims=False
    )
    own_mask, match = masks_here[0], masks_here[1]
    match_mine = jnp.bitwise_xor(own_mask, match)
    upward = list(range(levels))
    bits = [bit_of(mask, index) for mask in (own_mask, match_mine, match) for index in upward]
    contract = (((1,), (1,)), ((), ()))
    hidden_width = gate_weight.shape[3]

    gate_raw, up_raw, down_raw = gate_weight[0, 0], up_weight[0, 0], down_weight[0, 0]
    slow_float = slow_down[0, 0].astype(jnp.float32)
    down_float = down_raw.astype(jnp.float32)
    static_part = ((0.5 - pull_rate) * slow_float - 0.5 * down_float).astype(jnp.bfloat16)

    selector = slot_table(expert_ids, sections, capacity)
    placed = lax.dot_general(
        selector, token_rows, (((0,), (0,)), ((), ())), preferred_element_type=jnp.float32
    )
    dispatched = placed.astype(jnp.bfloat16).reshape(sections, capacity, model_width)

    line = None
    if levels == 2:
        line = FourInLine(
            gate_raw,
            up_raw,
            stacked(down_raw, hidden_width),
            stacked(lax.optimization_barrier(static_part), hidden_width),
            own_mask,
        )
        bits = line.forward(bits)
        dispatched = after(dispatched, line.quiet)
        line.handed_up((dispatched,))
    arrived = lax.all_to_all(dispatched, "section", split_axis=0, concat_axis=0, tiled=True)
    rows = arrived.reshape(-1, model_width)
    cotangent = slot_cot[0, 0].reshape(-1, model_width)
    if line is not None:
        gate_mat, up_mat, static_in = line.handed_gate((rows,))
        static_in = side_by_side(static_in)
    else:
        gate_mat, up_mat, down_mat = [
            route(weight, own_mask, upward) for weight in (gate_raw, up_raw, down_raw)
        ]
        static_in = from_partner(static_part, 0)

    gate_act = jnp.dot(rows, gate_mat, preferred_element_type=jnp.float32)
    up_act = jnp.dot(rows, up_mat, preferred_element_type=jnp.float32)
    if line is not None:
        line.swap_down((up_act, gate_act))
    sigmoid_gate = jax.nn.sigmoid(gate_act)
    hidden = (gate_act * sigmoid_gate * up_act).astype(jnp.bfloat16)
    half = hidden_width // 2
    parts = [slice(0, half), slice(half, hidden_width)]
    down_grads, down_grads_in = [], []
    for part in parts:
        down_grads.append(
            lax.dot_general(
                hidden[:, part],
                cotangent,
                (((0,), (0,)), ((), ())),
                preferred_element_type=jnp.float32,
            ).astype(jnp.bfloat16)
        )
        down_grads_in.append(from_partner(down_grads[-1], 0))

    lower, top = upward[:-1], levels - 1
    own_bits, mine_bits, match_bits = [
        bits[number * levels : (number + 1) * levels] for number in range(3)
    ]
    if line is not None:
        sent = line.handed_down((down_grads[1],))
        static_in = lax.optimization_barrier(after(static_in, sent))
        down_grads_in[0] = after(down_grads_in[0], static_in)
        down_grads_in[1] = after(down_grads_in[1], line.down_hub)

    def combined(side, own_routed, match_routed, static_routed):
        def pick(bit, value):
            return jnp.where(bit == side, value.astype(jnp.float32), 0.0)

        return pick(match_bits[top], static_routed) + 0.5 * inner_rate * (
            pick(own_bits[top], own_routed) + pick(mine_bits[top], match_routed)
        )

    crossing_out, crossings, stayings = static_part, [], []
    for number, part in enumerate(parts):
        own_routed = match_routed = down_grads[number]
        down_grad_in = after(down_grads_in[number], crossing_out)
        static_routed = static_part[part]
        for index in lower:
            if index == 0:
                own_in, match_in, static_here = down_grad_in, down_grad_in, static_in[part]
            else:
                own_in = from_partner(own_routed, index)
                match_in = from_partner(match_routed, index)
                static_here = from_partner(static_routed, index)
            own_routed = jnp.where(own_bits[index], own_in, own_routed)
            match_routed = jnp.where(mine_bits[index], match_in, match_routed)
            static_routed = jnp.where(match_bits[index], static_here, static_routed)
        routed = (own_routed, match_routed, static_routed)
        crossing_out = lax.optimization_barrier(combined(True, *routed).astype(jnp.bfloat16))
        crossings.append(from_partner(crossing_out, top))
        stayings.append(combined(False, *(after(value, crossing_out) for value in routed)))
    slow_float = after(slow_down[0, 0], crossing_out).astype(jnp.float32)
    outer_here = (
        (0.5 + pull_rate) * slow_float - 0.5 * down_float + jnp.concatenate(stayings, axis=0)
    )
    pull = outer_rate * (1.0 + moment_rate)
    kept = (
        slow_float
        - pull * outer_here
        - (outer_rate * moment_rate * moment_rate) * momentum[0, 0].astype(jnp.float32)
    )
    if line is not None:
        down_mat = side_by_side(line.down_here((crossing_out,)))
    hidden_grad = lax.dot_general(
        cotangent, down_mat, contract, preferred_element_type=jnp.float32
    )
    gate_grad = (
        hidden_grad * up_act * sigmoid_gate * (1.0 + gate_act * (1.0 - sigmoid_gate))
    ).astype(jnp.bfloat16)
    up_grad = (hidden_grad * gate_act * sigmoid_gate).astype(jnp.bfloat16)
    slot_grad = (
        lax.dot_general(gate_grad, gate_mat, contract, preferred_element_type=jnp.float32)
        + lax.dot_general(up_grad, up_mat, contract, preferred_element_type=jnp.float32)
    ).astype(jnp.bfloat16)
    kept, *crossings = lax.optimization_barrier((kept, *crossings, slot_grad))[:3]
    crossing = jnp.concatenate(crossings, axis=0)
    new_slow = (kept - pull * crossing.astype(jnp.float32)).astype(jnp.bfloat16)
    slot_grad = slot_grad.reshape(sections, capacity, model_width)
    returned = lax.all_to_all(slot_grad, "section", split_axis=0, concat_axis=0, tiled=True)
    input_grad = jnp.dot(
        selector, returned.reshape(-1, model_width), preferred_element_type=jnp.float32
    ).astype(jnp.bfloat16)
    return (input_grad[None, None], new_slow[None, None])


def solution(mesh):
    in_specs = (
        P("section", "rep", None, None),
        P("section", "rep", None, None),
        P(),
        P(),
        P("section", "rep", None, None),
        P("section", "rep", None, None),
        P("section", "rep", None, None),
        P("section", "rep", None, None),
        P("section", "rep", None, None),
        P("section", "rep", None, None, None),
    )
    out_specs = (P("section", "rep", None, None), P("section", "rep", None, None))
    return jax.shard_map(
        on_device, mesh=mesh, in_specs=in_specs, out_specs=out_specs, check_vma=False
    )
```

```python
import jax
import jax.numpy as jnp
from jax import lax
from jax.sharding import PartitionSpec as P

inner_rate = 0.05
pull_rate = 0.25
moment_rate = 0.9
outer_rate = 0.7

OUTWARD = [(1, 0), (2, 3)]
INWARD = [(0, 1), (3, 2)]
ACROSS = [(1, 2), (2, 1)]


def from_partner(value, distance):
    pairs = [(source, source ^ 2**distance) for source in range(lax.axis_size("rep"))]
    return lax.ppermute(value, "rep", pairs)


def bit_of(mask, index):
    return jnp.bitwise_and(jnp.right_shift(mask, index), 1) == 1


def route(value, mask, bits):
    for index in bits:
        value = jnp.where(bit_of(mask, index), from_partner(value, index), value)
    return value


def after(value, *earlier):
    return lax.optimization_barrier((value, *earlier))[0]


def slot_table(expert_ids, sections, capacity):
    expert_hot = (expert_ids[:, None] == jnp.arange(sections, dtype=jnp.int32)[None, :]).astype(
        jnp.int32
    )
    position = jnp.sum((jnp.cumsum(expert_hot, axis=0) - 1) * expert_hot, axis=1)
    slot_index = expert_ids * capacity + position
    return (
        slot_index[:, None] == jnp.arange(sections * capacity, dtype=jnp.int32)[None, :]
    ).astype(jnp.bfloat16)


def stacked(wide, width):
    return jnp.concatenate(jnp.split(wide, wide.shape[1] // width, axis=1), axis=0)


def side_by_side(tall):
    return jnp.concatenate(jnp.split(tall, tall.shape[0] // tall.shape[1], axis=0), axis=1)


class FourInLine:
    def __init__(self, gate, up, down, static_part, mask):
        replica = lax.axis_index("rep")
        self.inner = (replica == 1) | (replica == 2)
        self.near, self.far = mask == 1, mask == 3
        self.gate, self.up, self.down = gate, up, down
        self.static_part = static_part

    def forward(self, bits):
        self.up_side = lax.ppermute(self.up, "rep", INWARD)
        self.gate_hub = lax.ppermute(self.gate, "rep", ACROSS)
        inner, self.near, self.far, *bits = lax.optimization_barrier(
            (self.inner, self.near, self.far, *bits)
        )
        send = lax.optimization_barrier(jnp.where(inner, self.static_part, self.gate))
        self.one = from_partner(send, 0)
        side, self.gate_hub, self.near, self.far = lax.optimization_barrier(
            (self.up_side, self.gate_hub, self.near, self.far)
        )
        first = jnp.where(self.far, side, self.up)
        second = jnp.where(self.far, self.up, side)
        first_in = lax.ppermute(first, "rep", ACROSS)
        self.quiet, self.first_in = first, first_in
        self.gate_edge = lax.ppermute(self.one, "rep", ACROSS)
        self.second = second
        return bits

    def handed_up(self, earlier):
        first_in = after(self.first_in, *earlier)
        send = jnp.where(self.inner, jnp.where(self.near, self.up, first_in), self.down)
        self.two = from_partner(send, 0)
        self.up_hub = lax.ppermute(after(self.second, send), "rep", ACROSS)
        self.later = send

    def handed_gate(self, earlier):
        gate_edge = after(self.gate_edge, self.later, *earlier)
        gate_out = jnp.where(
            self.near, self.gate, jnp.where(self.far, gate_edge, self.gate_hub)
        )
        send = jnp.where(self.inner, gate_out, self.static_part)
        self.three = from_partner(send, 0)
        two = after(self.two, send)
        first = jnp.where(self.far, two, self.down)
        second = jnp.where(self.far, self.down, two)
        self.down_first = lax.ppermute(first, "rep", ACROSS)
        gate_in = jnp.where(
            self.near, self.one, jnp.where(self.far, self.gate_hub, self.gate_edge)
        )
        two, up_hub = lax.optimization_barrier((two, self.up_hub, first))[:2]
        self.second_down = second
        up_in = jnp.where(self.near, self.up_side, up_hub)
        self.gate_in = gate_in
        return jnp.where(self.inner, up_in, two)

    def gate_here(self, earlier):
        three = after(self.three, *earlier)
        static_in = jnp.where(self.inner, three, self.one)
        return lax.optimization_barrier(jnp.where(self.inner, self.gate_in, three)), static_in

    def swap_down(self, earlier):
        second = after(self.second_down, *earlier)
        self.down_hub = lax.ppermute(second, "rep", ACROSS)

    def handed_down(self, earlier):
        send = jnp.where(self.near, self.down, after(self.down_first, *earlier))
        self.four = lax.ppermute(send, "rep", OUTWARD)
        return send

    def down_here(self, earlier):
        down_hub = after(self.down_hub, *earlier)
        down_in = jnp.where(self.near, self.two, down_hub)
        return jnp.where(self.inner, down_in, self.four)


def on_device(
    tokens,
    assign,
    route_mask,
    match_mask,
    gate_weight,
    up_weight,
    down_weight,
    slow_down,
    momentum,
    slot_cot,
):
    sections = lax.axis_size("section")
    levels = lax.axis_size("rep").bit_length() - 1
    section_here = lax.axis_index("section")
    token_rows = tokens[0, 0]
    expert_ids = assign[0, 0, :, 0]
    capacity = slot_cot.shape[3]
    model_width = token_rows.shape[1]
    masks_here = lax.dynamic_index_in_dim(
        jnp.stack([route_mask, match_mask]), section_here, axis=1, keepdims=False
    )
    own_mask, match = masks_here[0], masks_here[1]
    match_mine = jnp.bitwise_xor(own_mask, match)
    upward = list(range(levels))
    bits = [bit_of(mask, index) for mask in (own_mask, match_mine, match) for index in upward]
    contract = (((1,), (1,)), ((), ()))
    hidden_width = gate_weight.shape[3]

    gate_raw, up_raw, down_raw = gate_weight[0, 0], up_weight[0, 0], down_weight[0, 0]
    slow_float = slow_down[0, 0].astype(jnp.float32)
    down_float = down_raw.astype(jnp.float32)
    static_part = ((0.5 - pull_rate) * slow_float - 0.5 * down_float).astype(jnp.bfloat16)

    selector = slot_table(expert_ids, sections, capacity)
    placed = lax.dot_general(
        selector, token_rows, (((0,), (0,)), ((), ())), preferred_element_type=jnp.float32
    )
    dispatched = placed.astype(jnp.bfloat16).reshape(sections, capacity, model_width)

    line = None
    if levels == 2:
        line = FourInLine(
            gate_raw,
            up_raw,
            stacked(down_raw, hidden_width),
            stacked(lax.optimization_barrier(static_part), hidden_width),
            own_mask,
        )
        bits = line.forward(bits)
        dispatched = after(dispatched, line.quiet)
        line.handed_up((dispatched,))
    arrived = lax.all_to_all(dispatched, "section", split_axis=0, concat_axis=0, tiled=True)
    rows = arrived.reshape(-1, model_width)
    cotangent = slot_cot[0, 0].reshape(-1, model_width)
    if line is not None:
        up_mat = line.handed_gate((rows,))
    else:
        gate_mat, up_mat, down_mat = [
            route(weight, own_mask, upward) for weight in (gate_raw, up_raw, down_raw)
        ]
        static_in = from_partner(static_part, 0)

    up_act = jnp.dot(rows, up_mat, preferred_element_type=jnp.float32)
    if line is not None:
        gate_mat, static_in = line.gate_here((up_act,))
        static_in = side_by_side(static_in)
    gate_act = jnp.dot(rows, gate_mat, preferred_element_type=jnp.float32)
    sigmoid_gate = jax.nn.sigmoid(gate_act)
    hidden = (gate_act * sigmoid_gate * up_act).astype(jnp.bfloat16)
    down_grad = lax.dot_general(
        hidden, cotangent, (((0,), (0,)), ((), ())), preferred_element_type=jnp.float32
    ).astype(jnp.bfloat16)

    if line is not None:
        line.swap_down((down_grad,))

    own_bits, mine_bits, match_bits = [
        bits[number * levels : (number + 1) * levels] for number in range(3)
    ]
    lower, top = upward[:-1], levels - 1
    down_grad_in = from_partner(down_grad, 0)
    if line is not None:
        sent = line.handed_down((down_grad,))
        static_in = after(static_in, sent)
        down_grad_in = after(down_grad_in, static_in, line.down_hub)
    own_routed, match_routed, static_routed = down_grad, down_grad, static_part
    for index in lower:
        if index == 0:
            own_in, match_in, static_here = down_grad_in, down_grad_in, static_in
        else:
            own_in = from_partner(own_routed, index)
            match_in = from_partner(match_routed, index)
            static_here = from_partner(static_routed, index)
        own_routed = jnp.where(own_bits[index], own_in, own_routed)
        match_routed = jnp.where(mine_bits[index], match_in, match_routed)
        static_routed = jnp.where(match_bits[index], static_here, static_routed)

    def combined(side, static_routed, own_routed, match_routed):
        def pick(bit, value):
            return jnp.where(bit == side, value.astype(jnp.float32), 0.0)

        return pick(match_bits[top], static_routed) + 0.5 * inner_rate * (
            pick(own_bits[top], own_routed) + pick(mine_bits[top], match_routed)
        )

    crossing_out = combined(True, static_routed, own_routed, match_routed).astype(jnp.bfloat16)
    crossing = from_partner(crossing_out, top)
    slow_float = after(slow_down[0, 0], crossing_out).astype(jnp.float32)
    staying = combined(False, static_routed, own_routed, match_routed)
    outer_here = (0.5 + pull_rate) * slow_float - 0.5 * down_float + staying
    pull = outer_rate * (1.0 + moment_rate)
    kept = (
        slow_float
        - pull * outer_here
        - (outer_rate * moment_rate * moment_rate) * momentum[0, 0].astype(jnp.float32)
    )
    kept = after(kept, crossing_out)
    new_slow = (kept - pull * crossing.astype(jnp.float32)).astype(jnp.bfloat16)

    if line is not None:
        down_mat = side_by_side(line.down_here((crossing_out,)))
    hidden_grad = lax.dot_general(
        cotangent, down_mat, contract, preferred_element_type=jnp.float32
    )
    gate_grad = (
        hidden_grad * up_act * sigmoid_gate * (1.0 + gate_act * (1.0 - sigmoid_gate))
    ).astype(jnp.bfloat16)
    up_grad = (hidden_grad * gate_act * sigmoid_gate).astype(jnp.bfloat16)
    slot_grad = (
        lax.dot_general(gate_grad, gate_mat, contract, preferred_element_type=jnp.float32)
        + lax.dot_general(up_grad, up_mat, contract, preferred_element_type=jnp.float32)
    ).astype(jnp.bfloat16)
    slot_grad = slot_grad.reshape(sections, capacity, model_width)
    returned = lax.all_to_all(slot_grad, "section", split_axis=0, concat_axis=0, tiled=True)
    input_grad = jnp.dot(
        selector, returned.reshape(-1, model_width), preferred_element_type=jnp.float32
    ).astype(jnp.bfloat16)
    return (input_grad[None, None], new_slow[None, None])


def solution(mesh):
    in_specs = (
        P("section", "rep", None, None),
        P("section", "rep", None, None),
        P(),
        P(),
        P("section", "rep", None, None),
        P("section", "rep", None, None),
        P("section", "rep", None, None),
        P("section", "rep", None, None),
        P("section", "rep", None, None),
        P("section", "rep", None, None, None),
    )
    out_specs = (P("section", "rep", None, None), P("section", "rep", None, None))
    return jax.shard_map(
        on_device, mesh=mesh, in_specs=in_specs, out_specs=out_specs, check_vma=False
    )
```

```python
import jax
import jax.numpy as jnp
from jax import lax
from jax.sharding import PartitionSpec as P

inner_rate = 0.05
pull_rate = 0.25
moment_rate = 0.9
outer_rate = 0.7

OUTWARD = [(1, 0), (2, 3)]
INWARD = [(0, 1), (3, 2)]
ACROSS = [(1, 2), (2, 1)]


def from_partner(value, distance):
    pairs = [(source, source ^ 2**distance) for source in range(lax.axis_size("rep"))]
    return lax.ppermute(value, "rep", pairs)


def bit_of(mask, index):
    return jnp.bitwise_and(jnp.right_shift(mask, index), 1) == 1


def route(value, mask, bits):
    for index in bits:
        value = jnp.where(bit_of(mask, index), from_partner(value, index), value)
    return value


def after(value, *earlier):
    return lax.optimization_barrier((value, *earlier))[0]


def slot_table(expert_ids, sections, capacity):
    expert_hot = (expert_ids[:, None] == jnp.arange(sections, dtype=jnp.int32)[None, :]).astype(
        jnp.int32
    )
    position = jnp.sum((jnp.cumsum(expert_hot, axis=0) - 1) * expert_hot, axis=1)
    slot_index = expert_ids * capacity + position
    return (
        slot_index[:, None] == jnp.arange(sections * capacity, dtype=jnp.int32)[None, :]
    ).astype(jnp.bfloat16)


def stacked(wide, width):
    return jnp.concatenate(jnp.split(wide, wide.shape[1] // width, axis=1), axis=0)


def side_by_side(tall):
    return jnp.concatenate(jnp.split(tall, tall.shape[0] // tall.shape[1], axis=0), axis=1)


class FourInLine:
    def __init__(self, gate, up, down, static_part, mask):
        replica = lax.axis_index("rep")
        self.inner = (replica == 1) | (replica == 2)
        self.near, self.far = mask == 1, mask == 3
        self.gate, self.up, self.down = gate, up, down
        self.static_part = static_part

    def forward(self, bits):
        self.up_side = lax.ppermute(self.up, "rep", INWARD)
        self.gate_hub = lax.ppermute(self.gate, "rep", ACROSS)
        inner, self.near, self.far, *bits = lax.optimization_barrier(
            (self.inner, self.near, self.far, *bits)
        )
        send = lax.optimization_barrier(jnp.where(inner, self.static_part, self.gate))
        self.one = from_partner(send, 0)
        side, self.gate_hub, self.near, self.far = lax.optimization_barrier(
            (self.up_side, self.gate_hub, self.near, self.far)
        )
        first = jnp.where(self.far, side, self.up)
        second = jnp.where(self.far, self.up, side)
        first_in = lax.ppermute(first, "rep", ACROSS)
        self.quiet, self.first_in = first, first_in
        self.gate_edge = lax.ppermute(self.one, "rep", ACROSS)
        self.second = second
        return bits

    def handed_up(self, earlier):
        first_in = after(self.first_in, *earlier)
        send = jnp.where(self.inner, jnp.where(self.near, self.up, first_in), self.down)
        self.two = from_partner(send, 0)
        self.up_hub = lax.ppermute(after(self.second, send), "rep", ACROSS)
        self.later = send

    def handed_gate(self, earlier):
        gate_edge = after(self.gate_edge, self.later, *earlier)
        gate_out = jnp.where(
            self.near, self.gate, jnp.where(self.far, gate_edge, self.gate_hub)
        )
        send = jnp.where(self.inner, gate_out, self.static_part)
        self.three = from_partner(send, 0)
        two = after(self.two, send)
        first = jnp.where(self.far, two, self.down)
        second = jnp.where(self.far, self.down, two)
        self.down_first = lax.ppermute(first, "rep", ACROSS)
        gate_in = jnp.where(
            self.near, self.one, jnp.where(self.far, self.gate_hub, self.gate_edge)
        )
        two, up_hub = lax.optimization_barrier((two, self.up_hub, first))[:2]
        self.second_down = second
        up_in = jnp.where(self.near, self.up_side, up_hub)
        self.gate_in = gate_in
        return jnp.where(self.inner, up_in, two)

    def gate_here(self, earlier):
        three = after(self.three, *earlier)
        static_in = jnp.where(self.inner, three, self.one)
        return lax.optimization_barrier(jnp.where(self.inner, self.gate_in, three)), static_in

    def swap_down(self, earlier):
        second = after(self.second_down, *earlier)
        self.down_hub = lax.ppermute(second, "rep", ACROSS)

    def handed_down(self, earlier):
        send = jnp.where(self.near, self.down, after(self.down_first, *earlier))
        self.four = lax.ppermute(send, "rep", OUTWARD)
        return send

    def down_here(self, earlier):
        down_hub = after(self.down_hub, *earlier)
        down_in = jnp.where(self.near, self.two, down_hub)
        return jnp.where(self.inner, down_in, self.four)


def on_device(
    tokens,
    assign,
    route_mask,
    match_mask,
    gate_weight,
    up_weight,
    down_weight,
    slow_down,
    momentum,
    slot_cot,
):
    sections = lax.axis_size("section")
    levels = lax.axis_size("rep").bit_length() - 1
    section_here = lax.axis_index("section")
    token_rows = tokens[0, 0]
    expert_ids = assign[0, 0, :, 0]
    capacity = slot_cot.shape[3]
    model_width = token_rows.shape[1]
    masks_here = lax.dynamic_index_in_dim(
        jnp.stack([route_mask, match_mask]), section_here, axis=1, keepdims=False
    )
    own_mask, match = masks_here[0], masks_here[1]
    match_mine = jnp.bitwise_xor(own_mask, match)
    upward = list(range(levels))
    bits = [bit_of(mask, index) for mask in (own_mask, match_mine, match) for index in upward]
    contract = (((1,), (1,)), ((), ()))
    hidden_width = gate_weight.shape[3]

    gate_raw, up_raw, down_raw = gate_weight[0, 0], up_weight[0, 0], down_weight[0, 0]
    slow_float = slow_down[0, 0].astype(jnp.float32)
    down_float = down_raw.astype(jnp.float32)
    static_part = ((0.5 - pull_rate) * slow_float - 0.5 * down_float).astype(jnp.bfloat16)

    selector = slot_table(expert_ids, sections, capacity)
    placed = lax.dot_general(
        selector, token_rows, (((0,), (0,)), ((), ())), preferred_element_type=jnp.float32
    )
    dispatched = placed.astype(jnp.bfloat16).reshape(sections, capacity, model_width)

    line = None
    if levels == 2:
        line = FourInLine(
            gate_raw,
            up_raw,
            stacked(down_raw, hidden_width),
            stacked(lax.optimization_barrier(static_part), hidden_width),
            own_mask,
        )
        bits = line.forward(bits)
        dispatched = after(dispatched, line.quiet)
        line.handed_up((dispatched,))
    arrived = lax.all_to_all(dispatched, "section", split_axis=0, concat_axis=0, tiled=True)
    rows = arrived.reshape(-1, model_width)
    cotangent = slot_cot[0, 0].reshape(-1, model_width)
    if line is not None:
        up_mat = line.handed_gate((rows,))
    else:
        gate_mat, up_mat, down_mat = [
            route(weight, own_mask, upward) for weight in (gate_raw, up_raw, down_raw)
        ]
        static_in = from_partner(static_part, 0)

    up_act = jnp.dot(rows, up_mat, preferred_element_type=jnp.float32)
    if line is not None:
        gate_mat, static_in = line.gate_here((up_act,))
        static_in = side_by_side(static_in)
    gate_act = jnp.dot(rows, gate_mat, preferred_element_type=jnp.float32)
    sigmoid_gate = jax.nn.sigmoid(gate_act)
    hidden = (gate_act * sigmoid_gate * up_act).astype(jnp.bfloat16)
    down_grad = lax.dot_general(
        hidden, cotangent, (((0,), (0,)), ((), ())), preferred_element_type=jnp.float32
    ).astype(jnp.bfloat16)

    if line is not None:
        line.swap_down((down_grad,))

    own_bits, mine_bits, match_bits = [
        bits[number * levels : (number + 1) * levels] for number in range(3)
    ]
    lower, top = upward[:-1], levels - 1
    down_grad_in = from_partner(down_grad, 0)
    if line is not None:
        sent = line.handed_down((down_grad,))
        static_in = after(static_in, sent)
        down_grad_in = after(down_grad_in, static_in)
    own_routed, match_routed, static_routed = down_grad, down_grad, static_part
    for index in lower:
        if index == 0:
            own_in, match_in, static_here = down_grad_in, down_grad_in, static_in
        else:
            own_in = from_partner(own_routed, index)
            match_in = from_partner(match_routed, index)
            static_here = from_partner(static_routed, index)
        own_routed = jnp.where(own_bits[index], own_in, own_routed)
        match_routed = jnp.where(mine_bits[index], match_in, match_routed)
        static_routed = jnp.where(match_bits[index], static_here, static_routed)

    def combined(side, static_routed, own_routed, match_routed):
        def pick(bit, value):
            return jnp.where(bit == side, value.astype(jnp.float32), 0.0)

        return pick(match_bits[top], static_routed) + 0.5 * inner_rate * (
            pick(own_bits[top], own_routed) + pick(mine_bits[top], match_routed)
        )

    crossing_out = combined(True, static_routed, own_routed, match_routed).astype(jnp.bfloat16)
    crossing = from_partner(crossing_out, top)
    slow_float = after(slow_down[0, 0], crossing_out).astype(jnp.float32)
    staying = combined(False, static_routed, own_routed, match_routed)
    outer_here = (0.5 + pull_rate) * slow_float - 0.5 * down_float + staying
    pull = outer_rate * (1.0 + moment_rate)
    kept = (
        slow_float
        - pull * outer_here
        - (outer_rate * moment_rate * moment_rate) * momentum[0, 0].astype(jnp.float32)
    )
    kept = after(kept, crossing_out)
    new_slow = (kept - pull * crossing.astype(jnp.float32)).astype(jnp.bfloat16)

    if line is not None:
        down_mat = side_by_side(line.down_here((crossing_out,)))
    hidden_grad = lax.dot_general(
        cotangent, down_mat, contract, preferred_element_type=jnp.float32
    )
    gate_grad = (
        hidden_grad * up_act * sigmoid_gate * (1.0 + gate_act * (1.0 - sigmoid_gate))
    ).astype(jnp.bfloat16)
    up_grad = (hidden_grad * gate_act * sigmoid_gate).astype(jnp.bfloat16)
    slot_grad = (
        lax.dot_general(gate_grad, gate_mat, contract, preferred_element_type=jnp.float32)
        + lax.dot_general(up_grad, up_mat, contract, preferred_element_type=jnp.float32)
    ).astype(jnp.bfloat16)
    slot_grad = slot_grad.reshape(sections, capacity, model_width)
    returned = lax.all_to_all(slot_grad, "section", split_axis=0, concat_axis=0, tiled=True)
    input_grad = jnp.dot(
        selector, returned.reshape(-1, model_width), preferred_element_type=jnp.float32
    ).astype(jnp.bfloat16)
    return (input_grad[None, None], new_slow[None, None])


def solution(mesh):
    in_specs = (
        P("section", "rep", None, None),
        P("section", "rep", None, None),
        P(),
        P(),
        P("section", "rep", None, None),
        P("section", "rep", None, None),
        P("section", "rep", None, None),
        P("section", "rep", None, None),
        P("section", "rep", None, None),
        P("section", "rep", None, None, None),
    )
    out_specs = (P("section", "rep", None, None), P("section", "rep", None, None))
    return jax.shard_map(
        on_device, mesh=mesh, in_specs=in_specs, out_specs=out_specs, check_vma=False
    )
```

```python
import jax
import jax.numpy as jnp
from jax import lax
from jax.sharding import PartitionSpec as P

inner_rate = 0.05
pull_rate = 0.25
moment_rate = 0.9
outer_rate = 0.7

OUTWARD = [(1, 0), (2, 3)]
INWARD = [(0, 1), (3, 2)]
ACROSS = [(1, 2), (2, 1)]


def from_partner(value, distance):
    pairs = [(source, source ^ 2**distance) for source in range(lax.axis_size("rep"))]
    return lax.ppermute(value, "rep", pairs)


def bit_of(mask, index):
    return jnp.bitwise_and(jnp.right_shift(mask, index), 1) == 1


def route(value, mask, bits):
    for index in bits:
        value = jnp.where(bit_of(mask, index), from_partner(value, index), value)
    return value


def after(value, *earlier):
    return lax.optimization_barrier((value, *earlier))[0]


def slot_table(expert_ids, sections, capacity):
    expert_hot = (expert_ids[:, None] == jnp.arange(sections, dtype=jnp.int32)[None, :]).astype(
        jnp.int32
    )
    position = jnp.sum((jnp.cumsum(expert_hot, axis=0) - 1) * expert_hot, axis=1)
    slot_index = expert_ids * capacity + position
    return (
        slot_index[:, None] == jnp.arange(sections * capacity, dtype=jnp.int32)[None, :]
    ).astype(jnp.bfloat16)


def stacked(wide, width):
    return jnp.concatenate(jnp.split(wide, wide.shape[1] // width, axis=1), axis=0)


def side_by_side(tall):
    return jnp.concatenate(jnp.split(tall, tall.shape[0] // tall.shape[1], axis=0), axis=1)


class FourInLine:
    def __init__(self, gate, up, down, static_part, mask):
        replica = lax.axis_index("rep")
        self.inner = (replica == 1) | (replica == 2)
        self.near, self.far = mask == 1, mask == 3
        self.gate, self.up, self.down = gate, up, down
        self.static_part = static_part

    def forward(self, bits):
        self.up_side = lax.ppermute(self.up, "rep", INWARD)
        self.gate_hub = lax.ppermute(self.gate, "rep", ACROSS)
        inner, self.near, self.far, *bits = lax.optimization_barrier(
            (self.inner, self.near, self.far, *bits)
        )
        send = lax.optimization_barrier(jnp.where(inner, self.static_part, self.gate))
        self.one = from_partner(send, 0)
        side, self.gate_hub, self.near, self.far = lax.optimization_barrier(
            (self.up_side, self.gate_hub, self.near, self.far)
        )
        first = jnp.where(self.far, side, self.up)
        second = jnp.where(self.far, self.up, side)
        first_in = lax.ppermute(first, "rep", ACROSS)
        self.quiet, self.first_in = first, first_in
        self.gate_edge = lax.ppermute(self.one, "rep", ACROSS)
        self.second = second
        return bits

    def handed_up(self, earlier):
        first_in = after(self.first_in, *earlier)
        send = jnp.where(self.inner, jnp.where(self.near, self.up, first_in), self.down)
        self.two = from_partner(send, 0)
        self.up_hub = lax.ppermute(after(self.second, send), "rep", ACROSS)
        self.later = send

    def handed_gate(self, earlier):
        gate_edge = after(self.gate_edge, self.later, *earlier)
        gate_out = jnp.where(
            self.near, self.gate, jnp.where(self.far, gate_edge, self.gate_hub)
        )
        send = jnp.where(self.inner, gate_out, self.static_part)
        self.three = from_partner(send, 0)
        two = after(self.two, send)
        first = jnp.where(self.far, two, self.down)
        second = jnp.where(self.far, self.down, two)
        self.down_first = lax.ppermute(first, "rep", ACROSS)
        gate_in = jnp.where(
            self.near, self.one, jnp.where(self.far, self.gate_hub, self.gate_edge)
        )
        two, up_hub = lax.optimization_barrier((two, self.up_hub, first))[:2]
        self.second_down = second
        up_in = jnp.where(self.near, self.up_side, up_hub)
        self.gate_in = gate_in
        return jnp.where(self.inner, up_in, two)

    def gate_here(self, earlier):
        three = after(self.three, *earlier)
        static_in = jnp.where(self.inner, three, self.one)
        return lax.optimization_barrier(jnp.where(self.inner, self.gate_in, three)), static_in

    def swap_down(self, earlier):
        second = after(self.second_down, *earlier)
        self.down_hub = lax.ppermute(second, "rep", ACROSS)

    def handed_down(self, earlier):
        send = jnp.where(self.near, self.down, after(self.down_first, *earlier))
        self.four = lax.ppermute(send, "rep", OUTWARD)
        return send

    def down_here(self, earlier):
        down_hub = after(self.down_hub, *earlier)
        down_in = jnp.where(self.near, self.two, down_hub)
        return jnp.where(self.inner, down_in, self.four)


def on_device(
    tokens,
    assign,
    route_mask,
    match_mask,
    gate_weight,
    up_weight,
    down_weight,
    slow_down,
    momentum,
    slot_cot,
):
    sections = lax.axis_size("section")
    levels = lax.axis_size("rep").bit_length() - 1
    section_here = lax.axis_index("section")
    token_rows = tokens[0, 0]
    expert_ids = assign[0, 0, :, 0]
    capacity = slot_cot.shape[3]
    model_width = token_rows.shape[1]
    masks_here = lax.dynamic_index_in_dim(
        jnp.stack([route_mask, match_mask]), section_here, axis=1, keepdims=False
    )
    own_mask, match = masks_here[0], masks_here[1]
    match_mine = jnp.bitwise_xor(own_mask, match)
    upward = list(range(levels))
    bits = [bit_of(mask, index) for mask in (own_mask, match_mine, match) for index in upward]
    contract = (((1,), (1,)), ((), ()))
    hidden_width = gate_weight.shape[3]

    gate_raw, up_raw, down_raw = gate_weight[0, 0], up_weight[0, 0], down_weight[0, 0]
    slow_float = slow_down[0, 0].astype(jnp.float32)
    down_float = down_raw.astype(jnp.float32)
    static_part = ((0.5 - pull_rate) * slow_float - 0.5 * down_float).astype(jnp.bfloat16)

    selector = slot_table(expert_ids, sections, capacity)
    placed = lax.dot_general(
        selector, token_rows, (((0,), (0,)), ((), ())), preferred_element_type=jnp.float32
    )
    dispatched = placed.astype(jnp.bfloat16).reshape(sections, capacity, model_width)

    line = None
    if levels == 2:
        line = FourInLine(
            gate_raw,
            up_raw,
            stacked(down_raw, hidden_width),
            stacked(lax.optimization_barrier(static_part), hidden_width),
            own_mask,
        )
        bits = line.forward(bits)
        dispatched = after(dispatched, line.quiet)
        line.handed_up((dispatched,))
    arrived = lax.all_to_all(dispatched, "section", split_axis=0, concat_axis=0, tiled=True)
    rows = arrived.reshape(-1, model_width)
    cotangent = slot_cot[0, 0].reshape(-1, model_width)
    if line is not None:
        up_mat = line.handed_gate((rows,))
    else:
        gate_mat, up_mat, down_mat = [
            route(weight, own_mask, upward) for weight in (gate_raw, up_raw, down_raw)
        ]
        static_in = from_partner(static_part, 0)

    up_act = jnp.dot(rows, up_mat, preferred_element_type=jnp.float32)
    if line is not None:
        line.swap_down((up_act,))
        gate_mat, static_in = line.gate_here((up_act,))
        static_in = side_by_side(static_in)
    gate_act = jnp.dot(rows, gate_mat, preferred_element_type=jnp.float32)
    sigmoid_gate = jax.nn.sigmoid(gate_act)
    hidden = (gate_act * sigmoid_gate * up_act).astype(jnp.bfloat16)
    down_grad = lax.dot_general(
        hidden, cotangent, (((0,), (0,)), ((), ())), preferred_element_type=jnp.float32
    ).astype(jnp.bfloat16)

    own_bits, mine_bits, match_bits = [
        bits[number * levels : (number + 1) * levels] for number in range(3)
    ]
    lower, top = upward[:-1], levels - 1
    down_grad_in = from_partner(down_grad, 0)
    if line is not None:
        sent = line.handed_down((down_grad,))
        static_in = after(static_in, sent)
        down_grad_in = after(down_grad_in, static_in, line.down_hub)
    own_routed, match_routed, static_routed = down_grad, down_grad, static_part
    for index in lower:
        if index == 0:
            own_in, match_in, static_here = down_grad_in, down_grad_in, static_in
        else:
            own_in = from_partner(own_routed, index)
            match_in = from_partner(match_routed, index)
            static_here = from_partner(static_routed, index)
        own_routed = jnp.where(own_bits[index], own_in, own_routed)
        match_routed = jnp.where(mine_bits[index], match_in, match_routed)
        static_routed = jnp.where(match_bits[index], static_here, static_routed)

    def combined(side, static_routed, own_routed, match_routed):
        def pick(bit, value):
            return jnp.where(bit == side, value.astype(jnp.float32), 0.0)

        return pick(match_bits[top], static_routed) + 0.5 * inner_rate * (
            pick(own_bits[top], own_routed) + pick(mine_bits[top], match_routed)
        )

    crossing_out = combined(True, static_routed, own_routed, match_routed).astype(jnp.bfloat16)
    crossing = from_partner(crossing_out, top)
    slow_float = after(slow_down[0, 0], crossing_out).astype(jnp.float32)
    staying = combined(False, static_routed, own_routed, match_routed)
    outer_here = (0.5 + pull_rate) * slow_float - 0.5 * down_float + staying
    pull = outer_rate * (1.0 + moment_rate)
    kept = (
        slow_float
        - pull * outer_here
        - (outer_rate * moment_rate * moment_rate) * momentum[0, 0].astype(jnp.float32)
    )
    kept = after(kept, crossing_out)
    new_slow = (kept - pull * crossing.astype(jnp.float32)).astype(jnp.bfloat16)

    if line is not None:
        down_mat = side_by_side(line.down_here((crossing_out,)))
    hidden_grad = lax.dot_general(
        cotangent, down_mat, contract, preferred_element_type=jnp.float32
    )
    gate_grad = (
        hidden_grad * up_act * sigmoid_gate * (1.0 + gate_act * (1.0 - sigmoid_gate))
    ).astype(jnp.bfloat16)
    up_grad = (hidden_grad * gate_act * sigmoid_gate).astype(jnp.bfloat16)
    slot_grad = (
        lax.dot_general(gate_grad, gate_mat, contract, preferred_element_type=jnp.float32)
        + lax.dot_general(up_grad, up_mat, contract, preferred_element_type=jnp.float32)
    ).astype(jnp.bfloat16)
    slot_grad = slot_grad.reshape(sections, capacity, model_width)
    returned = lax.all_to_all(slot_grad, "section", split_axis=0, concat_axis=0, tiled=True)
    input_grad = jnp.dot(
        selector, returned.reshape(-1, model_width), preferred_element_type=jnp.float32
    ).astype(jnp.bfloat16)
    return (input_grad[None, None], new_slow[None, None])


def solution(mesh):
    in_specs = (
        P("section", "rep", None, None),
        P("section", "rep", None, None),
        P(),
        P(),
        P("section", "rep", None, None),
        P("section", "rep", None, None),
        P("section", "rep", None, None),
        P("section", "rep", None, None),
        P("section", "rep", None, None),
        P("section", "rep", None, None, None),
    )
    out_specs = (P("section", "rep", None, None), P("section", "rep", None, None))
    return jax.shard_map(
        on_device, mesh=mesh, in_specs=in_specs, out_specs=out_specs, check_vma=False
    )
```

```python
import jax
import jax.numpy as jnp
from jax import lax
from jax.sharding import PartitionSpec as P

inner_rate = 0.05
pull_rate = 0.25
moment_rate = 0.9
outer_rate = 0.7

OUTWARD = [(1, 0), (2, 3)]
BEYOND = [(1, 3), (2, 0)]
INWARD = [(0, 1), (3, 2)]
ACROSS = [(1, 2), (2, 1)]


def from_partner(value, distance):
    pairs = [(source, source ^ 2**distance) for source in range(lax.axis_size("rep"))]
    return lax.ppermute(value, "rep", pairs)


def bit_of(mask, index):
    return jnp.bitwise_and(jnp.right_shift(mask, index), 1) == 1


def route(value, mask, bits):
    for index in bits:
        value = jnp.where(bit_of(mask, index), from_partner(value, index), value)
    return value


def after(value, *earlier):
    return lax.optimization_barrier((value, *earlier))[0]


def slot_table(expert_ids, sections, capacity):
    expert_hot = (expert_ids[:, None] == jnp.arange(sections, dtype=jnp.int32)[None, :]).astype(
        jnp.int32
    )
    position = jnp.sum((jnp.cumsum(expert_hot, axis=0) - 1) * expert_hot, axis=1)
    slot_index = expert_ids * capacity + position
    return (
        slot_index[:, None] == jnp.arange(sections * capacity, dtype=jnp.int32)[None, :]
    ).astype(jnp.bfloat16)


def stacked(wide, width):
    return jnp.concatenate(jnp.split(wide, wide.shape[1] // width, axis=1), axis=0)


def side_by_side(tall):
    return jnp.concatenate(jnp.split(tall, tall.shape[0] // tall.shape[1], axis=0), axis=1)


class FourInLine:
    def __init__(self, gate, up, down, static_part, mask):
        replica = lax.axis_index("rep")
        self.inner = (replica == 1) | (replica == 2)
        self.near, self.far = mask == 1, mask == 3
        self.gate, self.up, self.down = gate, up, down
        self.static_part = static_part

    def forward(self, bits):
        self.up_side = lax.ppermute(self.up, "rep", INWARD)
        self.gate_hub = lax.ppermute(self.gate, "rep", ACROSS)
        inner, self.near, self.far, *bits = lax.optimization_barrier(
            (self.inner, self.near, self.far, *bits)
        )
        send = lax.optimization_barrier(jnp.where(inner, self.static_part, self.gate))
        self.one = from_partner(send, 0)
        side, self.gate_hub, self.near, self.far = lax.optimization_barrier(
            (self.up_side, self.gate_hub, self.near, self.far)
        )
        first = jnp.where(self.far, side, self.up)
        second = jnp.where(self.far, self.up, side)
        first_in = lax.ppermute(first, "rep", ACROSS)
        self.quiet, self.first_in = first, first_in
        self.down_out = lax.ppermute(self.down, "rep", OUTWARD)
        self.gate_edge = lax.ppermute(self.one, "rep", ACROSS)
        self.second = second
        return bits

    def handed_up(self, earlier):
        first_in, self.down_out = lax.optimization_barrier(
            (self.first_in, self.down_out, *earlier)
        )[:2]
        send = jnp.where(self.inner, jnp.where(self.near, self.up, first_in), self.down)
        self.two = from_partner(send, 0)
        self.up_hub = lax.ppermute(after(self.second, send), "rep", ACROSS)
        self.later = send

    def handed_gate(self, earlier):
        gate_edge = after(self.gate_edge, self.later, *earlier)
        gate_out = jnp.where(
            self.near, self.gate, jnp.where(self.far, gate_edge, self.gate_hub)
        )
        send = jnp.where(self.inner, gate_out, self.static_part)
        self.three = from_partner(send, 0)
        two = after(self.two, send)
        first = jnp.where(self.far, two, self.down)
        second = jnp.where(self.far, self.down, two)
        self.down_first = lax.ppermute(first, "rep", BEYOND)
        gate_in = jnp.where(
            self.near, self.one, jnp.where(self.far, self.gate_hub, self.gate_edge)
        )
        two, up_hub = lax.optimization_barrier((two, self.up_hub, first))[:2]
        self.second_down = second
        up_in = jnp.where(self.near, self.up_side, up_hub)
        self.gate_in = gate_in
        return jnp.where(self.inner, up_in, two)

    def gate_here(self, earlier):
        three = after(self.three, *earlier)
        static_in = jnp.where(self.inner, three, self.one)
        return lax.optimization_barrier(jnp.where(self.inner, self.gate_in, three)), static_in

    def swap_down(self, earlier):
        second = after(self.second_down, *earlier)
        self.down_hub = lax.ppermute(second, "rep", ACROSS)

    def down_here(self, earlier):
        down_hub, down_first = lax.optimization_barrier(
            (self.down_hub, self.down_first, *earlier)
        )[:2]
        down_in = jnp.where(self.near, self.two, down_hub)
        return jnp.where(self.inner, down_in, jnp.where(self.near, self.down_out, down_first))


def on_device(
    tokens,
    assign,
    route_mask,
    match_mask,
    gate_weight,
    up_weight,
    down_weight,
    slow_down,
    momentum,
    slot_cot,
):
    sections = lax.axis_size("section")
    levels = lax.axis_size("rep").bit_length() - 1
    section_here = lax.axis_index("section")
    token_rows = tokens[0, 0]
    expert_ids = assign[0, 0, :, 0]
    capacity = slot_cot.shape[3]
    model_width = token_rows.shape[1]
    masks_here = lax.dynamic_index_in_dim(
        jnp.stack([route_mask, match_mask]), section_here, axis=1, keepdims=False
    )
    own_mask, match = masks_here[0], masks_here[1]
    match_mine = jnp.bitwise_xor(own_mask, match)
    upward = list(range(levels))
    bits = [bit_of(mask, index) for mask in (own_mask, match_mine, match) for index in upward]
    contract = (((1,), (1,)), ((), ()))
    hidden_width = gate_weight.shape[3]

    gate_raw, up_raw, down_raw = gate_weight[0, 0], up_weight[0, 0], down_weight[0, 0]
    slow_float = slow_down[0, 0].astype(jnp.float32)
    down_float = down_raw.astype(jnp.float32)
    static_part = ((0.5 - pull_rate) * slow_float - 0.5 * down_float).astype(jnp.bfloat16)

    selector = slot_table(expert_ids, sections, capacity)
    placed = lax.dot_general(
        selector, token_rows, (((0,), (0,)), ((), ())), preferred_element_type=jnp.float32
    )
    dispatched = placed.astype(jnp.bfloat16).reshape(sections, capacity, model_width)

    line = None
    if levels == 2:
        line = FourInLine(
            gate_raw,
            up_raw,
            stacked(down_raw, hidden_width),
            stacked(lax.optimization_barrier(static_part), hidden_width),
            own_mask,
        )
        bits = line.forward(bits)
        dispatched = after(dispatched, line.quiet)
        line.handed_up((dispatched,))
    arrived = lax.all_to_all(dispatched, "section", split_axis=0, concat_axis=0, tiled=True)
    rows = arrived.reshape(-1, model_width)
    cotangent = slot_cot[0, 0].reshape(-1, model_width)
    if line is not None:
        up_mat = line.handed_gate((rows,))
    else:
        gate_mat, up_mat, down_mat = [
            route(weight, own_mask, upward) for weight in (gate_raw, up_raw, down_raw)
        ]
        static_in = from_partner(static_part, 0)

    up_act = jnp.dot(rows, up_mat, preferred_element_type=jnp.float32)
    if line is not None:
        gate_mat, static_in = line.gate_here((up_act,))
    gate_act = jnp.dot(rows, gate_mat, preferred_element_type=jnp.float32)
    sigmoid_gate = jax.nn.sigmoid(gate_act)
    hidden = (gate_act * sigmoid_gate * up_act).astype(jnp.bfloat16)
    down_grad = lax.dot_general(
        hidden, cotangent, (((0,), (0,)), ((), ())), preferred_element_type=jnp.float32
    ).astype(jnp.bfloat16)

    if line is not None:
        line.swap_down((down_grad,))

    own_bits, mine_bits, match_bits = [
        bits[number * levels : (number + 1) * levels] for number in range(3)
    ]
    lower, top = upward[:-1], levels - 1
    down_grad_in = from_partner(down_grad, 0)
    if line is not None:
        static_in = after(static_in, line.down_first, down_grad)
        static_in = lax.optimization_barrier(side_by_side(static_in))
        down_grad_in = after(down_grad_in, static_in, line.down_hub)
    own_routed, match_routed, static_routed = down_grad, down_grad, static_part
    for index in lower:
        if index == 0:
            own_in, match_in, static_here = down_grad_in, down_grad_in, static_in
        else:
            own_in = from_partner(own_routed, index)
            match_in = from_partner(match_routed, index)
            static_here = from_partner(static_routed, index)
        own_routed = jnp.where(own_bits[index], own_in, own_routed)
        match_routed = jnp.where(mine_bits[index], match_in, match_routed)
        static_routed = jnp.where(match_bits[index], static_here, static_routed)

    def combined(side, static_routed, own_routed, match_routed):
        def pick(bit, value):
            return jnp.where(bit == side, value.astype(jnp.float32), 0.0)

        return pick(match_bits[top], static_routed) + 0.5 * inner_rate * (
            pick(own_bits[top], own_routed) + pick(mine_bits[top], match_routed)
        )

    crossing_out = combined(True, static_routed, own_routed, match_routed).astype(jnp.bfloat16)
    crossing = from_partner(crossing_out, top)
    slow_float = after(slow_down[0, 0], crossing_out).astype(jnp.float32)
    staying = combined(False, static_routed, own_routed, match_routed)
    outer_here = (0.5 + pull_rate) * slow_float - 0.5 * down_float + staying
    pull = outer_rate * (1.0 + moment_rate)
    kept = (
        slow_float
        - pull * outer_here
        - (outer_rate * moment_rate * moment_rate) * momentum[0, 0].astype(jnp.float32)
    )
    kept = after(kept, crossing_out)
    new_slow = (kept - pull * crossing.astype(jnp.float32)).astype(jnp.bfloat16)

    if line is not None:
        down_mat = side_by_side(line.down_here((crossing_out,)))
    hidden_grad = lax.dot_general(
        cotangent, down_mat, contract, preferred_element_type=jnp.float32
    )
    gate_grad = (
        hidden_grad * up_act * sigmoid_gate * (1.0 + gate_act * (1.0 - sigmoid_gate))
    ).astype(jnp.bfloat16)
    up_grad = (hidden_grad * gate_act * sigmoid_gate).astype(jnp.bfloat16)
    slot_grad = (
        lax.dot_general(gate_grad, gate_mat, contract, preferred_element_type=jnp.float32)
        + lax.dot_general(up_grad, up_mat, contract, preferred_element_type=jnp.float32)
    ).astype(jnp.bfloat16)
    slot_grad = slot_grad.reshape(sections, capacity, model_width)
    returned = lax.all_to_all(slot_grad, "section", split_axis=0, concat_axis=0, tiled=True)
    input_grad = jnp.dot(
        selector, returned.reshape(-1, model_width), preferred_element_type=jnp.float32
    ).astype(jnp.bfloat16)
    return (input_grad[None, None], new_slow[None, None])


def solution(mesh):
    in_specs = (
        P("section", "rep", None, None),
        P("section", "rep", None, None),
        P(),
        P(),
        P("section", "rep", None, None),
        P("section", "rep", None, None),
        P("section", "rep", None, None),
        P("section", "rep", None, None),
        P("section", "rep", None, None),
        P("section", "rep", None, None, None),
    )
    out_specs = (P("section", "rep", None, None), P("section", "rep", None, None))
    return jax.shard_map(
        on_device, mesh=mesh, in_specs=in_specs, out_specs=out_specs, check_vma=False
    )
```

```python
import jax
import jax.numpy as jnp
from jax import lax
from jax.sharding import PartitionSpec as P

inner_rate = 0.05
pull_rate = 0.25
moment_rate = 0.9
outer_rate = 0.7

OUTWARD = [(1, 0), (2, 3)]
INWARD = [(0, 1), (3, 2)]
ACROSS = [(1, 2), (2, 1)]


def from_partner(value, distance):
    pairs = [(source, source ^ 2**distance) for source in range(lax.axis_size("rep"))]
    return lax.ppermute(value, "rep", pairs)


def bit_of(mask, index):
    return jnp.bitwise_and(jnp.right_shift(mask, index), 1) == 1


def route(value, mask, bits):
    for index in bits:
        value = jnp.where(bit_of(mask, index), from_partner(value, index), value)
    return value


def after(value, *earlier):
    return lax.optimization_barrier((value, *earlier))[0]


def slot_table(expert_ids, sections, capacity):
    expert_hot = (expert_ids[:, None] == jnp.arange(sections, dtype=jnp.int32)[None, :]).astype(
        jnp.int32
    )
    position = jnp.sum((jnp.cumsum(expert_hot, axis=0) - 1) * expert_hot, axis=1)
    slot_index = expert_ids * capacity + position
    return (
        slot_index[:, None] == jnp.arange(sections * capacity, dtype=jnp.int32)[None, :]
    ).astype(jnp.bfloat16)


def stacked(wide, width):
    return jnp.concatenate(jnp.split(wide, wide.shape[1] // width, axis=1), axis=0)


def side_by_side(tall):
    return jnp.concatenate(jnp.split(tall, tall.shape[0] // tall.shape[1], axis=0), axis=1)


class FourInLine:
    def __init__(self, gate, up, down, static_part, mask):
        replica = lax.axis_index("rep")
        self.inner = (replica == 1) | (replica == 2)
        self.near, self.far = mask == 1, mask == 3
        self.gate, self.up, self.down = gate, up, down
        self.static_part = static_part

    def forward(self, bits):
        self.up_side = lax.ppermute(self.up, "rep", INWARD)
        self.gate_hub = lax.ppermute(self.gate, "rep", ACROSS)
        inner, self.near, self.far, *bits = lax.optimization_barrier(
            (self.inner, self.near, self.far, *bits)
        )
        send = lax.optimization_barrier(jnp.where(inner, self.static_part, self.gate))
        self.one = from_partner(send, 0)
        self.down_hub = lax.ppermute(self.down, "rep", ACROSS)
        side = self.up_side
        first = jnp.where(self.far, side, self.up)
        second = jnp.where(self.far, self.up, side)
        first_in = lax.ppermute(first, "rep", ACROSS)
        self.quiet, self.first_in = first, first_in
        self.gate_edge = lax.ppermute(self.one, "rep", ACROSS)
        self.second = second
        return bits

    def handed_up(self, earlier):
        first_in = after(self.first_in, *earlier)
        send = jnp.where(self.inner, jnp.where(self.near, self.up, first_in), self.down)
        self.two = from_partner(send, 0)
        self.up_hub = lax.ppermute(after(self.second, send), "rep", ACROSS)
        self.later = send

    def handed_gate(self, earlier):
        gate_edge = after(self.gate_edge, self.later, *earlier)
        gate_out = jnp.where(
            self.near, self.gate, jnp.where(self.far, gate_edge, self.gate_hub)
        )
        send = jnp.where(self.inner, gate_out, self.static_part)
        self.three = from_partner(send, 0)
        two = after(self.two, send)
        self.down_edge = lax.ppermute(two, "rep", ACROSS)
        first = two
        gate_in = jnp.where(
            self.near, self.one, jnp.where(self.far, self.gate_hub, self.gate_edge)
        )
        two, up_hub = lax.optimization_barrier((two, self.up_hub, first))[:2]
        up_in = jnp.where(self.near, self.up_side, up_hub)
        self.gate_in = gate_in
        return jnp.where(self.inner, up_in, two)

    def gate_here(self, earlier):
        three = after(self.three, *earlier)
        static_in = jnp.where(self.inner, three, self.one)
        return lax.optimization_barrier(jnp.where(self.inner, self.gate_in, three)), static_in

    def handed_down(self, earlier):
        down_edge = after(self.down_edge, *earlier)
        down_out = jnp.where(
            self.near, self.down, jnp.where(self.far, down_edge, self.down_hub)
        )
        self.four = lax.ppermute(down_out, "rep", OUTWARD)
        return down_out

    def down_here(self, earlier):
        four = after(self.four, *earlier)
        down_in = jnp.where(
            self.near, self.two, jnp.where(self.far, self.down_hub, self.down_edge)
        )
        return jnp.where(self.inner, down_in, four)


def on_device(
    tokens,
    assign,
    route_mask,
    match_mask,
    gate_weight,
    up_weight,
    down_weight,
    slow_down,
    momentum,
    slot_cot,
):
    sections = lax.axis_size("section")
    levels = lax.axis_size("rep").bit_length() - 1
    section_here = lax.axis_index("section")
    token_rows = tokens[0, 0]
    expert_ids = assign[0, 0, :, 0]
    capacity = slot_cot.shape[3]
    model_width = token_rows.shape[1]
    masks_here = lax.dynamic_index_in_dim(
        jnp.stack([route_mask, match_mask]), section_here, axis=1, keepdims=False
    )
    own_mask, match = masks_here[0], masks_here[1]
    match_mine = jnp.bitwise_xor(own_mask, match)
    upward = list(range(levels))
    bits = [bit_of(mask, index) for mask in (own_mask, match_mine, match) for index in upward]
    contract = (((1,), (1,)), ((), ()))
    hidden_width = gate_weight.shape[3]

    gate_raw, up_raw, down_raw = gate_weight[0, 0], up_weight[0, 0], down_weight[0, 0]
    slow_float = slow_down[0, 0].astype(jnp.float32)
    down_float = down_raw.astype(jnp.float32)
    static_part = ((0.5 - pull_rate) * slow_float - 0.5 * down_float).astype(jnp.bfloat16)

    selector = slot_table(expert_ids, sections, capacity)
    placed = lax.dot_general(
        selector, token_rows, (((0,), (0,)), ((), ())), preferred_element_type=jnp.float32
    )
    dispatched = placed.astype(jnp.bfloat16).reshape(sections, capacity, model_width)

    line = None
    if levels == 2:
        line = FourInLine(
            gate_raw,
            up_raw,
            stacked(down_raw, hidden_width),
            stacked(lax.optimization_barrier(static_part), hidden_width),
            own_mask,
        )
        bits = line.forward(bits)
        dispatched, line.gate_hub, line.down_hub = lax.optimization_barrier(
            (dispatched, line.gate_hub, line.down_hub, line.quiet)
        )[:3]
        line.handed_up((dispatched,))
    arrived = lax.all_to_all(dispatched, "section", split_axis=0, concat_axis=0, tiled=True)
    rows = arrived.reshape(-1, model_width)
    cotangent = slot_cot[0, 0].reshape(-1, model_width)
    if line is not None:
        up_mat = line.handed_gate((rows,))
    else:
        gate_mat, up_mat, down_mat = [
            route(weight, own_mask, upward) for weight in (gate_raw, up_raw, down_raw)
        ]
        static_in = from_partner(static_part, 0)

    up_act = jnp.dot(rows, up_mat, preferred_element_type=jnp.float32)
    if line is not None:
        gate_mat, static_in = line.gate_here((up_act,))
        static_in = side_by_side(static_in)
    gate_act = jnp.dot(rows, gate_mat, preferred_element_type=jnp.float32)
    sigmoid_gate = jax.nn.sigmoid(gate_act)
    hidden = (gate_act * sigmoid_gate * up_act).astype(jnp.bfloat16)
    down_grad = lax.dot_general(
        hidden, cotangent, (((0,), (0,)), ((), ())), preferred_element_type=jnp.float32
    ).astype(jnp.bfloat16)

    own_bits, mine_bits, match_bits = [
        bits[number * levels : (number + 1) * levels] for number in range(3)
    ]
    lower, top = upward[:-1], levels - 1
    down_grad_in = from_partner(down_grad, 0)
    if line is not None:
        sent = line.handed_down((down_grad,))
        static_in = after(static_in, sent)
        down_grad_in = after(down_grad_in, static_in)
    own_routed, match_routed, static_routed = down_grad, down_grad, static_part
    for index in lower:
        if index == 0:
            own_in, match_in, static_here = down_grad_in, down_grad_in, static_in
        else:
            own_in = from_partner(own_routed, index)
            match_in = from_partner(match_routed, index)
            static_here = from_partner(static_routed, index)
        own_routed = jnp.where(own_bits[index], own_in, own_routed)
        match_routed = jnp.where(mine_bits[index], match_in, match_routed)
        static_routed = jnp.where(match_bits[index], static_here, static_routed)

    def combined(side, static_routed, own_routed, match_routed):
        def pick(bit, value):
            return jnp.where(bit == side, value.astype(jnp.float32), 0.0)

        return pick(match_bits[top], static_routed) + 0.5 * inner_rate * (
            pick(own_bits[top], own_routed) + pick(mine_bits[top], match_routed)
        )

    crossing_out = combined(True, static_routed, own_routed, match_routed).astype(jnp.bfloat16)
    crossing = from_partner(crossing_out, top)
    slow_float = after(slow_down[0, 0], crossing_out).astype(jnp.float32)
    staying = combined(False, static_routed, own_routed, match_routed)
    outer_here = (0.5 + pull_rate) * slow_float - 0.5 * down_float + staying
    pull = outer_rate * (1.0 + moment_rate)
    kept = (
        slow_float
        - pull * outer_here
        - (outer_rate * moment_rate * moment_rate) * momentum[0, 0].astype(jnp.float32)
    )
    kept = after(kept, crossing_out)
    new_slow = (kept - pull * crossing.astype(jnp.float32)).astype(jnp.bfloat16)

    if line is not None:
        down_mat = side_by_side(line.down_here((crossing_out,)))
    hidden_grad = lax.dot_general(
        cotangent, down_mat, contract, preferred_element_type=jnp.float32
    )
    gate_grad = (
        hidden_grad * up_act * sigmoid_gate * (1.0 + gate_act * (1.0 - sigmoid_gate))
    ).astype(jnp.bfloat16)
    up_grad = (hidden_grad * gate_act * sigmoid_gate).astype(jnp.bfloat16)
    slot_grad = (
        lax.dot_general(gate_grad, gate_mat, contract, preferred_element_type=jnp.float32)
        + lax.dot_general(up_grad, up_mat, contract, preferred_element_type=jnp.float32)
    ).astype(jnp.bfloat16)
    slot_grad = slot_grad.reshape(sections, capacity, model_width)
    returned = lax.all_to_all(slot_grad, "section", split_axis=0, concat_axis=0, tiled=True)
    input_grad = jnp.dot(
        selector, returned.reshape(-1, model_width), preferred_element_type=jnp.float32
    ).astype(jnp.bfloat16)
    return (input_grad[None, None], new_slow[None, None])


def solution(mesh):
    in_specs = (
        P("section", "rep", None, None),
        P("section", "rep", None, None),
        P(),
        P(),
        P("section", "rep", None, None),
        P("section", "rep", None, None),
        P("section", "rep", None, None),
        P("section", "rep", None, None),
        P("section", "rep", None, None),
        P("section", "rep", None, None, None),
    )
    out_specs = (P("section", "rep", None, None), P("section", "rep", None, None))
    return jax.shard_map(
        on_device, mesh=mesh, in_specs=in_specs, out_specs=out_specs, check_vma=False
    )
```

```python
import jax
import jax.numpy as jnp
from jax import lax
from jax.sharding import PartitionSpec as P

inner_rate = 0.05
pull_rate = 0.25
moment_rate = 0.9
outer_rate = 0.7

OUTWARD = [(1, 0), (2, 3)]
INWARD = [(0, 1), (3, 2)]
ACROSS = [(1, 2), (2, 1)]


def from_partner(value, distance):
    pairs = [(source, source ^ 2**distance) for source in range(lax.axis_size("rep"))]
    return lax.ppermute(value, "rep", pairs)


def bit_of(mask, index):
    return jnp.bitwise_and(jnp.right_shift(mask, index), 1) == 1


def route(value, mask, bits):
    for index in bits:
        value = jnp.where(bit_of(mask, index), from_partner(value, index), value)
    return value


def after(value, *earlier):
    return lax.optimization_barrier((value, *earlier))[0]


def slot_table(expert_ids, sections, capacity):
    expert_hot = (expert_ids[:, None] == jnp.arange(sections, dtype=jnp.int32)[None, :]).astype(
        jnp.int32
    )
    position = jnp.sum((jnp.cumsum(expert_hot, axis=0) - 1) * expert_hot, axis=1)
    slot_index = expert_ids * capacity + position
    return (
        slot_index[:, None] == jnp.arange(sections * capacity, dtype=jnp.int32)[None, :]
    ).astype(jnp.bfloat16)


def stacked(wide, width):
    return jnp.concatenate(jnp.split(wide, wide.shape[1] // width, axis=1), axis=0)


def side_by_side(tall):
    return jnp.concatenate(jnp.split(tall, tall.shape[0] // tall.shape[1], axis=0), axis=1)


class FourInLine:
    def __init__(self, gate, up, down, static_part, mask):
        replica = lax.axis_index("rep")
        self.inner = (replica == 1) | (replica == 2)
        self.near, self.far = mask == 1, mask == 3
        self.gate, self.up, self.down = gate, up, down
        self.static_part = static_part

    def forward(self, bits):
        self.up_side = lax.ppermute(self.up, "rep", INWARD)
        self.gate_hub = lax.ppermute(self.gate, "rep", ACROSS)
        inner, self.near, self.far, *bits = lax.optimization_barrier(
            (self.inner, self.near, self.far, *bits)
        )
        send = lax.optimization_barrier(jnp.where(inner, self.static_part, self.gate))
        self.one = from_partner(send, 0)
        side, self.gate_hub, self.near, self.far = lax.optimization_barrier(
            (self.up_side, self.gate_hub, self.near, self.far)
        )
        first = jnp.where(self.far, side, self.up)
        second = jnp.where(self.far, self.up, side)
        first_in = lax.ppermute(first, "rep", ACROSS)
        self.quiet, self.first_in = first, first_in
        self.gate_edge = lax.ppermute(self.one, "rep", ACROSS)
        self.second = second
        return bits

    def handed_up(self, earlier):
        first_in = after(self.first_in, *earlier)
        send = jnp.where(self.inner, jnp.where(self.near, self.up, first_in), self.down)
        self.two = from_partner(send, 0)
        self.up_hub = lax.ppermute(after(self.second, send), "rep", ACROSS)
        self.later = send

    def handed_gate(self, earlier):
        gate_edge = after(self.gate_edge, self.later, *earlier)
        gate_out = jnp.where(
            self.near, self.gate, jnp.where(self.far, gate_edge, self.gate_hub)
        )
        send = jnp.where(self.inner, gate_out, self.static_part)
        self.three = from_partner(send, 0)
        two = after(self.two, send)
        first = jnp.where(self.far, two, self.down)
        second = jnp.where(self.far, self.down, two)
        self.down_first = lax.ppermute(first, "rep", ACROSS)
        gate_in = jnp.where(
            self.near, self.one, jnp.where(self.far, self.gate_hub, self.gate_edge)
        )
        two, up_hub = lax.optimization_barrier((two, self.up_hub, first))[:2]
        self.second_down = second
        up_in = jnp.where(self.near, self.up_side, up_hub)
        self.gate_in = gate_in
        return jnp.where(self.inner, up_in, two)

    def gate_here(self, earlier):
        three = after(self.three, *earlier)
        static_in = jnp.where(self.inner, three, self.one)
        return lax.optimization_barrier(jnp.where(self.inner, self.gate_in, three)), static_in

    def swap_down(self, earlier):
        second = after(self.second_down, *earlier)
        self.down_hub = lax.ppermute(second, "rep", ACROSS)

    def handed_down(self, earlier):
        send = jnp.where(self.near, self.down, after(self.down_first, *earlier))
        self.four = lax.ppermute(send, "rep", OUTWARD)
        return send

    def down_here(self, earlier):
        down_hub = after(self.down_hub, *earlier)
        down_in = jnp.where(self.near, self.two, down_hub)
        return jnp.where(self.inner, down_in, self.four)


def on_device(
    tokens,
    assign,
    route_mask,
    match_mask,
    gate_weight,
    up_weight,
    down_weight,
    slow_down,
    momentum,
    slot_cot,
):
    sections = lax.axis_size("section")
    levels = lax.axis_size("rep").bit_length() - 1
    section_here = lax.axis_index("section")
    token_rows = tokens[0, 0]
    expert_ids = assign[0, 0, :, 0]
    capacity = slot_cot.shape[3]
    model_width = token_rows.shape[1]
    masks_here = lax.dynamic_index_in_dim(
        jnp.stack([route_mask, match_mask]), section_here, axis=1, keepdims=False
    )
    own_mask, match = masks_here[0], masks_here[1]
    match_mine = jnp.bitwise_xor(own_mask, match)
    upward = list(range(levels))
    bits = [bit_of(mask, index) for mask in (own_mask, match_mine, match) for index in upward]
    contract = (((1,), (1,)), ((), ()))
    hidden_width = gate_weight.shape[3]

    gate_raw, up_raw, down_raw = gate_weight[0, 0], up_weight[0, 0], down_weight[0, 0]
    slow_float = slow_down[0, 0].astype(jnp.float32)
    down_float = down_raw.astype(jnp.float32)
    static_part = ((0.5 - pull_rate) * slow_float - 0.5 * down_float).astype(jnp.bfloat16)

    selector = slot_table(expert_ids, sections, capacity)
    placed = lax.dot_general(
        selector, token_rows, (((0,), (0,)), ((), ())), preferred_element_type=jnp.float32
    )
    dispatched = placed.astype(jnp.bfloat16).reshape(sections, capacity, model_width)

    line = None
    if levels == 2:
        line = FourInLine(
            gate_raw,
            up_raw,
            stacked(down_raw, hidden_width),
            stacked(lax.optimization_barrier(static_part), hidden_width),
            own_mask,
        )
        bits = line.forward(bits)
        dispatched = after(dispatched, line.quiet)
        line.handed_up((dispatched,))
    arrived = lax.all_to_all(dispatched, "section", split_axis=0, concat_axis=0, tiled=True)
    rows = arrived.reshape(-1, model_width)
    cotangent = slot_cot[0, 0].reshape(-1, model_width)
    if line is not None:
        up_mat = line.handed_gate((rows,))
    else:
        gate_mat, up_mat, down_mat = [
            route(weight, own_mask, upward) for weight in (gate_raw, up_raw, down_raw)
        ]
        static_in = from_partner(static_part, 0)

    up_act = jnp.dot(rows, up_mat, preferred_element_type=jnp.float32)
    if line is not None:
        gate_mat, static_in = line.gate_here((up_act,))
    gate_act = jnp.dot(rows, gate_mat, preferred_element_type=jnp.float32)
    sigmoid_gate = jax.nn.sigmoid(gate_act)
    hidden = (gate_act * sigmoid_gate * up_act).astype(jnp.bfloat16)
    down_grad = lax.dot_general(
        hidden, cotangent, (((0,), (0,)), ((), ())), preferred_element_type=jnp.float32
    ).astype(jnp.bfloat16)

    if line is not None:
        line.swap_down((down_grad,))

    own_bits, mine_bits, match_bits = [
        bits[number * levels : (number + 1) * levels] for number in range(3)
    ]
    lower, top = upward[:-1], levels - 1
    down_grad_in = from_partner(down_grad, 0)
    if line is not None:
        static_in = after(static_in, line.down_first, down_grad)
        static_in = lax.optimization_barrier(side_by_side(static_in))
        sent = line.handed_down((down_grad_in, static_in))
        down_grad_in = after(down_grad_in, sent)
    own_routed, match_routed, static_routed = down_grad, down_grad, static_part
    for index in lower:
        if index == 0:
            own_in, match_in, static_here = down_grad_in, down_grad_in, static_in
        else:
            own_in = from_partner(own_routed, index)
            match_in = from_partner(match_routed, index)
            static_here = from_partner(static_routed, index)
        own_routed = jnp.where(own_bits[index], own_in, own_routed)
        match_routed = jnp.where(mine_bits[index], match_in, match_routed)
        static_routed = jnp.where(match_bits[index], static_here, static_routed)

    def combined(side, static_routed, own_routed, match_routed):
        def pick(bit, value):
            return jnp.where(bit == side, value.astype(jnp.float32), 0.0)

        return pick(match_bits[top], static_routed) + 0.5 * inner_rate * (
            pick(own_bits[top], own_routed) + pick(mine_bits[top], match_routed)
        )

    crossing_out = combined(True, static_routed, own_routed, match_routed).astype(jnp.bfloat16)
    if line is not None:
        crossing_out = after(crossing_out, line.down_hub)
    crossing = from_partner(crossing_out, top)
    slow_float = after(slow_down[0, 0], crossing_out).astype(jnp.float32)
    staying = combined(False, static_routed, own_routed, match_routed)
    outer_here = (0.5 + pull_rate) * slow_float - 0.5 * down_float + staying
    pull = outer_rate * (1.0 + moment_rate)
    kept = (
        slow_float
        - pull * outer_here
        - (outer_rate * moment_rate * moment_rate) * momentum[0, 0].astype(jnp.float32)
    )
    kept = after(kept, crossing_out)
    new_slow = (kept - pull * crossing.astype(jnp.float32)).astype(jnp.bfloat16)

    if line is not None:
        down_mat = side_by_side(line.down_here((crossing_out,)))
    hidden_grad = lax.dot_general(
        cotangent, down_mat, contract, preferred_element_type=jnp.float32
    )
    gate_grad = (
        hidden_grad * up_act * sigmoid_gate * (1.0 + gate_act * (1.0 - sigmoid_gate))
    ).astype(jnp.bfloat16)
    up_grad = (hidden_grad * gate_act * sigmoid_gate).astype(jnp.bfloat16)
    slot_grad = (
        lax.dot_general(gate_grad, gate_mat, contract, preferred_element_type=jnp.float32)
        + lax.dot_general(up_grad, up_mat, contract, preferred_element_type=jnp.float32)
    ).astype(jnp.bfloat16)
    slot_grad = slot_grad.reshape(sections, capacity, model_width)
    returned = lax.all_to_all(slot_grad, "section", split_axis=0, concat_axis=0, tiled=True)
    input_grad = jnp.dot(
        selector, returned.reshape(-1, model_width), preferred_element_type=jnp.float32
    ).astype(jnp.bfloat16)
    return (input_grad[None, None], new_slow[None, None])


def solution(mesh):
    in_specs = (
        P("section", "rep", None, None),
        P("section", "rep", None, None),
        P(),
        P(),
        P("section", "rep", None, None),
        P("section", "rep", None, None),
        P("section", "rep", None, None),
        P("section", "rep", None, None),
        P("section", "rep", None, None),
        P("section", "rep", None, None, None),
    )
    out_specs = (P("section", "rep", None, None), P("section", "rep", None, None))
    return jax.shard_map(
        on_device, mesh=mesh, in_specs=in_specs, out_specs=out_specs, check_vma=False
    )
```

```python
import jax
import jax.numpy as jnp
from jax import lax
from jax.sharding import PartitionSpec as P

inner_rate = 0.05
pull_rate = 0.25
moment_rate = 0.9
outer_rate = 0.7

OUTWARD = [(1, 0), (2, 3)]
INWARD = [(0, 1), (3, 2)]
ACROSS = [(1, 2), (2, 1)]


def from_partner(value, distance):
    pairs = [(source, source ^ 2**distance) for source in range(lax.axis_size("rep"))]
    return lax.ppermute(value, "rep", pairs)


def bit_of(mask, index):
    return jnp.bitwise_and(jnp.right_shift(mask, index), 1) == 1


def route(value, mask, bits):
    for index in bits:
        value = jnp.where(bit_of(mask, index), from_partner(value, index), value)
    return value


def after(value, *earlier):
    return lax.optimization_barrier((value, *earlier))[0]


def after_all(values, *earlier):
    return lax.optimization_barrier((*values, *earlier))[: len(values)]


def slot_table(expert_ids, sections, capacity):
    expert_hot = (expert_ids[:, None] == jnp.arange(sections, dtype=jnp.int32)[None, :]).astype(
        jnp.int32
    )
    position = jnp.sum((jnp.cumsum(expert_hot, axis=0) - 1) * expert_hot, axis=1)
    slot_index = expert_ids * capacity + position
    return (
        slot_index[:, None] == jnp.arange(sections * capacity, dtype=jnp.int32)[None, :]
    ).astype(jnp.bfloat16)


def stacked(wide, width):
    return jnp.concatenate(jnp.split(wide, wide.shape[1] // width, axis=1), axis=0)


def side_by_side(tall):
    return jnp.concatenate(jnp.split(tall, tall.shape[0] // tall.shape[1], axis=0), axis=1)


class FourInLine:
    def __init__(self, gate, up, down, static_part, mask):
        replica = lax.axis_index("rep")
        self.inner = (replica == 1) | (replica == 2)
        self.near, self.far = mask == 1, mask == 3
        self.gate, self.up, self.down = gate, up, down
        self.static_part = static_part

    def forward(self, bits):
        middle = self.up.shape[0] // 2
        halves = [lax.optimization_barrier(self.up[:middle])]
        sides, self.up_first, firsts = [], [], []
        sides.append(lax.ppermute(halves[0], "rep", INWARD))
        self.gate_hub = lax.ppermute(self.gate, "rep", ACROSS)
        inner, self.near, self.far, *bits = lax.optimization_barrier(
            (self.inner, self.near, self.far, *bits)
        )
        halves.append(after(self.up, self.far)[middle:])
        sides.append(lax.ppermute(halves[1], "rep", INWARD))
        send = lax.optimization_barrier(jnp.where(inner, self.static_part, self.gate))
        self.one = from_partner(send, 0)
        sides[0], self.gate_hub = lax.optimization_barrier((sides[0], self.gate_hub))
        for half, side in zip(halves, sides):
            side = after(side, *firsts)
            firsts.append(lax.optimization_barrier(jnp.where(self.far, side, half)))
            self.up_first.append(lax.ppermute(firsts[-1], "rep", ACROSS))
        self.up_side = jnp.concatenate([after(side, firsts[1]) for side in sides], axis=0)
        self.up_side = lax.optimization_barrier(self.up_side)
        self.second = jnp.where(self.far, self.up, self.up_side)
        self.quiet = firsts[1]
        return bits

    def settle(self, dispatched):
        dispatched, self.up_first[0] = lax.optimization_barrier(
            (dispatched, self.up_first[0], self.quiet)
        )[:2]
        return dispatched

    def handed_up(self, earlier):
        *first_in, self.one = after_all([*self.up_first, self.one], *earlier)
        self.gate_edge = lax.ppermute(self.one, "rep", ACROSS)
        first_in = jnp.concatenate(first_in, axis=0)
        send = jnp.where(self.inner, jnp.where(self.near, self.up, first_in), self.down)
        self.two = from_partner(send, 0)
        self.up_hub = lax.ppermute(after(self.second, send), "rep", ACROSS)
        self.later = send

    def handed_gate(self, earlier):
        gate_edge = after(self.gate_edge, self.later, *earlier)
        gate_out = jnp.where(
            self.near, self.gate, jnp.where(self.far, gate_edge, self.gate_hub)
        )
        send = jnp.where(self.inner, gate_out, self.static_part)
        self.three = from_partner(send, 0)
        two = after(self.two, send)
        first = jnp.where(self.far, two, self.down)
        second = jnp.where(self.far, self.down, two)
        self.down_first = lax.ppermute(first, "rep", ACROSS)
        gate_in = jnp.where(
            self.near, self.one, jnp.where(self.far, self.gate_hub, self.gate_edge)
        )
        two, up_hub = lax.optimization_barrier((two, self.up_hub, first))[:2]
        self.second_down = second
        up_in = jnp.where(self.near, self.up_side, up_hub)
        self.gate_in = gate_in
        return jnp.where(self.inner, up_in, two)

    def gate_here(self, earlier):
        three = after(self.three, *earlier)
        static_in = jnp.where(self.inner, three, self.one)
        return lax.optimization_barrier(jnp.where(self.inner, self.gate_in, three)), static_in

    def swap_down(self, earlier):
        second = after(self.second_down, *earlier)
        self.down_hub = lax.ppermute(second, "rep", ACROSS)

    def handed_down(self, earlier):
        send = jnp.where(self.near, self.down, after(self.down_first, *earlier))
        self.four = lax.ppermute(send, "rep", OUTWARD)
        return send

    def down_here(self, earlier):
        down_hub = after(self.down_hub, *earlier)
        down_in = jnp.where(self.near, self.two, down_hub)
        return jnp.where(self.inner, down_in, self.four)


def on_device(
    tokens,
    assign,
    route_mask,
    match_mask,
    gate_weight,
    up_weight,
    down_weight,
    slow_down,
    momentum,
    slot_cot,
):
    sections = lax.axis_size("section")
    levels = lax.axis_size("rep").bit_length() - 1
    section_here = lax.axis_index("section")
    token_rows = tokens[0, 0]
    expert_ids = assign[0, 0, :, 0]
    capacity = slot_cot.shape[3]
    model_width = token_rows.shape[1]
    masks_here = lax.dynamic_index_in_dim(
        jnp.stack([route_mask, match_mask]), section_here, axis=1, keepdims=False
    )
    own_mask, match = masks_here[0], masks_here[1]
    match_mine = jnp.bitwise_xor(own_mask, match)
    upward = list(range(levels))
    bits = [bit_of(mask, index) for mask in (own_mask, match_mine, match) for index in upward]
    contract = (((1,), (1,)), ((), ()))
    hidden_width = gate_weight.shape[3]

    gate_raw, up_raw, down_raw = gate_weight[0, 0], up_weight[0, 0], down_weight[0, 0]
    slow_float = slow_down[0, 0].astype(jnp.float32)
    down_float = down_raw.astype(jnp.float32)
    static_part = ((0.5 - pull_rate) * slow_float - 0.5 * down_float).astype(jnp.bfloat16)

    selector = slot_table(expert_ids, sections, capacity)
    placed = lax.dot_general(
        selector, token_rows, (((0,), (0,)), ((), ())), preferred_element_type=jnp.float32
    )
    dispatched = placed.astype(jnp.bfloat16).reshape(sections, capacity, model_width)

    line = None
    if levels == 2:
        line = FourInLine(
            gate_raw,
            up_raw,
            stacked(down_raw, hidden_width),
            stacked(lax.optimization_barrier(static_part), hidden_width),
            own_mask,
        )
        bits = line.forward(bits)
        dispatched = line.settle(dispatched)
        line.handed_up((dispatched,))
    arrived = lax.all_to_all(dispatched, "section", split_axis=0, concat_axis=0, tiled=True)
    rows = arrived.reshape(-1, model_width)
    cotangent = slot_cot[0, 0].reshape(-1, model_width)
    if line is not None:
        up_mat = line.handed_gate((rows,))
    else:
        gate_mat, up_mat, down_mat = [
            route(weight, own_mask, upward) for weight in (gate_raw, up_raw, down_raw)
        ]
        static_in = from_partner(static_part, 0)

    up_act = jnp.dot(rows, up_mat, preferred_element_type=jnp.float32)
    if line is not None:
        gate_mat, static_in = line.gate_here((up_act,))
    gate_act = jnp.dot(rows, gate_mat, preferred_element_type=jnp.float32)
    sigmoid_gate = jax.nn.sigmoid(gate_act)
    hidden = (gate_act * sigmoid_gate * up_act).astype(jnp.bfloat16)
    down_grad = lax.dot_general(
        hidden, cotangent, (((0,), (0,)), ((), ())), preferred_element_type=jnp.float32
    ).astype(jnp.bfloat16)

    if line is not None:
        line.swap_down((down_grad,))

    own_bits, mine_bits, match_bits = [
        bits[number * levels : (number + 1) * levels] for number in range(3)
    ]
    lower, top = upward[:-1], levels - 1
    down_grad_in = from_partner(down_grad, 0)
    if line is not None:
        static_in = after(static_in, line.down_first, down_grad)
        static_in = lax.optimization_barrier(side_by_side(static_in))
        sent = line.handed_down((down_grad_in, static_in))
        down_grad_in = after(down_grad_in, sent)
    own_routed, match_routed, static_routed = down_grad, down_grad, static_part
    for index in lower:
        if index == 0:
            own_in, match_in, static_here = down_grad_in, down_grad_in, static_in
        else:
            own_in = from_partner(own_routed, index)
            match_in = from_partner(match_routed, index)
            static_here = from_partner(static_routed, index)
        own_routed = jnp.where(own_bits[index], own_in, own_routed)
        match_routed = jnp.where(mine_bits[index], match_in, match_routed)
        static_routed = jnp.where(match_bits[index], static_here, static_routed)

    def combined(side, static_routed, own_routed, match_routed):
        def pick(bit, value):
            return jnp.where(bit == side, value.astype(jnp.float32), 0.0)

        return pick(match_bits[top], static_routed) + 0.5 * inner_rate * (
            pick(own_bits[top], own_routed) + pick(mine_bits[top], match_routed)
        )

    crossing_out = combined(True, static_routed, own_routed, match_routed).astype(jnp.bfloat16)
    if line is not None:
        crossing_out = after(crossing_out, line.down_hub)
    crossing = from_partner(crossing_out, top)
    slow_float = after(slow_down[0, 0], crossing_out).astype(jnp.float32)
    staying = combined(False, static_routed, own_routed, match_routed)
    outer_here = (0.5 + pull_rate) * slow_float - 0.5 * down_float + staying
    pull = outer_rate * (1.0 + moment_rate)
    kept = (
        slow_float
        - pull * outer_here
        - (outer_rate * moment_rate * moment_rate) * momentum[0, 0].astype(jnp.float32)
    )
    kept = after(kept, crossing_out)
    new_slow = (kept - pull * crossing.astype(jnp.float32)).astype(jnp.bfloat16)

    if line is not None:
        down_mat = side_by_side(line.down_here((crossing_out,)))
    hidden_grad = lax.dot_general(
        cotangent, down_mat, contract, preferred_element_type=jnp.float32
    )
    gate_grad = (
        hidden_grad * up_act * sigmoid_gate * (1.0 + gate_act * (1.0 - sigmoid_gate))
    ).astype(jnp.bfloat16)
    up_grad = (hidden_grad * gate_act * sigmoid_gate).astype(jnp.bfloat16)
    slot_grad = (
        lax.dot_general(gate_grad, gate_mat, contract, preferred_element_type=jnp.float32)
        + lax.dot_general(up_grad, up_mat, contract, preferred_element_type=jnp.float32)
    ).astype(jnp.bfloat16)
    slot_grad = slot_grad.reshape(sections, capacity, model_width)
    returned = lax.all_to_all(slot_grad, "section", split_axis=0, concat_axis=0, tiled=True)
    input_grad = jnp.dot(
        selector, returned.reshape(-1, model_width), preferred_element_type=jnp.float32
    ).astype(jnp.bfloat16)
    return (input_grad[None, None], new_slow[None, None])


def solution(mesh):
    in_specs = (
        P("section", "rep", None, None),
        P("section", "rep", None, None),
        P(),
        P(),
        P("section", "rep", None, None),
        P("section", "rep", None, None),
        P("section", "rep", None, None),
        P("section", "rep", None, None),
        P("section", "rep", None, None),
        P("section", "rep", None, None, None),
    )
    out_specs = (P("section", "rep", None, None), P("section", "rep", None, None))
    return jax.shard_map(
        on_device, mesh=mesh, in_specs=in_specs, out_specs=out_specs, check_vma=False
    )
```

```python
import jax
import jax.numpy as jnp
from jax import lax
from jax.sharding import PartitionSpec as P

inner_rate = 0.05
pull_rate = 0.25
moment_rate = 0.9
outer_rate = 0.7

OUTWARD = [(1, 0), (2, 3)]
INWARD = [(0, 1), (3, 2)]
ACROSS = [(1, 2), (2, 1)]


def from_partner(value, distance):
    pairs = [(source, source ^ 2**distance) for source in range(lax.axis_size("rep"))]
    return lax.ppermute(value, "rep", pairs)


def bit_of(mask, index):
    return jnp.bitwise_and(jnp.right_shift(mask, index), 1) == 1


def route(value, mask, bits):
    for index in bits:
        value = jnp.where(bit_of(mask, index), from_partner(value, index), value)
    return value


def after(value, *earlier):
    return lax.optimization_barrier((value, *earlier))[0]


def after_all(values, *earlier):
    return lax.optimization_barrier((*values, *earlier))[: len(values)]


def slot_table(expert_ids, sections, capacity):
    expert_hot = (expert_ids[:, None] == jnp.arange(sections, dtype=jnp.int32)[None, :]).astype(
        jnp.int32
    )
    position = jnp.sum((jnp.cumsum(expert_hot, axis=0) - 1) * expert_hot, axis=1)
    slot_index = expert_ids * capacity + position
    return (
        slot_index[:, None] == jnp.arange(sections * capacity, dtype=jnp.int32)[None, :]
    ).astype(jnp.bfloat16)


def stacked(wide, width):
    return jnp.concatenate(jnp.split(wide, wide.shape[1] // width, axis=1), axis=0)


def side_by_side(tall):
    return jnp.concatenate(jnp.split(tall, tall.shape[0] // tall.shape[1], axis=0), axis=1)


class FourInLine:
    def __init__(self, gate, up, down, static_part, mask):
        replica = lax.axis_index("rep")
        self.inner = (replica == 1) | (replica == 2)
        self.near, self.far = mask == 1, mask == 3
        self.gate, self.up, self.down = gate, up, down
        self.static_part = static_part

    def forward(self, bits):
        self.up_side = lax.ppermute(self.up, "rep", INWARD)
        self.gate_hub = lax.ppermute(self.gate, "rep", ACROSS)
        inner, self.near, self.far, *bits = lax.optimization_barrier(
            (self.inner, self.near, self.far, *bits)
        )
        send = lax.optimization_barrier(jnp.where(inner, self.static_part, self.gate))
        self.one = from_partner(send, 0)
        side, self.gate_hub, self.near, self.far = lax.optimization_barrier(
            (self.up_side, self.gate_hub, self.near, self.far)
        )
        first = jnp.where(self.far, side, self.up)
        second = jnp.where(self.far, self.up, side)
        first_in = lax.ppermute(first, "rep", ACROSS)
        self.quiet, self.first_in = first, first_in
        self.gate_edge = lax.ppermute(self.one, "rep", ACROSS)
        self.second = second
        return bits

    def settle(self, dispatched):
        base = lax.optimization_barrier(jnp.where(self.inner, self.up, self.down))
        dispatched, self.up_base = lax.optimization_barrier((dispatched, base, self.quiet))[:2]
        return dispatched

    def handed_up(self, earlier):
        first_in = after(self.first_in, *earlier)
        send = jnp.where(self.inner & ~self.near, first_in, self.up_base)
        self.two = from_partner(send, 0)
        self.up_hub = lax.ppermute(after(self.second, send), "rep", ACROSS)
        self.later = send

    def handed_gate(self, earlier):
        gate, static_part, gate_hub = after_all(
            (self.gate, self.static_part, self.gate_hub), self.later
        )
        base = jnp.where(self.inner, jnp.where(self.near, gate, gate_hub), static_part)
        base = lax.optimization_barrier(base)
        gate_edge = after(self.gate_edge, self.later, base, *earlier)
        send = jnp.where(self.inner & self.far, gate_edge, base)
        self.three = from_partner(send, 0)
        two = after(self.two, send)
        first = jnp.where(self.far, two, self.down)
        second = jnp.where(self.far, self.down, two)
        self.down_first = lax.ppermute(first, "rep", ACROSS)
        gate_in = jnp.where(
            self.near, self.one, jnp.where(self.far, self.gate_hub, self.gate_edge)
        )
        two, up_hub = lax.optimization_barrier((two, self.up_hub, first))[:2]
        self.second_down = second
        up_in = jnp.where(self.near, self.up_side, up_hub)
        self.gate_in = lax.optimization_barrier(gate_in)
        return jnp.where(self.inner, up_in, two)

    def gate_here(self, earlier):
        three, gate_in = lax.optimization_barrier((self.three, self.gate_in, *earlier))[:2]
        gate_here = lax.optimization_barrier(jnp.where(self.inner, gate_in, three))
        return gate_here, jnp.where(self.inner, after(three, gate_here), self.one)

    def swap_down(self, earlier):
        second = after(self.second_down, *earlier)
        self.down_hub = lax.ppermute(second, "rep", ACROSS)

    def handed_down(self, earlier):
        send = jnp.where(self.near, self.down, after(self.down_first, *earlier))
        self.four = lax.ppermute(send, "rep", OUTWARD)
        return send

    def down_here(self, earlier):
        down_hub = after(self.down_hub, *earlier)
        down_in = jnp.where(self.near, self.two, down_hub)
        return jnp.where(self.inner, down_in, self.four)


def on_device(
    tokens,
    assign,
    route_mask,
    match_mask,
    gate_weight,
    up_weight,
    down_weight,
    slow_down,
    momentum,
    slot_cot,
):
    sections = lax.axis_size("section")
    levels = lax.axis_size("rep").bit_length() - 1
    section_here = lax.axis_index("section")
    token_rows = tokens[0, 0]
    expert_ids = assign[0, 0, :, 0]
    capacity = slot_cot.shape[3]
    model_width = token_rows.shape[1]
    masks_here = lax.dynamic_index_in_dim(
        jnp.stack([route_mask, match_mask]), section_here, axis=1, keepdims=False
    )
    own_mask, match = masks_here[0], masks_here[1]
    match_mine = jnp.bitwise_xor(own_mask, match)
    upward = list(range(levels))
    bits = [bit_of(mask, index) for mask in (own_mask, match_mine, match) for index in upward]
    contract = (((1,), (1,)), ((), ()))
    hidden_width = gate_weight.shape[3]

    gate_raw, up_raw, down_raw = gate_weight[0, 0], up_weight[0, 0], down_weight[0, 0]
    slow_float = slow_down[0, 0].astype(jnp.float32)
    down_float = down_raw.astype(jnp.float32)
    static_part = ((0.5 - pull_rate) * slow_float - 0.5 * down_float).astype(jnp.bfloat16)

    selector = slot_table(expert_ids, sections, capacity)
    placed = lax.dot_general(
        selector, token_rows, (((0,), (0,)), ((), ())), preferred_element_type=jnp.float32
    )
    dispatched = placed.astype(jnp.bfloat16).reshape(sections, capacity, model_width)

    line = None
    if levels == 2:
        line = FourInLine(
            gate_raw,
            up_raw,
            stacked(down_raw, hidden_width),
            stacked(lax.optimization_barrier(static_part), hidden_width),
            own_mask,
        )
        bits = line.forward(bits)
        dispatched = line.settle(dispatched)
        line.handed_up((dispatched,))
    arrived = lax.all_to_all(dispatched, "section", split_axis=0, concat_axis=0, tiled=True)
    rows = arrived.reshape(-1, model_width)
    cotangent = slot_cot[0, 0].reshape(-1, model_width)
    if line is not None:
        up_mat = line.handed_gate((rows,))
    else:
        gate_mat, up_mat, down_mat = [
            route(weight, own_mask, upward) for weight in (gate_raw, up_raw, down_raw)
        ]
        static_in = from_partner(static_part, 0)

    up_act = jnp.dot(rows, up_mat, preferred_element_type=jnp.float32)
    if line is not None:
        gate_mat, static_in = line.gate_here((up_act,))
    gate_act = jnp.dot(rows, gate_mat, preferred_element_type=jnp.float32)
    sigmoid_gate = jax.nn.sigmoid(gate_act)
    hidden = (gate_act * sigmoid_gate * up_act).astype(jnp.bfloat16)
    down_grad = lax.dot_general(
        hidden, cotangent, (((0,), (0,)), ((), ())), preferred_element_type=jnp.float32
    ).astype(jnp.bfloat16)

    if line is not None:
        line.swap_down((down_grad,))

    own_bits, mine_bits, match_bits = [
        bits[number * levels : (number + 1) * levels] for number in range(3)
    ]
    lower, top = upward[:-1], levels - 1
    down_grad_in = from_partner(down_grad, 0)
    if line is not None:
        static_in = after(static_in, line.down_first, down_grad)
        static_in = lax.optimization_barrier(side_by_side(static_in))
        sent = line.handed_down((down_grad_in, static_in))
        down_grad_in = after(down_grad_in, sent)
    own_routed, match_routed, static_routed = down_grad, down_grad, static_part
    for index in lower:
        if index == 0:
            own_in, match_in, static_here = down_grad_in, down_grad_in, static_in
        else:
            own_in = from_partner(own_routed, index)
            match_in = from_partner(match_routed, index)
            static_here = from_partner(static_routed, index)
        own_routed = jnp.where(own_bits[index], own_in, own_routed)
        match_routed = jnp.where(mine_bits[index], match_in, match_routed)
        static_routed = jnp.where(match_bits[index], static_here, static_routed)

    def combined(side, static_routed, own_routed, match_routed):
        def pick(bit, value):
            return jnp.where(bit == side, value.astype(jnp.float32), 0.0)

        return pick(match_bits[top], static_routed) + 0.5 * inner_rate * (
            pick(own_bits[top], own_routed) + pick(mine_bits[top], match_routed)
        )

    crossing_out = combined(True, static_routed, own_routed, match_routed).astype(jnp.bfloat16)
    if line is not None:
        crossing_out = after(crossing_out, line.down_hub)
    crossing = from_partner(crossing_out, top)
    slow_float = after(slow_down[0, 0], crossing_out).astype(jnp.float32)
    staying = combined(False, static_routed, own_routed, match_routed)
    outer_here = (0.5 + pull_rate) * slow_float - 0.5 * down_float + staying
    pull = outer_rate * (1.0 + moment_rate)
    kept = (
        slow_float
        - pull * outer_here
        - (outer_rate * moment_rate * moment_rate) * momentum[0, 0].astype(jnp.float32)
    )
    kept = after(kept, crossing_out)
    new_slow = (kept - pull * crossing.astype(jnp.float32)).astype(jnp.bfloat16)

    if line is not None:
        down_mat = side_by_side(line.down_here((crossing_out,)))
    hidden_grad = lax.dot_general(
        cotangent, down_mat, contract, preferred_element_type=jnp.float32
    )
    gate_grad = (
        hidden_grad * up_act * sigmoid_gate * (1.0 + gate_act * (1.0 - sigmoid_gate))
    ).astype(jnp.bfloat16)
    up_grad = (hidden_grad * gate_act * sigmoid_gate).astype(jnp.bfloat16)
    slot_grad = (
        lax.dot_general(gate_grad, gate_mat, contract, preferred_element_type=jnp.float32)
        + lax.dot_general(up_grad, up_mat, contract, preferred_element_type=jnp.float32)
    ).astype(jnp.bfloat16)
    slot_grad = slot_grad.reshape(sections, capacity, model_width)
    returned = lax.all_to_all(slot_grad, "section", split_axis=0, concat_axis=0, tiled=True)
    input_grad = jnp.dot(
        selector, returned.reshape(-1, model_width), preferred_element_type=jnp.float32
    ).astype(jnp.bfloat16)
    return (input_grad[None, None], new_slow[None, None])


def solution(mesh):
    in_specs = (
        P("section", "rep", None, None),
        P("section", "rep", None, None),
        P(),
        P(),
        P("section", "rep", None, None),
        P("section", "rep", None, None),
        P("section", "rep", None, None),
        P("section", "rep", None, None),
        P("section", "rep", None, None),
        P("section", "rep", None, None, None),
    )
    out_specs = (P("section", "rep", None, None), P("section", "rep", None, None))
    return jax.shard_map(
        on_device, mesh=mesh, in_specs=in_specs, out_specs=out_specs, check_vma=False
    )
```

```python
import jax
import jax.numpy as jnp
from jax import lax
from jax.sharding import PartitionSpec as P

inner_rate = 0.05
pull_rate = 0.25
moment_rate = 0.9
outer_rate = 0.7

OUTWARD = [(1, 0), (2, 3)]
INWARD = [(0, 1), (3, 2)]
ACROSS = [(1, 2), (2, 1)]


def from_partner(value, distance):
    pairs = [(source, source ^ 2**distance) for source in range(lax.axis_size("rep"))]
    return lax.ppermute(value, "rep", pairs)


def bit_of(mask, index):
    return jnp.bitwise_and(jnp.right_shift(mask, index), 1) == 1


def route(value, mask, bits):
    for index in bits:
        value = jnp.where(bit_of(mask, index), from_partner(value, index), value)
    return value


def after(value, *earlier):
    return lax.optimization_barrier((value, *earlier))[0]


def after_all(values, *earlier):
    return lax.optimization_barrier((*values, *earlier))[: len(values)]


def slot_table(expert_ids, sections, capacity):
    expert_hot = (expert_ids[:, None] == jnp.arange(sections, dtype=jnp.int32)[None, :]).astype(
        jnp.int32
    )
    position = jnp.sum((jnp.cumsum(expert_hot, axis=0) - 1) * expert_hot, axis=1)
    slot_index = expert_ids * capacity + position
    return (
        slot_index[:, None] == jnp.arange(sections * capacity, dtype=jnp.int32)[None, :]
    ).astype(jnp.bfloat16)


def stacked(wide, width):
    return jnp.concatenate(jnp.split(wide, wide.shape[1] // width, axis=1), axis=0)


def side_by_side(tall):
    return jnp.concatenate(jnp.split(tall, tall.shape[0] // tall.shape[1], axis=0), axis=1)


class FourInLine:
    def __init__(self, gate, up, down, static_part, mask):
        replica = lax.axis_index("rep")
        self.inner = (replica == 1) | (replica == 2)
        self.near, self.far = mask == 1, mask == 3
        self.gate, self.up, self.down = gate, up, down
        self.static_part = static_part

    def forward(self, bits):
        self.up_side = lax.ppermute(self.up, "rep", INWARD)
        self.gate_hub = lax.ppermute(self.gate, "rep", ACROSS)
        inner, self.near, self.far, *bits = lax.optimization_barrier(
            (self.inner, self.near, self.far, *bits)
        )
        send = lax.optimization_barrier(jnp.where(inner, self.static_part, self.gate))
        self.one = from_partner(send, 0)
        side, self.gate_hub, self.near, self.far = lax.optimization_barrier(
            (self.up_side, self.gate_hub, self.near, self.far)
        )
        first = lax.optimization_barrier(jnp.where(self.far, side, self.up))
        second = jnp.where(self.far, self.up, after(side, first))
        first_in = lax.ppermute(first, "rep", ACROSS)
        self.quiet, self.first_in = first, first_in
        self.gate_edge = lax.ppermute(self.one, "rep", ACROSS)
        self.second = second
        return bits

    def settle(self, dispatched):
        base = lax.optimization_barrier(jnp.where(self.inner, self.up, self.down))
        dispatched, self.up_base = lax.optimization_barrier((dispatched, base, self.quiet))[:2]
        return dispatched

    def handed_up(self, earlier):
        first_in = after(self.first_in, *earlier)
        send = jnp.where(self.inner & ~self.near, first_in, self.up_base)
        self.two = from_partner(send, 0)
        self.up_hub = lax.ppermute(after(self.second, send), "rep", ACROSS)
        self.later = send

    def handed_gate(self, earlier):
        gate_edge = after(self.gate_edge, self.later, *earlier)
        gate_out = jnp.where(
            self.near, self.gate, jnp.where(self.far, gate_edge, self.gate_hub)
        )
        send = jnp.where(self.inner, gate_out, self.static_part)
        self.three = from_partner(send, 0)
        two = after(self.two, send)
        first = jnp.where(self.far, two, self.down)
        second = jnp.where(self.far, self.down, two)
        self.down_first = lax.ppermute(first, "rep", ACROSS)
        gate_in = jnp.where(
            self.near, self.one, jnp.where(self.far, self.gate_hub, self.gate_edge)
        )
        two, up_hub = lax.optimization_barrier((two, self.up_hub, first))[:2]
        self.second_down = second
        up_in = jnp.where(self.near, self.up_side, up_hub)
        self.gate_in = gate_in
        return jnp.where(self.inner, up_in, two)

    def gate_here(self, earlier):
        three = after(self.three, *earlier)
        static_in = jnp.where(self.inner, three, self.one)
        return lax.optimization_barrier(jnp.where(self.inner, self.gate_in, three)), static_in

    def swap_down(self, earlier):
        second = after(self.second_down, *earlier)
        self.down_hub = lax.ppermute(second, "rep", ACROSS)

    def handed_down(self, earlier):
        send = jnp.where(self.near, self.down, after(self.down_first, *earlier))
        self.four = lax.ppermute(send, "rep", OUTWARD)
        return send

    def down_here(self, earlier):
        down_hub = after(self.down_hub, *earlier)
        down_in = jnp.where(self.near, self.two, down_hub)
        return jnp.where(self.inner, down_in, self.four)


def on_device(
    tokens,
    assign,
    route_mask,
    match_mask,
    gate_weight,
    up_weight,
    down_weight,
    slow_down,
    momentum,
    slot_cot,
):
    sections = lax.axis_size("section")
    levels = lax.axis_size("rep").bit_length() - 1
    section_here = lax.axis_index("section")
    token_rows = tokens[0, 0]
    expert_ids = assign[0, 0, :, 0]
    capacity = slot_cot.shape[3]
    model_width = token_rows.shape[1]
    masks_here = lax.dynamic_index_in_dim(
        jnp.stack([route_mask, match_mask]), section_here, axis=1, keepdims=False
    )
    own_mask, match = masks_here[0], masks_here[1]
    match_mine = jnp.bitwise_xor(own_mask, match)
    upward = list(range(levels))
    bits = [bit_of(mask, index) for mask in (own_mask, match_mine, match) for index in upward]
    contract = (((1,), (1,)), ((), ()))
    hidden_width = gate_weight.shape[3]

    gate_raw, up_raw, down_raw = gate_weight[0, 0], up_weight[0, 0], down_weight[0, 0]
    slow_float = slow_down[0, 0].astype(jnp.float32)
    down_float = down_raw.astype(jnp.float32)
    static_part = ((0.5 - pull_rate) * slow_float - 0.5 * down_float).astype(jnp.bfloat16)

    selector = slot_table(expert_ids, sections, capacity)
    placed = lax.dot_general(
        selector, token_rows, (((0,), (0,)), ((), ())), preferred_element_type=jnp.float32
    )
    dispatched = placed.astype(jnp.bfloat16).reshape(sections, capacity, model_width)

    line = None
    if levels == 2:
        line = FourInLine(
            gate_raw,
            up_raw,
            stacked(down_raw, hidden_width),
            stacked(lax.optimization_barrier(static_part), hidden_width),
            own_mask,
        )
        bits = line.forward(bits)
        dispatched = line.settle(dispatched)
        line.handed_up((dispatched,))
    arrived = lax.all_to_all(dispatched, "section", split_axis=0, concat_axis=0, tiled=True)
    rows = arrived.reshape(-1, model_width)
    cotangent = slot_cot[0, 0].reshape(-1, model_width)
    if line is not None:
        up_mat = line.handed_gate((rows,))
    else:
        gate_mat, up_mat, down_mat = [
            route(weight, own_mask, upward) for weight in (gate_raw, up_raw, down_raw)
        ]
        static_in = from_partner(static_part, 0)

    up_act = jnp.dot(rows, up_mat, preferred_element_type=jnp.float32)
    if line is not None:
        gate_mat, static_in = line.gate_here((up_act,))
    gate_act = jnp.dot(rows, gate_mat, preferred_element_type=jnp.float32)
    sigmoid_gate = jax.nn.sigmoid(gate_act)
    hidden = (gate_act * sigmoid_gate * up_act).astype(jnp.bfloat16)
    down_grad = lax.dot_general(
        hidden, cotangent, (((0,), (0,)), ((), ())), preferred_element_type=jnp.float32
    ).astype(jnp.bfloat16)

    if line is not None:
        line.swap_down((down_grad,))

    own_bits, mine_bits, match_bits = [
        bits[number * levels : (number + 1) * levels] for number in range(3)
    ]
    lower, top = upward[:-1], levels - 1
    down_grad_in = from_partner(down_grad, 0)
    if line is not None:
        static_in = after(static_in, line.down_first, down_grad)
        static_in = lax.optimization_barrier(side_by_side(static_in))
        sent = line.handed_down((down_grad_in, static_in))
        down_grad_in = after(down_grad_in, sent)
    own_routed, match_routed, static_routed = down_grad, down_grad, static_part
    for index in lower:
        if index == 0:
            own_in, match_in, static_here = down_grad_in, down_grad_in, static_in
        else:
            own_in = from_partner(own_routed, index)
            match_in = from_partner(match_routed, index)
            static_here = from_partner(static_routed, index)
        own_routed = jnp.where(own_bits[index], own_in, own_routed)
        match_routed = jnp.where(mine_bits[index], match_in, match_routed)
        static_routed = jnp.where(match_bits[index], static_here, static_routed)

    def combined(side, static_routed, own_routed, match_routed):
        def pick(bit, value):
            return jnp.where(bit == side, value.astype(jnp.float32), 0.0)

        return pick(match_bits[top], static_routed) + 0.5 * inner_rate * (
            pick(own_bits[top], own_routed) + pick(mine_bits[top], match_routed)
        )

    crossing_out = combined(True, static_routed, own_routed, match_routed).astype(jnp.bfloat16)
    if line is not None:
        crossing_out = after(crossing_out, line.down_hub)
    crossing = from_partner(crossing_out, top)
    slow_float = after(slow_down[0, 0], crossing_out).astype(jnp.float32)
    staying = combined(False, static_routed, own_routed, match_routed)
    outer_here = (0.5 + pull_rate) * slow_float - 0.5 * down_float + staying
    pull = outer_rate * (1.0 + moment_rate)
    kept = (
        slow_float
        - pull * outer_here
        - (outer_rate * moment_rate * moment_rate) * momentum[0, 0].astype(jnp.float32)
    )
    kept = after(kept, crossing_out)
    new_slow = (kept - pull * crossing.astype(jnp.float32)).astype(jnp.bfloat16)

    if line is not None:
        down_mat = side_by_side(line.down_here((crossing_out,)))
    hidden_grad = lax.dot_general(
        cotangent, down_mat, contract, preferred_element_type=jnp.float32
    )
    gate_grad = (
        hidden_grad * up_act * sigmoid_gate * (1.0 + gate_act * (1.0 - sigmoid_gate))
    ).astype(jnp.bfloat16)
    up_grad = (hidden_grad * gate_act * sigmoid_gate).astype(jnp.bfloat16)
    slot_grad = (
        lax.dot_general(gate_grad, gate_mat, contract, preferred_element_type=jnp.float32)
        + lax.dot_general(up_grad, up_mat, contract, preferred_element_type=jnp.float32)
    ).astype(jnp.bfloat16)
    slot_grad = slot_grad.reshape(sections, capacity, model_width)
    returned = lax.all_to_all(slot_grad, "section", split_axis=0, concat_axis=0, tiled=True)
    input_grad = jnp.dot(
        selector, returned.reshape(-1, model_width), preferred_element_type=jnp.float32
    ).astype(jnp.bfloat16)
    return (input_grad[None, None], new_slow[None, None])


def solution(mesh):
    in_specs = (
        P("section", "rep", None, None),
        P("section", "rep", None, None),
        P(),
        P(),
        P("section", "rep", None, None),
        P("section", "rep", None, None),
        P("section", "rep", None, None),
        P("section", "rep", None, None),
        P("section", "rep", None, None),
        P("section", "rep", None, None, None),
    )
    out_specs = (P("section", "rep", None, None), P("section", "rep", None, None))
    return jax.shard_map(
        on_device, mesh=mesh, in_specs=in_specs, out_specs=out_specs, check_vma=False
    )
```

```python
import jax
import jax.numpy as jnp
from jax import lax
from jax.sharding import PartitionSpec as P

inner_rate = 0.05
pull_rate = 0.25
moment_rate = 0.9
outer_rate = 0.7

OUTWARD = [(1, 0), (2, 3)]
INWARD = [(0, 1), (3, 2)]
ACROSS = [(1, 2), (2, 1)]


def from_partner(value, distance):
    pairs = [(source, source ^ 2**distance) for source in range(lax.axis_size("rep"))]
    return lax.ppermute(value, "rep", pairs)


def bit_of(mask, index):
    return jnp.bitwise_and(jnp.right_shift(mask, index), 1) == 1


def route(value, mask, bits):
    for index in bits:
        value = jnp.where(bit_of(mask, index), from_partner(value, index), value)
    return value


def after(value, *earlier):
    return lax.optimization_barrier((value, *earlier))[0]


def slot_table(expert_ids, sections, capacity):
    expert_hot = (expert_ids[:, None] == jnp.arange(sections, dtype=jnp.int32)[None, :]).astype(
        jnp.int32
    )
    position = jnp.sum((jnp.cumsum(expert_hot, axis=0) - 1) * expert_hot, axis=1)
    slot_index = expert_ids * capacity + position
    return (
        slot_index[:, None] == jnp.arange(sections * capacity, dtype=jnp.int32)[None, :]
    ).astype(jnp.bfloat16)


def stacked(wide, width):
    return jnp.concatenate(jnp.split(wide, wide.shape[1] // width, axis=1), axis=0)


def side_by_side(tall):
    return jnp.concatenate(jnp.split(tall, tall.shape[0] // tall.shape[1], axis=0), axis=1)


class FourInLine:
    def __init__(self, gate, up, down, static_part, mask):
        replica = lax.axis_index("rep")
        self.inner = (replica == 1) | (replica == 2)
        self.near, self.far = mask == 1, mask == 3
        self.gate, self.up, self.down = gate, up, down
        self.static_part = static_part

    def forward(self, bits):
        self.up_side = lax.ppermute(self.up, "rep", INWARD)
        self.gate_hub = lax.ppermute(self.gate, "rep", ACROSS)
        inner, self.near, self.far, *bits = lax.optimization_barrier(
            (self.inner, self.near, self.far, *bits)
        )
        send = lax.optimization_barrier(jnp.where(inner, self.static_part, self.gate))
        self.one = from_partner(send, 0)
        side, self.near, self.far = lax.optimization_barrier((self.up_side, self.near, self.far))
        first = jnp.where(self.far, side, self.up)
        second = jnp.where(self.far, self.up, side)
        first_in = lax.ppermute(first, "rep", ACROSS)
        self.quiet, self.first_in = first, first_in
        self.gate_edge = lax.ppermute(self.one, "rep", ACROSS)
        self.second = second
        return bits

    def handed_up(self, earlier):
        first_in = after(self.first_in, *earlier)
        send = jnp.where(self.inner, jnp.where(self.near, self.up, first_in), self.down)
        self.two = from_partner(send, 0)
        self.up_hub = lax.ppermute(after(self.second, send), "rep", ACROSS)
        self.later = send

    def handed_gate(self, earlier):
        gate_edge = after(self.gate_edge, self.later, *earlier)
        gate_out = jnp.where(
            self.near, self.gate, jnp.where(self.far, gate_edge, self.gate_hub)
        )
        send = jnp.where(self.inner, gate_out, self.static_part)
        self.three = from_partner(send, 0)
        two = after(self.two, send)
        first = jnp.where(self.far, two, self.down)
        second = jnp.where(self.far, self.down, two)
        self.down_first = lax.ppermute(first, "rep", ACROSS)
        gate_in = jnp.where(
            self.near, self.one, jnp.where(self.far, self.gate_hub, self.gate_edge)
        )
        two, up_hub = lax.optimization_barrier((two, self.up_hub, first))[:2]
        self.second_down = second
        up_in = jnp.where(self.near, self.up_side, up_hub)
        self.gate_in = gate_in
        return jnp.where(self.inner, up_in, two)

    def gate_here(self, earlier):
        three = after(self.three, *earlier)
        static_in = jnp.where(self.inner, three, self.one)
        return lax.optimization_barrier(jnp.where(self.inner, self.gate_in, three)), static_in

    def swap_down(self, earlier):
        second = after(self.second_down, *earlier)
        self.down_hub = lax.ppermute(second, "rep", ACROSS)

    def handed_down(self, earlier):
        send = jnp.where(self.near, self.down, after(self.down_first, *earlier))
        self.four = lax.ppermute(send, "rep", OUTWARD)
        return send

    def down_here(self, earlier):
        down_hub = after(self.down_hub, *earlier)
        down_in = jnp.where(self.near, self.two, down_hub)
        return jnp.where(self.inner, down_in, self.four)


def on_device(
    tokens,
    assign,
    route_mask,
    match_mask,
    gate_weight,
    up_weight,
    down_weight,
    slow_down,
    momentum,
    slot_cot,
):
    sections = lax.axis_size("section")
    levels = lax.axis_size("rep").bit_length() - 1
    section_here = lax.axis_index("section")
    token_rows = tokens[0, 0]
    expert_ids = assign[0, 0, :, 0]
    capacity = slot_cot.shape[3]
    model_width = token_rows.shape[1]
    masks_here = lax.dynamic_index_in_dim(
        jnp.stack([route_mask, match_mask]), section_here, axis=1, keepdims=False
    )
    own_mask, match = masks_here[0], masks_here[1]
    match_mine = jnp.bitwise_xor(own_mask, match)
    upward = list(range(levels))
    bits = [bit_of(mask, index) for mask in (own_mask, match_mine, match) for index in upward]
    contract = (((1,), (1,)), ((), ()))
    hidden_width = gate_weight.shape[3]

    gate_raw, up_raw, down_raw = gate_weight[0, 0], up_weight[0, 0], down_weight[0, 0]
    slow_float = slow_down[0, 0].astype(jnp.float32)
    down_float = down_raw.astype(jnp.float32)
    static_part = ((0.5 - pull_rate) * slow_float - 0.5 * down_float).astype(jnp.bfloat16)

    selector = slot_table(expert_ids, sections, capacity)
    placed = lax.dot_general(
        selector, token_rows, (((0,), (0,)), ((), ())), preferred_element_type=jnp.float32
    )
    dispatched = placed.astype(jnp.bfloat16).reshape(sections, capacity, model_width)

    line = None
    if levels == 2:
        line = FourInLine(
            gate_raw,
            up_raw,
            stacked(down_raw, hidden_width),
            stacked(lax.optimization_barrier(static_part), hidden_width),
            own_mask,
        )
        bits = line.forward(bits)
        dispatched, line.gate_hub = lax.optimization_barrier(
            (dispatched, line.gate_hub, line.quiet)
        )[:2]
        line.handed_up((dispatched,))
    arrived = lax.all_to_all(dispatched, "section", split_axis=0, concat_axis=0, tiled=True)
    rows = arrived.reshape(-1, model_width)
    cotangent = slot_cot[0, 0].reshape(-1, model_width)
    if line is not None:
        up_mat = line.handed_gate((rows,))
    else:
        gate_mat, up_mat, down_mat = [
            route(weight, own_mask, upward) for weight in (gate_raw, up_raw, down_raw)
        ]
        static_in = from_partner(static_part, 0)

    up_act = jnp.dot(rows, up_mat, preferred_element_type=jnp.float32)
    if line is not None:
        gate_mat, static_in = line.gate_here((up_act,))
    gate_act = jnp.dot(rows, gate_mat, preferred_element_type=jnp.float32)
    sigmoid_gate = jax.nn.sigmoid(gate_act)
    hidden = (gate_act * sigmoid_gate * up_act).astype(jnp.bfloat16)
    down_grad = lax.dot_general(
        hidden, cotangent, (((0,), (0,)), ((), ())), preferred_element_type=jnp.float32
    ).astype(jnp.bfloat16)

    if line is not None:
        line.swap_down((down_grad,))

    own_bits, mine_bits, match_bits = [
        bits[number * levels : (number + 1) * levels] for number in range(3)
    ]
    lower, top = upward[:-1], levels - 1
    down_grad_in = from_partner(down_grad, 0)
    if line is not None:
        static_in = after(static_in, line.down_first, down_grad)
        static_in = lax.optimization_barrier(side_by_side(static_in))
        sent = line.handed_down((down_grad_in, static_in))
        down_grad_in = after(down_grad_in, sent)
    own_routed, match_routed, static_routed = down_grad, down_grad, static_part
    for index in lower:
        if index == 0:
            own_in, match_in, static_here = down_grad_in, down_grad_in, static_in
        else:
            own_in = from_partner(own_routed, index)
            match_in = from_partner(match_routed, index)
            static_here = from_partner(static_routed, index)
        own_routed = jnp.where(own_bits[index], own_in, own_routed)
        match_routed = jnp.where(mine_bits[index], match_in, match_routed)
        static_routed = jnp.where(match_bits[index], static_here, static_routed)

    def combined(side, static_routed, own_routed, match_routed):
        def pick(bit, value):
            return jnp.where(bit == side, value.astype(jnp.float32), 0.0)

        return pick(match_bits[top], static_routed) + 0.5 * inner_rate * (
            pick(own_bits[top], own_routed) + pick(mine_bits[top], match_routed)
        )

    crossing_out = combined(True, static_routed, own_routed, match_routed).astype(jnp.bfloat16)
    if line is not None:
        crossing_out = after(crossing_out, line.down_hub)
    crossing = from_partner(crossing_out, top)
    slow_float = after(slow_down[0, 0], crossing_out).astype(jnp.float32)
    staying = combined(False, static_routed, own_routed, match_routed)
    outer_here = (0.5 + pull_rate) * slow_float - 0.5 * down_float + staying
    pull = outer_rate * (1.0 + moment_rate)
    kept = (
        slow_float
        - pull * outer_here
        - (outer_rate * moment_rate * moment_rate) * momentum[0, 0].astype(jnp.float32)
    )
    kept = after(kept, crossing_out)
    new_slow = (kept - pull * crossing.astype(jnp.float32)).astype(jnp.bfloat16)

    if line is not None:
        down_mat = side_by_side(line.down_here((crossing_out,)))
    hidden_grad = lax.dot_general(
        cotangent, down_mat, contract, preferred_element_type=jnp.float32
    )
    gate_grad = (
        hidden_grad * up_act * sigmoid_gate * (1.0 + gate_act * (1.0 - sigmoid_gate))
    ).astype(jnp.bfloat16)
    up_grad = (hidden_grad * gate_act * sigmoid_gate).astype(jnp.bfloat16)
    slot_grad = (
        lax.dot_general(gate_grad, gate_mat, contract, preferred_element_type=jnp.float32)
        + lax.dot_general(up_grad, up_mat, contract, preferred_element_type=jnp.float32)
    ).astype(jnp.bfloat16)
    slot_grad = slot_grad.reshape(sections, capacity, model_width)
    returned = lax.all_to_all(slot_grad, "section", split_axis=0, concat_axis=0, tiled=True)
    input_grad = jnp.dot(
        selector, returned.reshape(-1, model_width), preferred_element_type=jnp.float32
    ).astype(jnp.bfloat16)
    return (input_grad[None, None], new_slow[None, None])


def solution(mesh):
    in_specs = (
        P("section", "rep", None, None),
        P("section", "rep", None, None),
        P(),
        P(),
        P("section", "rep", None, None),
        P("section", "rep", None, None),
        P("section", "rep", None, None),
        P("section", "rep", None, None),
        P("section", "rep", None, None),
        P("section", "rep", None, None, None),
    )
    out_specs = (P("section", "rep", None, None), P("section", "rep", None, None))
    return jax.shard_map(
        on_device, mesh=mesh, in_specs=in_specs, out_specs=out_specs, check_vma=False
    )
```

```python
import jax
import jax.numpy as jnp
from jax import lax
from jax.sharding import PartitionSpec as P

inner_rate = 0.05
pull_rate = 0.25
moment_rate = 0.9
outer_rate = 0.7

OUTWARD = [(1, 0), (2, 3)]
INWARD = [(0, 1), (3, 2)]
ACROSS = [(1, 2), (2, 1)]


def from_partner(value, distance):
    pairs = [(source, source ^ 2**distance) for source in range(lax.axis_size("rep"))]
    return lax.ppermute(value, "rep", pairs)


def bit_of(mask, index):
    return jnp.bitwise_and(jnp.right_shift(mask, index), 1) == 1


def route(value, mask, bits):
    for index in bits:
        value = jnp.where(bit_of(mask, index), from_partner(value, index), value)
    return value


def after(value, *earlier):
    return lax.optimization_barrier((value, *earlier))[0]


def slot_table(expert_ids, sections, capacity):
    expert_hot = (expert_ids[:, None] == jnp.arange(sections, dtype=jnp.int32)[None, :]).astype(
        jnp.int32
    )
    position = jnp.sum((jnp.cumsum(expert_hot, axis=0) - 1) * expert_hot, axis=1)
    slot_index = expert_ids * capacity + position
    return (
        slot_index[:, None] == jnp.arange(sections * capacity, dtype=jnp.int32)[None, :]
    ).astype(jnp.bfloat16)


def stacked(wide, width):
    return jnp.concatenate(jnp.split(wide, wide.shape[1] // width, axis=1), axis=0)


def side_by_side(tall):
    return jnp.concatenate(jnp.split(tall, tall.shape[0] // tall.shape[1], axis=0), axis=1)


class FourInLine:
    def __init__(self, gate, up, down, static_part, mask):
        replica = lax.axis_index("rep")
        self.inner = (replica == 1) | (replica == 2)
        self.near, self.far = mask == 1, mask == 3
        self.gate, self.up, self.down = gate, up, down
        self.static_part = static_part

    def forward(self, bits):
        self.up_side = lax.ppermute(self.up, "rep", INWARD)
        self.gate_hub = lax.ppermute(self.gate, "rep", ACROSS)
        inner, self.near, self.far, *bits = lax.optimization_barrier(
            (self.inner, self.near, self.far, *bits)
        )
        send = lax.optimization_barrier(jnp.where(inner, self.static_part, self.gate))
        self.one = from_partner(send, 0)
        side, self.near, self.far = lax.optimization_barrier((self.up_side, self.near, self.far))
        first = jnp.where(self.far, side, self.up)
        second = jnp.where(self.far, self.up, side)
        first_in = lax.ppermute(first, "rep", ACROSS)
        self.quiet, self.first_in = first, first_in
        self.gate_edge = lax.ppermute(self.one, "rep", ACROSS)
        self.second = second
        return bits

    def handed_up(self, earlier):
        first_in = after(self.first_in, *earlier)
        send = jnp.where(self.inner, jnp.where(self.near, self.up, first_in), self.down)
        self.two = from_partner(send, 0)
        self.up_hub = lax.ppermute(after(self.second, send), "rep", ACROSS)
        self.later = send

    def handed_gate(self, earlier):
        gate_edge = after(self.gate_edge, self.later, *earlier)
        gate_out = jnp.where(
            self.near, self.gate, jnp.where(self.far, gate_edge, self.gate_hub)
        )
        send = jnp.where(self.inner, gate_out, self.static_part)
        self.three = from_partner(send, 0)
        two = after(self.two, send)
        first = jnp.where(self.far, two, self.down)
        second = jnp.where(self.far, self.down, two)
        self.down_first = lax.ppermute(first, "rep", ACROSS)
        gate_in = jnp.where(
            self.near, self.one, jnp.where(self.far, self.gate_hub, self.gate_edge)
        )
        two, up_hub = lax.optimization_barrier((two, self.up_hub, first))[:2]
        self.second_down = second
        up_in = jnp.where(self.near, self.up_side, up_hub)
        self.gate_in = gate_in
        return jnp.where(self.inner, up_in, two)

    def gate_here(self, earlier):
        three = after(self.three, *earlier)
        static_in = jnp.where(self.inner, three, self.one)
        return lax.optimization_barrier(jnp.where(self.inner, self.gate_in, three)), static_in

    def swap_down(self, earlier):
        second = after(self.second_down, *earlier)
        self.down_hub = lax.ppermute(second, "rep", ACROSS)

    def handed_down(self, earlier):
        send = jnp.where(self.near, self.down, after(self.down_first, *earlier))
        self.four = lax.ppermute(send, "rep", OUTWARD)
        return send

    def down_here(self, earlier):
        down_hub = after(self.down_hub, *earlier)
        down_in = jnp.where(self.near, self.two, down_hub)
        return jnp.where(self.inner, down_in, self.four)


def on_device(
    tokens,
    assign,
    route_mask,
    match_mask,
    gate_weight,
    up_weight,
    down_weight,
    slow_down,
    momentum,
    slot_cot,
):
    sections = lax.axis_size("section")
    levels = lax.axis_size("rep").bit_length() - 1
    section_here = lax.axis_index("section")
    token_rows = tokens[0, 0]
    expert_ids = assign[0, 0, :, 0]
    capacity = slot_cot.shape[3]
    model_width = token_rows.shape[1]
    masks_here = lax.dynamic_index_in_dim(
        jnp.stack([route_mask, match_mask]), section_here, axis=1, keepdims=False
    )
    own_mask, match = masks_here[0], masks_here[1]
    match_mine = jnp.bitwise_xor(own_mask, match)
    upward = list(range(levels))
    bits = [bit_of(mask, index) for mask in (own_mask, match_mine, match) for index in upward]
    contract = (((1,), (1,)), ((), ()))
    hidden_width = gate_weight.shape[3]

    gate_raw, up_raw, down_raw = gate_weight[0, 0], up_weight[0, 0], down_weight[0, 0]
    slow_float = slow_down[0, 0].astype(jnp.float32)
    down_float = down_raw.astype(jnp.float32)
    static_part = ((0.5 - pull_rate) * slow_float - 0.5 * down_float).astype(jnp.bfloat16)

    selector = slot_table(expert_ids, sections, capacity)
    placed = lax.dot_general(
        selector, token_rows, (((0,), (0,)), ((), ())), preferred_element_type=jnp.float32
    )
    dispatched = placed.astype(jnp.bfloat16).reshape(sections, capacity, model_width)

    line = None
    if levels == 2:
        line = FourInLine(
            gate_raw,
            up_raw,
            stacked(down_raw, hidden_width),
            stacked(lax.optimization_barrier(static_part), hidden_width),
            own_mask,
        )
        bits = line.forward(bits)
        dispatched, line.gate_hub = lax.optimization_barrier(
            (dispatched, line.gate_hub, line.quiet)
        )[:2]
        line.handed_up((dispatched,))
    arrived = lax.all_to_all(dispatched, "section", split_axis=0, concat_axis=0, tiled=True)
    rows = arrived.reshape(-1, model_width)
    cotangent = slot_cot[0, 0].reshape(-1, model_width)
    if line is not None:
        up_mat = line.handed_gate((rows,))
    else:
        gate_mat, up_mat, down_mat = [
            route(weight, own_mask, upward) for weight in (gate_raw, up_raw, down_raw)
        ]
        static_in = from_partner(static_part, 0)

    up_act = jnp.dot(rows, up_mat, preferred_element_type=jnp.float32)
    if line is not None:
        gate_mat, static_in = line.gate_here((up_act,))
        static_in = side_by_side(static_in)
    gate_act = jnp.dot(rows, gate_mat, preferred_element_type=jnp.float32)
    sigmoid_gate = jax.nn.sigmoid(gate_act)
    hidden = (gate_act * sigmoid_gate * up_act).astype(jnp.bfloat16)
    down_grad = lax.dot_general(
        hidden, cotangent, (((0,), (0,)), ((), ())), preferred_element_type=jnp.float32
    ).astype(jnp.bfloat16)

    if line is not None:
        line.swap_down((down_grad,))

    own_bits, mine_bits, match_bits = [
        bits[number * levels : (number + 1) * levels] for number in range(3)
    ]
    lower, top = upward[:-1], levels - 1
    down_grad_in = from_partner(down_grad, 0)
    if line is not None:
        sent = line.handed_down((down_grad,))
        static_in = after(static_in, sent)
        down_grad_in = after(down_grad_in, static_in)
    own_routed, match_routed, static_routed = down_grad, down_grad, static_part
    for index in lower:
        if index == 0:
            own_in, match_in, static_here = down_grad_in, down_grad_in, static_in
        else:
            own_in = from_partner(own_routed, index)
            match_in = from_partner(match_routed, index)
            static_here = from_partner(static_routed, index)
        own_routed = jnp.where(own_bits[index], own_in, own_routed)
        match_routed = jnp.where(mine_bits[index], match_in, match_routed)
        static_routed = jnp.where(match_bits[index], static_here, static_routed)

    def combined(side, static_routed, own_routed, match_routed):
        def pick(bit, value):
            return jnp.where(bit == side, value.astype(jnp.float32), 0.0)

        return pick(match_bits[top], static_routed) + 0.5 * inner_rate * (
            pick(own_bits[top], own_routed) + pick(mine_bits[top], match_routed)
        )

    crossing_out = combined(True, static_routed, own_routed, match_routed).astype(jnp.bfloat16)
    if line is not None:
        crossing_out = after(crossing_out, line.down_hub)
    crossing = from_partner(crossing_out, top)
    slow_float = after(slow_down[0, 0], crossing_out).astype(jnp.float32)
    staying = combined(False, static_routed, own_routed, match_routed)
    outer_here = (0.5 + pull_rate) * slow_float - 0.5 * down_float + staying
    pull = outer_rate * (1.0 + moment_rate)
    kept = (
        slow_float
        - pull * outer_here
        - (outer_rate * moment_rate * moment_rate) * momentum[0, 0].astype(jnp.float32)
    )
    kept = after(kept, crossing_out)
    new_slow = (kept - pull * crossing.astype(jnp.float32)).astype(jnp.bfloat16)

    if line is not None:
        down_mat = side_by_side(line.down_here((crossing_out,)))
    hidden_grad = lax.dot_general(
        cotangent, down_mat, contract, preferred_element_type=jnp.float32
    )
    gate_grad = (
        hidden_grad * up_act * sigmoid_gate * (1.0 + gate_act * (1.0 - sigmoid_gate))
    ).astype(jnp.bfloat16)
    up_grad = (hidden_grad * gate_act * sigmoid_gate).astype(jnp.bfloat16)
    slot_grad = (
        lax.dot_general(gate_grad, gate_mat, contract, preferred_element_type=jnp.float32)
        + lax.dot_general(up_grad, up_mat, contract, preferred_element_type=jnp.float32)
    ).astype(jnp.bfloat16)
    slot_grad = slot_grad.reshape(sections, capacity, model_width)
    returned = lax.all_to_all(slot_grad, "section", split_axis=0, concat_axis=0, tiled=True)
    input_grad = jnp.dot(
        selector, returned.reshape(-1, model_width), preferred_element_type=jnp.float32
    ).astype(jnp.bfloat16)
    return (input_grad[None, None], new_slow[None, None])


def solution(mesh):
    in_specs = (
        P("section", "rep", None, None),
        P("section", "rep", None, None),
        P(),
        P(),
        P("section", "rep", None, None),
        P("section", "rep", None, None),
        P("section", "rep", None, None),
        P("section", "rep", None, None),
        P("section", "rep", None, None),
        P("section", "rep", None, None, None),
    )
    out_specs = (P("section", "rep", None, None), P("section", "rep", None, None))
    return jax.shard_map(
        on_device, mesh=mesh, in_specs=in_specs, out_specs=out_specs, check_vma=False
    )
```

```python
import jax
import jax.numpy as jnp
from jax import lax
from jax.sharding import PartitionSpec as P

inner_rate = 0.05
pull_rate = 0.25
moment_rate = 0.9
outer_rate = 0.7

OUTWARD = [(1, 0), (2, 3)]
INWARD = [(0, 1), (3, 2)]
ACROSS = [(1, 2), (2, 1)]


def from_partner(value, distance):
    pairs = [(source, source ^ 2**distance) for source in range(lax.axis_size("rep"))]
    return lax.ppermute(value, "rep", pairs)


def bit_of(mask, index):
    return jnp.bitwise_and(jnp.right_shift(mask, index), 1) == 1


def route(value, mask, bits):
    for index in bits:
        value = jnp.where(bit_of(mask, index), from_partner(value, index), value)
    return value


def after(value, *earlier):
    return lax.optimization_barrier((value, *earlier))[0]


def slot_table(expert_ids, sections, capacity):
    expert_hot = (expert_ids[:, None] == jnp.arange(sections, dtype=jnp.int32)[None, :]).astype(
        jnp.int32
    )
    position = jnp.sum((jnp.cumsum(expert_hot, axis=0) - 1) * expert_hot, axis=1)
    slot_index = expert_ids * capacity + position
    return (
        slot_index[:, None] == jnp.arange(sections * capacity, dtype=jnp.int32)[None, :]
    ).astype(jnp.bfloat16)


def stacked(wide, width):
    return jnp.concatenate(jnp.split(wide, wide.shape[1] // width, axis=1), axis=0)


def side_by_side(tall):
    return jnp.concatenate(jnp.split(tall, tall.shape[0] // tall.shape[1], axis=0), axis=1)


class FourInLine:
    def __init__(self, gate, up, down, static_part, mask):
        replica = lax.axis_index("rep")
        self.inner = (replica == 1) | (replica == 2)
        self.near, self.far = mask == 1, mask == 3
        self.gate, self.up, self.down = gate, up, down
        self.static_part = static_part

    def forward(self, bits):
        self.up_side = lax.ppermute(self.up, "rep", INWARD)
        self.gate_hub = lax.ppermute(self.gate, "rep", ACROSS)
        inner, self.near, self.far, *bits = lax.optimization_barrier(
            (self.inner, self.near, self.far, *bits)
        )
        send = lax.optimization_barrier(jnp.where(inner, self.static_part, self.gate))
        self.one = from_partner(send, 0)
        side, self.near, self.far = lax.optimization_barrier((self.up_side, self.near, self.far))
        first = jnp.where(self.far, side, self.up)
        second = jnp.where(self.far, self.up, side)
        first_in = lax.ppermute(first, "rep", ACROSS)
        self.quiet, self.first_in = first, first_in
        self.gate_edge = lax.ppermute(self.one, "rep", ACROSS)
        self.second = second
        return bits

    def handed_up(self, earlier):
        first_in = after(self.first_in, *earlier)
        send = jnp.where(self.inner, jnp.where(self.near, self.up, first_in), self.down)
        self.two = from_partner(send, 0)
        self.up_hub = lax.ppermute(after(self.second, send), "rep", ACROSS)
        self.later = send

    def handed_gate(self, earlier):
        gate_edge = after(self.gate_edge, self.later, *earlier)
        gate_out = jnp.where(
            self.near, self.gate, jnp.where(self.far, gate_edge, self.gate_hub)
        )
        send = jnp.where(self.inner, gate_out, self.static_part)
        self.three = from_partner(send, 0)
        two = after(self.two, send)
        first = jnp.where(self.far, two, self.down)
        second = jnp.where(self.far, self.down, two)
        self.down_first = lax.ppermute(first, "rep", ACROSS)
        gate_in = jnp.where(
            self.near, self.one, jnp.where(self.far, self.gate_hub, self.gate_edge)
        )
        two, up_hub = lax.optimization_barrier((two, self.up_hub, first))[:2]
        self.second_down = second
        up_in = jnp.where(self.near, self.up_side, up_hub)
        self.gate_in = gate_in
        return jnp.where(self.inner, up_in, two)

    def gate_here(self, earlier):
        self.three, gate_in = lax.optimization_barrier((self.three, self.gate_in, *earlier))[:2]
        return jnp.where(self.inner, gate_in, self.three)

    def static_in(self, earlier):
        three = after(self.three, *earlier)
        return side_by_side(jnp.where(self.inner, three, self.one))

    def swap_down(self, earlier):
        second = after(self.second_down, *earlier)
        self.down_hub = lax.ppermute(second, "rep", ACROSS)

    def handed_down(self, earlier):
        send = jnp.where(self.near, self.down, after(self.down_first, *earlier))
        self.four = lax.ppermute(send, "rep", OUTWARD)
        return send

    def down_here(self, earlier):
        down_hub = after(self.down_hub, *earlier)
        down_in = jnp.where(self.near, self.two, down_hub)
        return jnp.where(self.inner, down_in, self.four)


def on_device(
    tokens,
    assign,
    route_mask,
    match_mask,
    gate_weight,
    up_weight,
    down_weight,
    slow_down,
    momentum,
    slot_cot,
):
    sections = lax.axis_size("section")
    levels = lax.axis_size("rep").bit_length() - 1
    section_here = lax.axis_index("section")
    token_rows = tokens[0, 0]
    expert_ids = assign[0, 0, :, 0]
    capacity = slot_cot.shape[3]
    model_width = token_rows.shape[1]
    masks_here = lax.dynamic_index_in_dim(
        jnp.stack([route_mask, match_mask]), section_here, axis=1, keepdims=False
    )
    own_mask, match = masks_here[0], masks_here[1]
    match_mine = jnp.bitwise_xor(own_mask, match)
    upward = list(range(levels))
    bits = [bit_of(mask, index) for mask in (own_mask, match_mine, match) for index in upward]
    contract = (((1,), (1,)), ((), ()))
    hidden_width = gate_weight.shape[3]

    gate_raw, up_raw, down_raw = gate_weight[0, 0], up_weight[0, 0], down_weight[0, 0]
    slow_float = slow_down[0, 0].astype(jnp.float32)
    down_float = down_raw.astype(jnp.float32)
    static_part = ((0.5 - pull_rate) * slow_float - 0.5 * down_float).astype(jnp.bfloat16)

    selector = slot_table(expert_ids, sections, capacity)
    placed = lax.dot_general(
        selector, token_rows, (((0,), (0,)), ((), ())), preferred_element_type=jnp.float32
    )
    dispatched = placed.astype(jnp.bfloat16).reshape(sections, capacity, model_width)

    line = None
    if levels == 2:
        line = FourInLine(
            gate_raw,
            up_raw,
            stacked(down_raw, hidden_width),
            stacked(lax.optimization_barrier(static_part), hidden_width),
            own_mask,
        )
        bits = line.forward(bits)
        dispatched, line.gate_hub = lax.optimization_barrier(
            (dispatched, line.gate_hub, line.quiet)
        )[:2]
        line.handed_up((dispatched,))
    arrived = lax.all_to_all(dispatched, "section", split_axis=0, concat_axis=0, tiled=True)
    rows = arrived.reshape(-1, model_width)
    cotangent = slot_cot[0, 0].reshape(-1, model_width)
    if line is not None:
        up_mat = line.handed_gate((rows,))
    else:
        gate_mat, up_mat, down_mat = [
            route(weight, own_mask, upward) for weight in (gate_raw, up_raw, down_raw)
        ]
        static_in = from_partner(static_part, 0)

    up_act = jnp.dot(rows, up_mat, preferred_element_type=jnp.float32)
    if line is not None:
        gate_mat = line.gate_here((up_act,))
    gate_act = jnp.dot(rows, gate_mat, preferred_element_type=jnp.float32)
    sigmoid_gate = jax.nn.sigmoid(gate_act)
    hidden = (gate_act * sigmoid_gate * up_act).astype(jnp.bfloat16)
    down_grad = lax.dot_general(
        hidden, cotangent, (((0,), (0,)), ((), ())), preferred_element_type=jnp.float32
    ).astype(jnp.bfloat16)

    if line is not None:
        line.swap_down((down_grad,))

    own_bits, mine_bits, match_bits = [
        bits[number * levels : (number + 1) * levels] for number in range(3)
    ]
    lower, top = upward[:-1], levels - 1
    down_grad_in = from_partner(down_grad, 0)
    if line is not None:
        sent = line.handed_down((down_grad,))
        static_in = line.static_in((sent,))
        down_grad_in = after(down_grad_in, static_in)
    own_routed, match_routed, static_routed = down_grad, down_grad, static_part
    for index in lower:
        if index == 0:
            own_in, match_in, static_here = down_grad_in, down_grad_in, static_in
        else:
            own_in = from_partner(own_routed, index)
            match_in = from_partner(match_routed, index)
            static_here = from_partner(static_routed, index)
        own_routed = jnp.where(own_bits[index], own_in, own_routed)
        match_routed = jnp.where(mine_bits[index], match_in, match_routed)
        static_routed = jnp.where(match_bits[index], static_here, static_routed)

    def combined(side, static_routed, own_routed, match_routed):
        def pick(bit, value):
            return jnp.where(bit == side, value.astype(jnp.float32), 0.0)

        return pick(match_bits[top], static_routed) + 0.5 * inner_rate * (
            pick(own_bits[top], own_routed) + pick(mine_bits[top], match_routed)
        )

    crossing_out = combined(True, static_routed, own_routed, match_routed).astype(jnp.bfloat16)
    if line is not None:
        crossing_out = after(crossing_out, line.down_hub)
    crossing = from_partner(crossing_out, top)
    slow_float = after(slow_down[0, 0], crossing_out).astype(jnp.float32)
    staying = combined(False, static_routed, own_routed, match_routed)
    outer_here = (0.5 + pull_rate) * slow_float - 0.5 * down_float + staying
    pull = outer_rate * (1.0 + moment_rate)
    kept = (
        slow_float
        - pull * outer_here
        - (outer_rate * moment_rate * moment_rate) * momentum[0, 0].astype(jnp.float32)
    )
    kept = after(kept, crossing_out)
    new_slow = (kept - pull * crossing.astype(jnp.float32)).astype(jnp.bfloat16)

    if line is not None:
        down_mat = side_by_side(line.down_here((crossing_out,)))
    hidden_grad = lax.dot_general(
        cotangent, down_mat, contract, preferred_element_type=jnp.float32
    )
    gate_grad = (
        hidden_grad * up_act * sigmoid_gate * (1.0 + gate_act * (1.0 - sigmoid_gate))
    ).astype(jnp.bfloat16)
    up_grad = (hidden_grad * gate_act * sigmoid_gate).astype(jnp.bfloat16)
    slot_grad = (
        lax.dot_general(gate_grad, gate_mat, contract, preferred_element_type=jnp.float32)
        + lax.dot_general(up_grad, up_mat, contract, preferred_element_type=jnp.float32)
    ).astype(jnp.bfloat16)
    slot_grad = slot_grad.reshape(sections, capacity, model_width)
    returned = lax.all_to_all(slot_grad, "section", split_axis=0, concat_axis=0, tiled=True)
    input_grad = jnp.dot(
        selector, returned.reshape(-1, model_width), preferred_element_type=jnp.float32
    ).astype(jnp.bfloat16)
    return (input_grad[None, None], new_slow[None, None])


def solution(mesh):
    in_specs = (
        P("section", "rep", None, None),
        P("section", "rep", None, None),
        P(),
        P(),
        P("section", "rep", None, None),
        P("section", "rep", None, None),
        P("section", "rep", None, None),
        P("section", "rep", None, None),
        P("section", "rep", None, None),
        P("section", "rep", None, None, None),
    )
    out_specs = (P("section", "rep", None, None), P("section", "rep", None, None))
    return jax.shard_map(
        on_device, mesh=mesh, in_specs=in_specs, out_specs=out_specs, check_vma=False
    )
```

```python
import jax
import jax.numpy as jnp
from jax import lax
from jax.sharding import PartitionSpec as P

inner_rate = 0.05
pull_rate = 0.25
moment_rate = 0.9
outer_rate = 0.7

OUTWARD = [(1, 0), (2, 3)]
INWARD = [(0, 1), (3, 2)]
ACROSS = [(1, 2), (2, 1)]


def from_partner(value, distance):
    pairs = [(source, source ^ 2**distance) for source in range(lax.axis_size("rep"))]
    return lax.ppermute(value, "rep", pairs)


def bit_of(mask, index):
    return jnp.bitwise_and(jnp.right_shift(mask, index), 1) == 1


def route(value, mask, bits):
    for index in bits:
        value = jnp.where(bit_of(mask, index), from_partner(value, index), value)
    return value


def after(value, *earlier):
    return lax.optimization_barrier((value, *earlier))[0]


def slot_table(expert_ids, sections, capacity):
    expert_hot = (expert_ids[:, None] == jnp.arange(sections, dtype=jnp.int32)[None, :]).astype(
        jnp.int32
    )
    position = jnp.sum((jnp.cumsum(expert_hot, axis=0) - 1) * expert_hot, axis=1)
    slot_index = expert_ids * capacity + position
    return (
        slot_index[:, None] == jnp.arange(sections * capacity, dtype=jnp.int32)[None, :]
    ).astype(jnp.bfloat16)


def stacked(wide, width):
    return jnp.concatenate(jnp.split(wide, wide.shape[1] // width, axis=1), axis=0)


def side_by_side(tall):
    return jnp.concatenate(jnp.split(tall, tall.shape[0] // tall.shape[1], axis=0), axis=1)


class FourInLine:
    def __init__(self, gate, up, down, static_part, mask):
        replica = lax.axis_index("rep")
        self.inner = (replica == 1) | (replica == 2)
        self.near, self.far = mask == 1, mask == 3
        self.gate, self.up, self.down = gate, up, down
        self.static_part = static_part

    def forward(self, bits):
        self.up_side = lax.ppermute(self.up, "rep", INWARD)
        self.gate_hub = lax.ppermute(self.gate, "rep", ACROSS)
        inner, self.near, self.far, *bits = lax.optimization_barrier(
            (self.inner, self.near, self.far, *bits)
        )
        send = lax.optimization_barrier(jnp.where(inner, self.static_part, self.gate))
        self.one = from_partner(send, 0)
        side, self.near, self.far = lax.optimization_barrier((self.up_side, self.near, self.far))
        first = lax.optimization_barrier(jnp.where(self.far, side, self.up))
        second = jnp.where(self.far, self.up, after(side, first))
        first_in = lax.ppermute(first, "rep", ACROSS)
        self.quiet, self.first_in = first, first_in
        self.gate_edge = lax.ppermute(self.one, "rep", ACROSS)
        self.second = second
        return bits

    def handed_up(self, earlier):
        first_in = after(self.first_in, *earlier)
        send = jnp.where(self.inner, jnp.where(self.near, self.up, first_in), self.down)
        self.two = from_partner(send, 0)
        self.up_hub = lax.ppermute(after(self.second, send), "rep", ACROSS)
        self.later = send

    def handed_gate(self, earlier):
        gate_edge = after(self.gate_edge, self.later, *earlier)
        gate_out = jnp.where(
            self.near, self.gate, jnp.where(self.far, gate_edge, self.gate_hub)
        )
        send = jnp.where(self.inner, gate_out, self.static_part)
        self.three = from_partner(send, 0)
        two = after(self.two, send)
        first = jnp.where(self.far, two, self.down)
        second = jnp.where(self.far, self.down, two)
        self.down_first = lax.ppermute(first, "rep", ACROSS)
        gate_in = jnp.where(
            self.near, self.one, jnp.where(self.far, self.gate_hub, self.gate_edge)
        )
        two, up_hub = lax.optimization_barrier((two, self.up_hub, first))[:2]
        self.second_down = second
        up_in = jnp.where(self.near, self.up_side, up_hub)
        self.gate_in = gate_in
        return jnp.where(self.inner, up_in, two)

    def gate_here(self, earlier):
        self.three, gate_in = lax.optimization_barrier((self.three, self.gate_in, *earlier))[:2]
        return jnp.where(self.inner, gate_in, self.three)

    def static_in(self, earlier):
        three = after(self.three, *earlier)
        return side_by_side(jnp.where(self.inner, three, self.one))

    def swap_down(self, earlier):
        second = after(self.second_down, *earlier)
        self.down_hub = lax.ppermute(second, "rep", ACROSS)

    def handed_down(self, earlier):
        send = jnp.where(self.near, self.down, after(self.down_first, *earlier))
        self.four = lax.ppermute(send, "rep", OUTWARD)
        return send

    def down_here(self, earlier):
        down_hub = after(self.down_hub, *earlier)
        down_in = jnp.where(self.near, self.two, down_hub)
        return jnp.where(self.inner, down_in, self.four)


def on_device(
    tokens,
    assign,
    route_mask,
    match_mask,
    gate_weight,
    up_weight,
    down_weight,
    slow_down,
    momentum,
    slot_cot,
):
    sections = lax.axis_size("section")
    levels = lax.axis_size("rep").bit_length() - 1
    section_here = lax.axis_index("section")
    token_rows = tokens[0, 0]
    expert_ids = assign[0, 0, :, 0]
    capacity = slot_cot.shape[3]
    model_width = token_rows.shape[1]
    masks_here = lax.dynamic_index_in_dim(
        jnp.stack([route_mask, match_mask]), section_here, axis=1, keepdims=False
    )
    own_mask, match = masks_here[0], masks_here[1]
    match_mine = jnp.bitwise_xor(own_mask, match)
    upward = list(range(levels))
    bits = [bit_of(mask, index) for mask in (own_mask, match_mine, match) for index in upward]
    contract = (((1,), (1,)), ((), ()))
    hidden_width = gate_weight.shape[3]

    gate_raw, up_raw, down_raw = gate_weight[0, 0], up_weight[0, 0], down_weight[0, 0]
    slow_float = slow_down[0, 0].astype(jnp.float32)
    down_float = down_raw.astype(jnp.float32)
    static_part = ((0.5 - pull_rate) * slow_float - 0.5 * down_float).astype(jnp.bfloat16)

    selector = slot_table(expert_ids, sections, capacity)
    placed = lax.dot_general(
        selector, token_rows, (((0,), (0,)), ((), ())), preferred_element_type=jnp.float32
    )
    dispatched = placed.astype(jnp.bfloat16).reshape(sections, capacity, model_width)

    line = None
    if levels == 2:
        line = FourInLine(
            gate_raw,
            up_raw,
            stacked(down_raw, hidden_width),
            stacked(lax.optimization_barrier(static_part), hidden_width),
            own_mask,
        )
        bits = line.forward(bits)
        dispatched, line.gate_hub, line.second = lax.optimization_barrier(
            (dispatched, line.gate_hub, line.second, line.quiet)
        )[:3]
        line.handed_up((dispatched,))
    arrived = lax.all_to_all(dispatched, "section", split_axis=0, concat_axis=0, tiled=True)
    rows = arrived.reshape(-1, model_width)
    cotangent = slot_cot[0, 0].reshape(-1, model_width)
    if line is not None:
        up_mat = line.handed_gate((rows,))
    else:
        gate_mat, up_mat, down_mat = [
            route(weight, own_mask, upward) for weight in (gate_raw, up_raw, down_raw)
        ]
        static_in = from_partner(static_part, 0)

    up_act = jnp.dot(rows, up_mat, preferred_element_type=jnp.float32)
    if line is not None:
        gate_mat = line.gate_here((up_act,))
    gate_act = jnp.dot(rows, gate_mat, preferred_element_type=jnp.float32)
    sigmoid_gate = jax.nn.sigmoid(gate_act)
    hidden = (gate_act * sigmoid_gate * up_act).astype(jnp.bfloat16)
    down_grad = lax.dot_general(
        hidden, cotangent, (((0,), (0,)), ((), ())), preferred_element_type=jnp.float32
    ).astype(jnp.bfloat16)

    if line is not None:
        line.swap_down((down_grad,))

    own_bits, mine_bits, match_bits = [
        bits[number * levels : (number + 1) * levels] for number in range(3)
    ]
    lower, top = upward[:-1], levels - 1
    down_grad_in = from_partner(down_grad, 0)
    if line is not None:
        sent = line.handed_down((down_grad,))
        static_in = line.static_in((sent,))
        down_grad_in = after(down_grad_in, static_in)
    own_routed, match_routed, static_routed = down_grad, down_grad, static_part
    for index in lower:
        if index == 0:
            own_in, match_in, static_here = down_grad_in, down_grad_in, static_in
        else:
            own_in = from_partner(own_routed, index)
            match_in = from_partner(match_routed, index)
            static_here = from_partner(static_routed, index)
        own_routed = jnp.where(own_bits[index], own_in, own_routed)
        match_routed = jnp.where(mine_bits[index], match_in, match_routed)
        static_routed = jnp.where(match_bits[index], static_here, static_routed)

    def combined(side, static_routed, own_routed, match_routed):
        def pick(bit, value):
            return jnp.where(bit == side, value.astype(jnp.float32), 0.0)

        return pick(match_bits[top], static_routed) + 0.5 * inner_rate * (
            pick(own_bits[top], own_routed) + pick(mine_bits[top], match_routed)
        )

    crossing_out = combined(True, static_routed, own_routed, match_routed).astype(jnp.bfloat16)
    if line is not None:
        crossing_out = after(crossing_out, line.down_hub)
    crossing = from_partner(crossing_out, top)
    slow_float = after(slow_down[0, 0], crossing_out).astype(jnp.float32)
    staying = combined(False, static_routed, own_routed, match_routed)
    outer_here = (0.5 + pull_rate) * slow_float - 0.5 * down_float + staying
    pull = outer_rate * (1.0 + moment_rate)
    kept = (
        slow_float
        - pull * outer_here
        - (outer_rate * moment_rate * moment_rate) * momentum[0, 0].astype(jnp.float32)
    )
    kept = after(kept, crossing_out)
    new_slow = (kept - pull * crossing.astype(jnp.float32)).astype(jnp.bfloat16)

    if line is not None:
        down_mat = side_by_side(line.down_here((crossing_out,)))
    hidden_grad = lax.dot_general(
        cotangent, down_mat, contract, preferred_element_type=jnp.float32
    )
    gate_grad = (
        hidden_grad * up_act * sigmoid_gate * (1.0 + gate_act * (1.0 - sigmoid_gate))
    ).astype(jnp.bfloat16)
    up_grad = (hidden_grad * gate_act * sigmoid_gate).astype(jnp.bfloat16)
    slot_grad = (
        lax.dot_general(gate_grad, gate_mat, contract, preferred_element_type=jnp.float32)
        + lax.dot_general(up_grad, up_mat, contract, preferred_element_type=jnp.float32)
    ).astype(jnp.bfloat16)
    slot_grad = slot_grad.reshape(sections, capacity, model_width)
    returned = lax.all_to_all(slot_grad, "section", split_axis=0, concat_axis=0, tiled=True)
    input_grad = jnp.dot(
        selector, returned.reshape(-1, model_width), preferred_element_type=jnp.float32
    ).astype(jnp.bfloat16)
    return (input_grad[None, None], new_slow[None, None])


def solution(mesh):
    in_specs = (
        P("section", "rep", None, None),
        P("section", "rep", None, None),
        P(),
        P(),
        P("section", "rep", None, None),
        P("section", "rep", None, None),
        P("section", "rep", None, None),
        P("section", "rep", None, None),
        P("section", "rep", None, None),
        P("section", "rep", None, None, None),
    )
    out_specs = (P("section", "rep", None, None), P("section", "rep", None, None))
    return jax.shard_map(
        on_device, mesh=mesh, in_specs=in_specs, out_specs=out_specs, check_vma=False
    )
```
